256 devices in a mesh: lon: 64 (over z, y, x_lo), lat: 4 (over x_hi, core).
Axes of the slice: x: 4 (x_hi: 2, x_lo: 2; x = x_hi * 2 + x_lo), y: 4, z: 8, core: 2. Of those that a mesh axis runs over, the one named last changes fastest.
Arguments:
- fields: bfloat16 [2, 24, 768, 192], P(None, 'lat', 'lon'), may hold values from -6 to 6
- upstream: bfloat16 [2, 24, 768, 192], P(None, 'lat', 'lon'), may hold values from -6 to 6
- gains: float32 [2, 192], replicated, may hold values from 0.5 to 1.5
- project_in: bfloat16 [2, 192, 576], replicated, may hold values from -0.4375 to 0.4375
- project_out: bfloat16 [2, 192, 192], replicated, may hold values from -0.4375 to 0.4375
- earth_bias: bfloat16 [2, 1, 4, 6, 2, 2, 6, 6, 23], P(None, None, 'lat'), may hold values from -320 to 320
- row_valid: int32 [24], replicated, may hold values 0 or 1
- regions: int32 [2, 24], replicated, may hold values from 0 to 3
Outputs:
- updated: bfloat16 [2, 24, 768, 192], P(None, 'lat', 'lon')
- grad_fields: bfloat16 [2, 24, 768, 192], P(None, 'lat', 'lon')
- grad_gains: float32 [2, 192], replicated
- grad_in: float32 [2, 192, 576], replicated
- grad_proj: float32 [2, 192, 192], replicated
- grad_bias: float32 [2, 1, 4, 6, 2, 2, 6, 6, 23], P(None, None, 'lat')
The draws below stay inside these ranges and needn't reach their ends.
All inputs are finite; a program needn't handle non-finite values.
Results may differ from the reference program's by a relative error of at most 0.018.
Values may be sent and summed in bfloat16 or wider, within the bound.
No kernel may reach another device: no remote copies, remote signals or barrier semaphores. Data moves between devices by JAX's collectives and lax.ppermute only.
A program may use at most 64 MiB of HBM per device.

```python
import jax
import jax.numpy as jnp
from jax import lax

CHANNELS = 192
HEADS = 6
HEAD_DIM = 32
WIN_DEPTH = 2
WIN_ROWS = 6
WIN_SPAN = 12
WINDOW = 144
LEVELS = 2
ROWS = 24
COLUMNS = 768
DEPTH_WINDOWS = 1
ROW_WINDOWS = 4


def draw_earth_bias(key, part):
    key = jax.random.fold_in(key, 7)
    layout = (2, DEPTH_WINDOWS, ROW_WINDOWS, HEADS, WIN_DEPTH, WIN_DEPTH, WIN_ROWS, WIN_ROWS, 2 * WIN_SPAN - 1)
    base_key = jax.random.fold_in(key, 0)
    bias_table = jnp.clip(jax.random.normal(base_key, layout, jnp.float32), -4.0, 4.0)
    return bias_table.astype(jnp.bfloat16)


def set_ends(values, own_key, smallest, high):
    longest = values.shape.index(max(values.shape))
    spots = []
    for shift in (0, 1):
        where = [jax.random.randint(jax.random.fold_in(own_key, axis), (), 0, length) for axis, length in enumerate(values.shape)]
        where[longest] = (where[longest] + shift) % values.shape[longest]
        spots.append(tuple(where))
    return values.at[spots[0]].set(smallest).at[spots[1]].set(high)


def steps_of(own_key, dims, cuts, smallest, largest):
    factor_of, own = 1.0, jax.random.fold_in(own_key, 6)
    for position, blocks in cuts:
        steps = jnp.exp(jax.random.uniform(jax.random.fold_in(own, position), (blocks,), jnp.float32, smallest / len(cuts), largest / len(cuts)))
        factor_of = factor_of * jnp.repeat(steps, dims[position] // blocks).reshape([-1 if axis == position else 1 for axis in range(len(dims))])
    return factor_of


def noise(own_key, extent, deviation, limit, cuts=(), kind=jnp.bfloat16):
    entries = deviation * jax.random.normal(own_key, extent, jnp.float32)
    if cuts:
        entries = entries * steps_of(own_key, extent, cuts, -0.22, 0.18)
    return jnp.clip(entries, -limit, limit).astype(kind)


def setup_inputs(seed: int = 0) -> dict:
    arg_keys = jax.random.split(jax.random.key(seed), 9)
    return {
        "fields": noise(arg_keys[0], (LEVELS, ROWS, COLUMNS, CHANNELS), 1.0, 6.0, ((1, 4), (2, 64))),
        "upstream": noise(arg_keys[1], (LEVELS, ROWS, COLUMNS, CHANNELS), 1.0, 6.0, ((1, 4), (2, 64))),
        "gains": jnp.clip(1.0 + 0.1 * jax.random.normal(arg_keys[2], (2, CHANNELS), jnp.float32), 0.5, 1.5),
        "project_in": noise(arg_keys[3], (2, CHANNELS, 3 * CHANNELS), CHANNELS ** -0.5, 0.4375),
        "project_out": noise(arg_keys[4], (2, CHANNELS, CHANNELS), CHANNELS ** -0.5, 0.4375),
        "earth_bias": draw_earth_bias(jax.random.fold_in(arg_keys[8], 71), 0),
        "row_valid": set_ends((jax.random.randint(arg_keys[6], (ROWS,), 0, 4) < 3).astype(jnp.int32), jax.random.fold_in(arg_keys[6], 1), 0, 1),
        "regions": set_ends(jax.random.randint(arg_keys[7], (LEVELS, ROWS), 0, 4), jax.random.fold_in(arg_keys[7], 1), 0, 3).astype(jnp.int32),
    }


NORM_EPS = 1e-05
RMS_EPS = 1e-06

def stored(tensor):
    return lax.optimization_barrier(tensor.astype(jnp.bfloat16))

def layer_norm(fields, scale_gain):
    center = fields - lax.optimization_barrier(jnp.mean(fields, axis=-1, keepdims=True))
    spread = lax.optimization_barrier(jnp.mean(center * center, axis=-1, keepdims=True))
    return stored(center * lax.rsqrt(spread + NORM_EPS) * scale_gain)

def to_windows(field):
    levels, lat_rows, columns, feature = field.shape
    field = field.reshape(levels // WIN_DEPTH, WIN_DEPTH, lat_rows // WIN_ROWS, WIN_ROWS, columns // WIN_SPAN, WIN_SPAN, feature)
    field = field.transpose(0, 2, 4, 1, 3, 5, 6)
    return field.reshape(levels // WIN_DEPTH, lat_rows // WIN_ROWS, columns // WIN_SPAN, WINDOW, feature)

def from_windows(blocks, levels, lat_rows, columns):
    feature = blocks.shape[-1]
    blocks = blocks.reshape(levels // WIN_DEPTH, lat_rows // WIN_ROWS, columns // WIN_SPAN, WIN_DEPTH, WIN_ROWS, WIN_SPAN, feature)
    return blocks.transpose(0, 3, 1, 4, 2, 5, 6).reshape(levels, lat_rows, columns, feature)

def expand_bias(bias_table):
    pieces = [jnp.flip(bias_table[..., offset:offset + WIN_SPAN], -1) for offset in range(WIN_SPAN)]
    stacked = jnp.stack(pieces, -2)
    layout = stacked.shape
    stacked = stacked.transpose(0, 1, 2, 3, 5, 7, 4, 6, 8)
    return stacked.reshape(layout[0], layout[1], layout[2], WINDOW, WINDOW)

def window_rows(marks):
    levels, lat_rows = marks.shape
    marks = marks.reshape(levels // WIN_DEPTH, WIN_DEPTH, lat_rows // WIN_ROWS, WIN_ROWS).transpose(0, 2, 1, 3)
    marks = jnp.broadcast_to(marks[..., None], marks.shape + (WIN_SPAN,))
    return marks.reshape(levels // WIN_DEPTH, lat_rows // WIN_ROWS, WINDOW)

def make_allowed(usable, labels):
    usable = window_rows(usable)
    labels = window_rows(labels)
    same = labels[..., :, None] == labels[..., None, :]
    diagonal = jnp.eye(WINDOW, dtype=bool)
    return same & (usable[..., None, :] > 0) | diagonal

def attend(triple, bias_table, allowed):
    leading = triple.shape[:3]
    heads_view = triple.reshape(leading + (WINDOW, 3, HEADS, HEAD_DIM)).astype(jnp.float32)
    query = heads_view[..., 0, :, :]
    keys = heads_view[..., 1, :, :]
    values = heads_view[..., 2, :, :]
    scores = jnp.einsum('abcihd,abcjhd->abchij', query, keys) * HEAD_DIM ** (-0.5)
    scores = scores + expand_bias(bias_table)[:, :, None]
    scores = jnp.where(allowed[:, :, None, None], scores, -jnp.inf)
    peak = lax.stop_gradient(lax.optimization_barrier(jnp.max(scores, axis=-1, keepdims=True)))
    raised = jnp.exp(scores - peak)
    attention = stored(raised / lax.optimization_barrier(jnp.sum(raised, axis=-1, keepdims=True)))
    mixture = jnp.einsum('abchij,abcjhd->abcihd', attention.astype(jnp.float32), values)
    return stored(mixture.reshape(leading + (WINDOW, CHANNELS)))

def attn_forward(hidden, weight_in, weight_out, bias_table, allowed):
    levels, lat_rows, columns, _ = hidden.shape
    flattened = hidden.reshape(-1, CHANNELS)
    triple = stored(jnp.dot(flattened, weight_in, preferred_element_type=jnp.float32))
    mixture = attend(to_windows(triple.reshape(levels, lat_rows, columns, 3 * CHANNELS)), bias_table.astype(jnp.float32), allowed)
    mixture = from_windows(mixture, levels, lat_rows, columns).reshape(-1, CHANNELS)
    return stored(jnp.dot(mixture, weight_out, preferred_element_type=jnp.float32)).reshape(levels, lat_rows, columns, CHANNELS)

def attn_backward(hidden, grad_out, weight_in, weight_out, bias_table, allowed):
    levels, lat_rows, columns, _ = hidden.shape
    flattened = hidden.reshape(-1, CHANNELS)
    triple = stored(jnp.dot(flattened, weight_in, preferred_element_type=jnp.float32))

    def local_core(windows_in, table_in):
        return attend(windows_in, table_in, allowed)
    mixture, pullback = jax.vjp(local_core, to_windows(triple.reshape(levels, lat_rows, columns, 3 * CHANNELS)), bias_table.astype(jnp.float32))
    mixture = from_windows(mixture, levels, lat_rows, columns).reshape(-1, CHANNELS)
    cotangent = grad_out.reshape(-1, CHANNELS)
    grad_proj = lax.dot_general(mixture, cotangent, (((0,), (0,)), ((), ())), preferred_element_type=jnp.float32)
    grad_mix = stored(jnp.dot(cotangent, weight_out.T, preferred_element_type=jnp.float32))
    grad_windows, grad_table = pullback(to_windows(grad_mix.reshape(levels, lat_rows, columns, CHANNELS)))
    grad_triple = from_windows(grad_windows, levels, lat_rows, columns).reshape(-1, 3 * CHANNELS)
    grad_weight = lax.dot_general(flattened, grad_triple, (((0,), (0,)), ((), ())), preferred_element_type=jnp.float32)
    grad_hidden = stored(jnp.dot(grad_triple, weight_in.T, preferred_element_type=jnp.float32))
    return (grad_hidden.reshape(levels, lat_rows, columns, CHANNELS), grad_weight, grad_proj, grad_table)

def column_view(field):
    levels, lat_rows, columns, feature = field.shape
    return field.reshape(levels, lat_rows, columns // WIN_SPAN, WIN_SPAN, feature).transpose(2, 0, 1, 3, 4)

def merge_columns(stack):
    count, levels, lat_rows, span_size, feature = stack.shape
    return stack.transpose(1, 2, 0, 3, 4).reshape(levels, lat_rows, count * span_size, feature)

def forward_block(hidden, weight_in, weight_out, bias_table, allowed):

    def one_column(column):
        return attn_forward(column, weight_in, weight_out, bias_table, allowed)
    return merge_columns(lax.map(one_column, column_view(hidden)))

def backward_block(hidden, grad_out, weight_in, weight_out, bias_table, allowed):
    initial = (jnp.zeros((CHANNELS, 3 * CHANNELS), jnp.float32), jnp.zeros((CHANNELS, CHANNELS), jnp.float32), jnp.zeros(bias_table.shape, jnp.float32))

    def step(carry, paired):
        grad_hidden, grad_weight, grad_proj, grad_table = attn_backward(paired[0], paired[1], weight_in, weight_out, bias_table, allowed)
        return ((carry[0] + grad_weight, carry[1] + grad_proj, carry[2] + grad_table), grad_hidden)
    totals, grads = lax.scan(step, initial, (column_view(hidden), column_view(grad_out)))
    return (merge_columns(grads), totals)

def roll_in(field):
    return jnp.roll(field, (-1, -(WIN_ROWS // 2), -(WIN_SPAN // 2)), (0, 1, 2))

def roll_out(field):
    return jnp.roll(field, (1, WIN_ROWS // 2, WIN_SPAN // 2), (0, 1, 2))

def masks(row_valid, regions):
    levels = regions.shape[0]
    lat_rows = row_valid.shape[0]
    plain = make_allowed(jnp.broadcast_to(row_valid[None, :], (levels, lat_rows)), jnp.zeros((levels, lat_rows), jnp.int32))
    source_rows = (jnp.arange(lat_rows, dtype=jnp.int32) + WIN_ROWS // 2) % lat_rows
    source_levels = (jnp.arange(levels, dtype=jnp.int32) + 1) % levels
    usable = jnp.roll(row_valid, -(WIN_ROWS // 2))
    labels = jnp.roll(regions, (-1, -(WIN_ROWS // 2)), (0, 1))
    labels = labels + 4 * (source_rows < WIN_ROWS // 2).astype(jnp.int32)[None, :] + 8 * (source_levels < 1).astype(jnp.int32)[:, None]
    shifted = make_allowed(jnp.broadcast_to(usable[None, :], (levels, lat_rows)), labels)
    return (plain, shifted)

def unit_rms(stack):
    sums = lax.optimization_barrier(jnp.sum(stack * stack, axis=tuple(range(1, stack.ndim))))
    factor = jnp.sqrt(sums / stack[0].size + RMS_EPS)
    return stack / factor.reshape((-1,) + (1,) * (stack.ndim - 1))

def reference(fields, upstream, gains, project_in, project_out, earth_bias, row_valid, regions):
    plain, shifted = masks(row_valid, regions)
    base = fields.astype(jnp.float32)
    hidden_a = layer_norm(base, gains[0])
    added_a = forward_block(hidden_a, project_in[0], project_out[0], earth_bias[0], plain)
    middle = stored(base + added_a.astype(jnp.float32))
    middle_wide = middle.astype(jnp.float32)
    hidden_b = layer_norm(middle_wide, gains[1])
    rolled_b = roll_in(hidden_b)
    added_b = roll_out(forward_block(rolled_b, project_in[1], project_out[1], earth_bias[1], shifted))
    updated = stored(middle_wide + added_b.astype(jnp.float32))
    grad_rolled, totals_b = backward_block(rolled_b, roll_in(upstream), project_in[1], project_out[1], earth_bias[1], shifted)
    grad_hidden_b = roll_out(grad_rolled)
    _, pull_b = jax.vjp(layer_norm, middle_wide, gains[1])
    norm_b, gain_sum_b = pull_b(grad_hidden_b)
    grad_middle = stored(upstream.astype(jnp.float32) + norm_b)
    grad_hidden_a, totals_a = backward_block(hidden_a, grad_middle, project_in[0], project_out[0], earth_bias[0], plain)
    _, pull_a = jax.vjp(layer_norm, base, gains[0])
    norm_a, gain_sum_a = pull_a(grad_hidden_a)
    grad_fields = stored(grad_middle.astype(jnp.float32) + norm_a)
    grad_gains = unit_rms(jnp.stack([gain_sum_a, gain_sum_b]))
    grad_in = unit_rms(jnp.stack([totals_a[0], totals_b[0]]))
    grad_proj = unit_rms(jnp.stack([totals_a[1], totals_b[1]]))
    grad_bias = unit_rms(jnp.stack([totals_a[2], totals_b[2]]))
    return (updated, grad_fields, grad_gains, grad_in, grad_proj, grad_bias)
```

```python
import functools

import jax
import jax.numpy as jnp
from jax import lax
from jax.experimental import pallas as pl
from jax.experimental.pallas import tpu as pltpu
from jax.sharding import PartitionSpec as P

CHANNELS = 192
HEADS = 6
HEAD_DIM = 32
WIN_ROWS = 6
WIN_SPAN = 12
WINDOW = 144
STACK = HEADS * WINDOW
GROUPS = 12
OFFSETS = 23
TABLE_LANES = 384
TABLE_ROWS = 72
NORM_EPS = 1e-05
RMS_EPS = 1e-06
SCALE = HEAD_DIM ** (-0.5)
MAIN_HALF = 72
TABLE_HALF = 14
HALF = MAIN_HALF + TABLE_HALF + 1
GAIN_SPOT = MAIN_HALF + 2 * TABLE_HALF
SLOTS = 128
BF = jnp.bfloat16
F32 = jnp.float32
AXES = ("lon", "lat")


def dot(left, right, left_dim=1, right_dim=0):
    return lax.dot_general(
        left, right, (((left_dim,), (right_dim,)), ((), ())), preferred_element_type=F32
    )


def iota(shape, axis):
    return lax.broadcasted_iota(jnp.int32, shape, axis)


def load_cells(ref, scratch):
    for block in range(GROUPS):
        scratch[block * WIN_SPAN : (block + 1) * WIN_SPAN, :] = ref[block // 6, block % 6].astype(F32)
    return scratch[...]


def store_cells(ref, value):
    for block in range(GROUPS):
        ref[block // 6, block % 6] = value[block * WIN_SPAN : (block + 1) * WIN_SPAN].astype(ref.dtype)


def norm_parts(value):
    center = value - jnp.mean(value, axis=1, keepdims=True)
    spread = jnp.mean(center * center, axis=1, keepdims=True)
    inverse = lax.rsqrt(spread + NORM_EPS)
    return center * inverse, inverse


def norm_backward(unit, inverse, gain, cotangent):
    scaled = cotangent * gain
    first = jnp.mean(scaled, axis=1, keepdims=True)
    second = jnp.mean(scaled * unit, axis=1, keepdims=True)
    grad = inverse * (scaled - first - unit * second)
    return grad, jnp.sum(cotangent * unit, axis=0, keepdims=True)


def head_masked(value):
    value = value.astype(F32)
    lane = iota(value.shape, 1)
    parts = [
        jnp.where((lane >= h * HEAD_DIM) & (lane < (h + 1) * HEAD_DIM), value, 0.0).astype(BF)
        for h in range(HEADS)
    ]
    return jnp.concatenate(parts, axis=0)


def head_merge(stacked):
    lane = iota((WINDOW, CHANNELS), 1)
    merged = stacked[:WINDOW]
    for h in range(1, HEADS):
        merged = jnp.where(lane >= h * HEAD_DIM, stacked[h * WINDOW : (h + 1) * WINDOW], merged)
    return merged


def table_spots():
    lane = iota((1, TABLE_LANES), 1)
    inner = lane & 127
    local = (inner * 2850) >> 16
    group = jnp.where(inner < 4 * OFFSETS, 4 * (lane >> 7) + local, -1)
    return group, inner - OFFSETS * local


def table_gather():
    row = iota((TABLE_ROWS, 1), 0)
    outer = (row * 43) >> 8
    start = row + 6 * outer
    block = iota((TABLE_ROWS, 8 * WINDOW), 1) >> 3
    return jnp.where((block == start) | (block == start + 6), 1.0, 0.0).astype(BF)


def table_keep():
    group, _ = table_spots()
    row = iota((96, 1), 0)
    wanted = jnp.where(row >= 48, 6, 0) + (row & 7)
    return ((group == wanted) & ((row & 7) < 6))[None]


def table_repeat():
    group, offset = table_spots()
    offset = jnp.where(group >= 0, offset, -1)
    return jnp.where(iota((128, TABLE_LANES), 0) == offset, 1.0, 0.0).astype(BF)


def table_spread():
    column = iota((1, 256), 1)
    group = (column * 5462) >> 16
    wanted = (group >> 2) * 128 + (group & 3) * OFFSETS + 11 - (column - WIN_SPAN * group)
    wanted = jnp.where(column < WINDOW, wanted, -1)
    return jnp.where(iota((TABLE_LANES, 256), 0) == wanted, 1.0, 0.0).astype(BF)


def compact_table(table_ref, tiles):
    tiles[...] = jnp.zeros(tiles.shape, F32)
    tiles[:, :6, :OFFSETS] = table_ref[...].astype(F32).reshape(WINDOW, 6, OFFSETS)
    flat = tiles[...].reshape(8 * WINDOW, 128).astype(BF)
    repeated = dot(flat, table_repeat()).reshape(GROUPS, 96, TABLE_LANES)
    kept = jnp.where(table_keep(), repeated, 0.0).reshape(8 * WINDOW, TABLE_LANES).astype(BF)
    return dot(table_gather(), kept)


def marks(valid_ref, region_ref, shifted):
    lat = lax.axis_index("lat")
    column = iota((1, WINDOW), 1)
    row = iota((WINDOW, 1), 0)
    key = jnp.zeros((1, WINDOW), jnp.int32)
    label = jnp.zeros((WINDOW, 1), jnp.int32)
    total = valid_ref.shape[0]
    for block in range(GROUPS):
        level, inner = block // 6, block % 6
        source = lat * WIN_ROWS + inner
        own = jnp.int32(0)
        if shifted:
            source = source + WIN_ROWS // 2
            source = jnp.where(source >= total, source - total, source)
            level = (level + 1) % 2
            own = region_ref[level, source] + jnp.where(source < WIN_ROWS // 2, 4, 0)
            own = own + (8 if level < 1 else 0)
        usable = jnp.where(valid_ref[source] > 0, own, -1)
        key = jnp.where(column >= block * WIN_SPAN, usable, key)
        label = jnp.where(row >= block * WIN_SPAN, own, label)
    return label, key


def build_bias(table_ref, valid_ref, region_ref, shifted, tiles, bias):
    compact = compact_table(table_ref, tiles)
    turned = [compact.astype(BF)]
    for c in range(1, WIN_SPAN):
        turned.append(pltpu.roll(compact, TABLE_LANES - c, 1).astype(BF))
    spread = table_spread()
    for c in range(WIN_SPAN):
        part = dot(turned[c], spread)
        for half in range(2):
            bias[half, pl.ds(c, TABLE_ROWS, stride=WIN_SPAN), :] = part[:, half * 128 : (half + 1) * 128]
    label, key = marks(valid_ref, region_ref, shifted)
    allowed = (label == key) | (iota((WINDOW, WINDOW), 0) == iota((WINDOW, WINDOW), 1))
    minus = jnp.where(allowed, 0.0, -jnp.inf)
    for h in range(HEADS):
        rows = slice(h * WINDOW, (h + 1) * WINDOW)
        bias[0, rows, :] = bias[0, rows, :] + minus[:, :128]
        bias[1, rows, : WINDOW - 128] = bias[1, rows, : WINDOW - 128] + minus[:, 128:]


def attend(triple, bias):
    query = head_masked(triple[:, :CHANNELS])
    keys = triple[:, CHANNELS : 2 * CHANNELS]
    values = triple[:, 2 * CHANNELS :]
    bias = jnp.concatenate([bias[0], bias[1, :, : WINDOW - 128]], axis=1)
    scores = dot(query, keys, 1, 1) * SCALE + bias
    raised = jnp.exp(scores - jnp.max(scores, axis=1, keepdims=True))
    weight = raised * (1.0 / jnp.sum(raised, axis=1, keepdims=True))
    attention = weight.astype(BF)
    mixture = head_merge(dot(attention, values)).astype(BF)
    return query, keys, values, weight, attention, mixture


def attend_backward(query, keys, values, weight, attention, grad_mix):
    stacked = head_masked(grad_mix)
    grad_attention = dot(stacked, values, 1, 1).astype(BF).astype(F32)
    product = weight * grad_attention
    grad_scores = product - weight * jnp.sum(product, axis=1, keepdims=True)
    narrow = grad_scores.astype(BF)
    grad_query = head_merge(dot(narrow, keys)) * SCALE
    grad_keys = dot(narrow, query, 0, 0) * SCALE
    grad_values = dot(attention, stacked, 0, 0)
    grad_triple = jnp.concatenate([grad_query, grad_keys, grad_values], axis=1).astype(BF)
    return grad_scores, grad_triple


def store_payload(keep, send, pay, hidden, grad_triple, mixture, grad_out, grad_scores, gather, gains):
    weight = dot(hidden, grad_triple, 0, 0)
    proj = dot(mixture, grad_out, 0, 0)
    main = jnp.concatenate([weight, proj], axis=1)
    for c in range(6):
        start = (c % 3) * 24
        pay[c // 3, start : start + 24] = main[:, c * 128 : (c + 1) * 128].reshape(24, 8, 128)
    gather[0] = grad_scores[:, :128]
    gather[1] = jnp.concatenate(
        [grad_scores[:, 128:], jnp.zeros((STACK, 256 - WINDOW), F32)], axis=1
    )
    spread = table_spread()
    total = jnp.zeros((TABLE_ROWS, TABLE_LANES), F32)
    for c in range(WIN_SPAN):
        halves = [gather[half, pl.ds(c, TABLE_ROWS, stride=WIN_SPAN), :] for half in range(2)]
        part = dot(jnp.concatenate(halves, axis=1).astype(BF), spread, 1, 1)
        total = total + (part if c == 0 else pltpu.roll(part, c, 1))
    tiles = [total[:, c * 128 : (c + 1) * 128].reshape(9, 8, 128) for c in range(3)]
    pay[0, MAIN_HALF : MAIN_HALF + 9] = tiles[0]
    pay[0, MAIN_HALF + 9 : HALF - 1] = tiles[1][:5]
    pay[1, MAIN_HALF : MAIN_HALF + 4] = tiles[1][5:]
    pay[1, MAIN_HALF + 4 : HALF - 2] = tiles[2]
    pay[1, HALF - 2] = jnp.zeros((8, 128), F32)
    for half in range(2):
        pay[half, HALF - 1] = gain_tile(gains[half])
    core = lax.rem(lax.axis_index("lat"), 2)
    keep[...] = pay[core].astype(BF)
    send[...] = pay[1 - core].astype(BF)


def gain_tile(gain):
    if gain is None:
        return jnp.zeros((8, 128), F32)
    tail = jnp.concatenate([gain[:, 128:], jnp.zeros((1, 256 - CHANNELS), F32)], axis=1)
    return jnp.concatenate([gain[:, :128], tail, jnp.zeros((6, 128), F32)], axis=0)


def join_cores(keep_a, got_a, keep_b, got_b, out):
    core = lax.rem(lax.axis_index("lat"), 2)
    for s, (keep, got) in enumerate(((keep_a, got_a), (keep_b, got_b))):
        rows = slice(s * 8, s * 8 + 8)
        mine, theirs = keep[...].astype(F32), got[...].astype(F32)
        out[:MAIN_HALF, rows] = mine[:MAIN_HALF] + theirs[:MAIN_HALF]
        out[pl.ds(MAIN_HALF + core * TABLE_HALF, TABLE_HALF), rows] = mine[MAIN_HALF : HALF - 1]
        out[pl.ds(MAIN_HALF + (1 - core) * TABLE_HALF, TABLE_HALF), rows] = theirs[MAIN_HALF : HALF - 1]
        out[GAIN_SPOT, rows] = mine[HALF - 1] + theirs[HALF - 1]
        out[GAIN_SPOT + 1 :, rows] = jnp.zeros((SLOTS - GAIN_SPOT - 1, 8, 128), F32)


def join_cores_narrow(keep_a, got_a, keep_b, got_b, out, wide):
    join_cores(keep_a, got_a, keep_b, got_b, wide)
    out[...] = wide[...].astype(BF)


def sum_sources(count, parts, out):
    own = SLOTS // count
    value = parts[...].astype(F32).reshape(count // 2, 2, own, 16, 128)
    sums = jnp.sum(value, axis=0)
    both = sums[0] + sums[1]
    lat = lax.axis_index("lat")
    first = (lax.axis_index("lon") * 2 + lax.shift_right_logical(lat, 1)) * own
    lane = iota((16, 128), 1)
    row = iota((16, 128), 0)
    for slot in range(own):
        spot = first + slot
        is_table = (spot >= MAIN_HALF) & (spot < GAIN_SPOT)
        squares = sums[0, slot] * sums[0, slot] + sums[1, slot] * sums[1, slot]
        high = jnp.zeros((16, 128), F32)
        for s in range(2):
            partial = jnp.sum(jnp.where((row >> 3) == s, squares, 0.0), keepdims=True)
            upper = partial.astype(BF).astype(F32)
            value = jnp.where(lane == 96, upper, partial - upper)
            high = jnp.where((row == s * 8) & (lane >= 96) & (lane < 98), value, high)
        for side in range(2):
            result = jnp.where(is_table, sums[side, slot] + high, both[slot]).astype(BF)
            for dest in range(count // 2):
                out[(dest * 2 + side) * own + slot] = result


def plain_forward(
    fields, upstream, gains, w_in, w_out, table, valid, region,
    middle, own, by_lat, by_lon, by_both, hidden_out, triple_out, attention_out, mixture_out,
    cells, tiles, bias, pieces,
):
    value = load_cells(fields, cells)
    unit, _ = norm_parts(value)
    hidden = (unit * gains[0:1, :]).astype(BF)
    hidden_out[...] = hidden
    triple = dot(hidden, w_in[...]).astype(BF)
    triple_out[...] = triple
    build_bias(table, valid, region, False, tiles, bias)
    _, _, _, _, attention, mixture = attend(triple, bias)
    attention_out[...] = attention
    mixture_out[...] = mixture
    added = dot(mixture, w_out[...]).astype(BF).astype(F32)
    result = (value + added).astype(BF)
    middle[...] = result
    unit, _ = norm_parts(result.astype(F32))
    hidden = (unit * gains[1:2, :]).astype(BF).astype(F32)
    raw = load_cells(upstream, cells)
    for index, (ref, row_start, column_start) in enumerate(
        ((own, 3, 6), (by_lat, 0, 6), (by_lon, 3, 0), (by_both, 0, 0))
    ):
        for which, source in enumerate((hidden, raw)):
            for level in range(2):
                for inner in range(3):
                    start = ((1 - level) * 6 + row_start + inner) * WIN_SPAN + column_start
                    place = which * 36 + (level * 3 + inner) * 6
                    pieces[index, place : place + 6, :] = source[start : start + 6]
        ref[...] = pieces[index].astype(BF)


def shifted_bias(table, valid, region, bias, tiles):
    build_bias(table, valid, region, True, tiles, bias)


def gather_pieces(pieces, which, cells, forward):
    for index, piece in enumerate(pieces):
        far_row, far_column = index & 1, index >> 1
        for level in range(2):
            for inner in range(3):
                if forward:
                    row, column, target = 3 * far_row + inner, 6 * far_column, level
                else:
                    row, column, target = 3 - 3 * far_row + inner, 6 - 6 * far_column, 1 - level
                start = (target * 6 + row) * WIN_SPAN + column
                place = which * 36 + (level * 3 + inner) * 6
                cells[start : start + 6, :] = piece[place : place + 6]
    return cells[...]


def shifted_core(
    own, by_lat, by_lon, by_both, bias, w_in, w_out,
    own_out, lat_out, lon_out, both_out, hidden_out, cot_out, triple_out, mixture_out, scores_out,
    cells, pieces_out,
):
    pieces = [ref[...].astype(F32) for ref in (own, by_lat, by_lon, by_both)]
    hidden = gather_pieces(pieces, 0, cells, True).astype(BF)
    grad_out = gather_pieces(pieces, 1, cells, True).astype(BF)
    hidden_out[...] = hidden
    cot_out[...] = grad_out
    triple = dot(hidden, w_in[...]).astype(BF)
    query, keys, values, weight, attention, mixture = attend(triple, bias)
    mixture_out[...] = mixture
    added = dot(mixture, w_out[...]).astype(BF).astype(F32)
    grad_mix = dot(grad_out, w_out[...], 1, 1).astype(BF)
    grad_scores, grad_triple = attend_backward(query, keys, values, weight, attention, grad_mix)
    triple_out[...] = grad_triple
    scores_out[...] = grad_scores.astype(BF)
    grad_hidden = dot(grad_triple, w_in[...], 1, 1).astype(BF).astype(F32)
    for index, ref in enumerate((own_out, lat_out, lon_out, both_out)):
        far_row, far_column = index & 1, index >> 1
        for which, source in enumerate((added, grad_hidden)):
            for level in range(2):
                for inner in range(3):
                    start = (level * 6 + 3 * far_row + inner) * WIN_SPAN + 6 * far_column
                    place = which * 36 + (level * 3 + inner) * 6
                    pieces_out[index, place : place + 6, :] = source[start : start + 6]
        ref[...] = pieces_out[index].astype(BF)


def shifted_sums(hidden, cot, triple, mixture, scores, keep, send, pay, gather):
    store_payload(
        keep, send, pay, hidden[...], triple[...], mixture[...], cot[...],
        scores[...].astype(F32), gather, (None, None),
    )


def plain_backward(
    own, by_lat, by_lon, by_both, middle, upstream, fields, gains, w_in, w_out,
    hidden_in, triple_in, attention_in, mixture_in,
    updated, grad_fields, keep, send,
    cells, pay, gather,
):
    pieces = [ref[...].astype(F32) for ref in (own, by_lat, by_lon, by_both)]
    base = middle[...].astype(F32)
    store_cells(updated, base + gather_pieces(pieces, 0, cells, False))
    grad_hidden = gather_pieces(pieces, 1, cells, False)
    unit, inverse = norm_parts(base)
    norm_grad, gain_b = norm_backward(unit, inverse, gains[1:2, :], grad_hidden)
    grad_middle = (load_cells(upstream, cells) + norm_grad).astype(BF)
    grad_mix = dot(grad_middle, w_out[...], 1, 1).astype(BF)
    triple = triple_in[...]
    attention = attention_in[...]
    grad_scores, grad_triple = attend_backward(
        head_masked(triple[:, :CHANNELS]),
        triple[:, CHANNELS : 2 * CHANNELS],
        triple[:, 2 * CHANNELS :],
        attention.astype(F32),
        attention,
        grad_mix,
    )
    grad_hidden = dot(grad_triple, w_in[...], 1, 1).astype(BF).astype(F32)
    unit, inverse = norm_parts(load_cells(fields, cells))
    norm_grad, gain_a = norm_backward(unit, inverse, gains[0:1, :], grad_hidden)
    store_cells(grad_fields, grad_middle.astype(F32) + norm_grad)
    store_payload(
        keep, send, pay, hidden_in[...], grad_triple, mixture_in[...], grad_middle,
        grad_scores, gather, (gain_a, gain_b),
    )


def finish(own, other, grad_gains, grad_in, grad_proj, grad_bias, tiles, halves):
    core = lax.rem(lax.axis_index("lat"), 2)
    halves[core] = own[...].astype(F32)
    halves[1 - core] = other[...].astype(F32)
    keep = table_keep()
    gather = table_gather()
    repeat = table_repeat()
    for s in range(2):
        rows = slice(s * 8, s * 8 + 8)
        main = jnp.concatenate(
            [halves[c // 3, (c % 3) * 24 : (c % 3) * 24 + 24, rows].reshape(CHANNELS, 128)
             for c in range(6)], axis=1
        )
        weight = main[:, : 3 * CHANNELS]
        factor = 1.0 / jnp.sqrt(jnp.sum(weight * weight, keepdims=True) / weight.size + RMS_EPS)
        grad_in[s] = weight * factor
        proj = main[:, 3 * CHANNELS :]
        factor = 1.0 / jnp.sqrt(jnp.sum(proj * proj, keepdims=True) / proj.size + RMS_EPS)
        grad_proj[s] = proj * factor
        gain = halves[s, GAIN_SPOT, :8]
        factor = 1.0 / jnp.sqrt(jnp.sum(gain * gain, keepdims=True) / CHANNELS + RMS_EPS)
        grad_gains[s : s + 1, :128] = gain[0:1, :] * factor
        grad_gains[s : s + 1, 128:] = gain[1:2, : CHANNELS - 128] * factor
        every = halves[:, MAIN_HALF:GAIN_SPOT, rows]
        lane = iota((1, 1, 1, 128), 3)
        squares = jnp.sum(jnp.where((lane >= 96) & (lane < 98), every, 0.0), axis=(0, 1))
        squares = jnp.sum(squares, keepdims=True)
        start = MAIN_HALF + core * TABLE_HALF
        found = [halves[half, pl.ds(start, TABLE_HALF), rows] for half in range(2)]
        found = jnp.concatenate([found[0], found[1][: TABLE_HALF - 1]], axis=0)
        table = jnp.concatenate(
            [found[c * 9 : (c + 1) * 9].reshape(TABLE_ROWS, 128) for c in range(3)], axis=1
        ).astype(BF)
        wide = dot(gather, table, 0, 0).reshape(GROUPS, 96, TABLE_LANES)
        wide = jnp.where(keep, wide, 0.0).reshape(8 * WINDOW, TABLE_LANES).astype(BF)
        tiles[...] = dot(wide, repeat, 1, 1).reshape(WINDOW, 8, 128)
        factor = 1.0 / jnp.sqrt(squares / (4 * WINDOW * 6 * OFFSETS) + RMS_EPS)
        spread = tiles[:, :6, :OFFSETS] * factor[None]
        grad_bias[s, 0, 0] = spread.reshape(HEADS, 2, 2, 6, 6, OFFSETS)


def whole():
    return pl.BlockSpec(memory_space=pltpu.VMEM)


def scalars():
    return pl.BlockSpec(memory_space=pltpu.SMEM)


def picked(shape, s):
    return pl.BlockSpec((None,) + shape, lambda i: (s,) + (0,) * len(shape))


def table_spec(s):
    return pl.BlockSpec(
        (None, None, None, HEADS, 2, 2, 6, 6, OFFSETS), lambda i: (s,) + (0,) * 8
    )


def run(body, outs, in_specs, scratch, args):
    return pl.pallas_call(
        body,
        grid=(1,),
        out_shape=[jax.ShapeDtypeStruct(shape, kind) for shape, kind in outs],
        in_specs=in_specs,
        out_specs=[whole() for _ in outs],
        scratch_shapes=[pltpu.VMEM(shape, F32) for shape in scratch],
        compiler_params=pltpu.CompilerParams(vmem_limit_bytes=40 * 1024 * 1024),
    )(*args)


CELLS = (WINDOW, CHANNELS)
PIECE = ((72, CHANNELS), BF)
FIELD = (2, WIN_ROWS, WIN_SPAN, CHANNELS)
WEIGHT = (CHANNELS, 3 * CHANNELS)
SQUARE = (CHANNELS, CHANNELS)
SCORES = (STACK, WINDOW)
SPREAD = (2, STACK, 128)
TABLE = (WINDOW, 8, 128)
PAY = (2, HALF, 8, 128)
PART = ((HALF, 8, 128), BF)
MESSAGE = ((SLOTS, 16, 128), BF)


def exchange(pieces, sign):
    lons, lats = lax.axis_size("lon"), lax.axis_size("lat")
    own, by_lat, by_lon, by_both = pieces

    def move(block, lon_step, lat_step):
        route = []
        for lon in range(lons):
            for lat in range(lats):
                target = ((lon + sign * lon_step) % lons) * lats + (lat + sign * lat_step) % lats
                route.append((lon * lats + lat, target))
        return lax.ppermute(block, AXES, route)

    return [own, move(by_lat, 0, 1), move(by_lon, 1, 0), move(by_both, 1, 1)]


def on_device(fields, upstream, gains, project_in, project_out, earth_bias, row_valid, regions):
    middle, *rest = run(
        plain_forward,
        [(CELLS, BF), PIECE, PIECE, PIECE, PIECE, (CELLS, BF), ((WINDOW, 3 * CHANNELS), BF),
         (SCORES, BF), (CELLS, BF)],
        [whole(), whole(), whole(), picked(WEIGHT, 0), picked(SQUARE, 0), table_spec(0),
         scalars(), scalars()],
        [CELLS, TABLE, SPREAD, (4, 72, CHANNELS)],
        (fields, upstream, gains, project_in, project_out, earth_bias, row_valid, regions),
    )
    pieces = exchange(rest[:4], -1)
    saved = rest[4:]
    (bias,) = run(
        shifted_bias,
        [(SPREAD, F32)],
        [table_spec(1), scalars(), scalars()],
        [TABLE],
        (earth_bias, row_valid, regions),
    )
    *back, hidden, cot, triple, mixture, scores = run(
        shifted_core,
        [PIECE, PIECE, PIECE, PIECE, (CELLS, BF), (CELLS, BF), ((WINDOW, 3 * CHANNELS), BF),
         (CELLS, BF), (SCORES, BF)],
        [whole()] * 5 + [picked(WEIGHT, 1), picked(SQUARE, 1)],
        [CELLS, (4, 72, CHANNELS)],
        (*pieces, bias, project_in, project_out),
    )
    back = exchange(back, 1)
    keep_b, send_b = run(
        shifted_sums,
        [PART, PART],
        [whole()] * 5,
        [PAY, SPREAD],
        (hidden, cot, triple, mixture, scores),
    )
    got_b = other_core(send_b)
    updated, grad_fields, keep_a, send_a = run(
        plain_backward,
        [(FIELD, BF), (FIELD, BF), PART, PART],
        [whole()] * 8 + [picked(WEIGHT, 0), picked(SQUARE, 0)] + [whole()] * 4,
        [CELLS, PAY, SPREAD],
        (*back, middle, upstream, fields, gains, project_in, project_out, *saved),
    )
    got_a = other_core(send_a)
    (joined,) = run(
        join_cores_narrow, [MESSAGE], [whole()] * 4, [MESSAGE[0]], (keep_a, got_a, keep_b, got_b)
    )
    lons, lats = lax.axis_size("lon"), lax.axis_size("lat")
    groups = [[d for d in range(lons * lats) if d % 2 == core] for core in range(2)]

    def trade(block):
        return lax.all_to_all(block, AXES, 0, 0, axis_index_groups=groups, tiled=True)

    (summed,) = run(
        functools.partial(sum_sources, lons * lats // 2), [MESSAGE], [whole()], [], (trade(joined),)
    )
    mine = trade(summed)
    grad_gains, grad_in, grad_proj, grad_bias = run(
        finish,
        [((2, CHANNELS), F32), ((2,) + WEIGHT, F32), ((2,) + SQUARE, F32),
         ((2, 1, 1, HEADS, 2, 2, 6, 6, OFFSETS), F32)],
        [whole()] * 2,
        [TABLE, (2,) + MESSAGE[0]],
        (mine, other_core(mine)),
    )
    return (updated, grad_fields, grad_gains, grad_in, grad_proj, grad_bias)


def other_core(block):
    count = lax.axis_size("lon") * lax.axis_size("lat")
    return lax.ppermute(block, AXES, [(d, d ^ 1) for d in range(count)])


def solution(mesh):
    spec = P(None, "lat", "lon", None)
    bias_spec = P(None, None, "lat", None, None, None, None, None, None)
    return jax.shard_map(
        on_device,
        mesh=mesh,
        in_specs=(spec, spec, P(), P(), P(), bias_spec, P(), P()),
        out_specs=(spec, spec, P(), P(), P(), bias_spec),
        check_vma=False,
    )
```

```python
import functools

import jax
import jax.numpy as jnp
from jax import lax
from jax.experimental import pallas as pl
from jax.experimental.pallas import tpu as pltpu
from jax.sharding import PartitionSpec as P

CHANNELS = 192
HEADS = 6
HEAD_DIM = 32
WIN_ROWS = 6
WIN_SPAN = 12
WINDOW = 144
STACK = HEADS * WINDOW
GROUPS = 12
OFFSETS = 23
TABLE_LANES = 384
TABLE_ROWS = 72
NORM_EPS = 1e-05
RMS_EPS = 1e-06
SCALE = HEAD_DIM ** (-0.5)
MAIN_HALF = 72
TABLE_HALF = 14
HALF = MAIN_HALF + TABLE_HALF + 1
TABLE_SPOT = 2 * MAIN_HALF
GAIN_SPOT = TABLE_SPOT + 4 * TABLE_HALF
BF = jnp.bfloat16
F32 = jnp.float32
AXES = ("lon", "lat")


def dot(left, right, left_dim=1, right_dim=0):
    return lax.dot_general(
        left, right, (((left_dim,), (right_dim,)), ((), ())), preferred_element_type=F32
    )


def iota(shape, axis):
    return lax.broadcasted_iota(jnp.int32, shape, axis)


def load_cells(ref, scratch):
    value = ref[...].astype(F32)
    for block in range(GROUPS):
        scratch[block * WIN_SPAN : (block + 1) * WIN_SPAN, :] = value[block % 6, :, block // 6, :]
    return scratch[...]


def store_cells(ref, value, scratch):
    for block in range(GROUPS):
        scratch[block % 6, :, block // 6, :] = value[block * WIN_SPAN : (block + 1) * WIN_SPAN]
    ref[...] = scratch[...].astype(ref.dtype)


def norm_parts(value):
    center = value - jnp.mean(value, axis=1, keepdims=True)
    spread = jnp.mean(center * center, axis=1, keepdims=True)
    inverse = lax.rsqrt(spread + NORM_EPS)
    return center * inverse, inverse


def norm_backward(unit, inverse, gain, cotangent):
    scaled = cotangent * gain
    first = jnp.mean(scaled, axis=1, keepdims=True)
    second = jnp.mean(scaled * unit, axis=1, keepdims=True)
    grad = inverse * (scaled - first - unit * second)
    return grad, jnp.sum(cotangent * unit, axis=0, keepdims=True)


def head_masked(value):
    value = value.astype(F32)
    lane = iota(value.shape, 1)
    parts = [
        jnp.where((lane >= h * HEAD_DIM) & (lane < (h + 1) * HEAD_DIM), value, 0.0).astype(BF)
        for h in range(HEADS)
    ]
    return jnp.concatenate(parts, axis=0)


def head_merge(stacked):
    lane = iota((WINDOW, CHANNELS), 1)
    merged = stacked[:WINDOW]
    for h in range(1, HEADS):
        merged = jnp.where(lane >= h * HEAD_DIM, stacked[h * WINDOW : (h + 1) * WINDOW], merged)
    return merged


def table_spots():
    lane = iota((1, TABLE_LANES), 1)
    inner = lane & 127
    local = (inner * 2850) >> 16
    group = jnp.where(inner < 4 * OFFSETS, 4 * (lane >> 7) + local, -1)
    return group, inner - OFFSETS * local


def table_gather():
    start = iota((TABLE_ROWS, 1), 0) * GROUPS
    column = iota((TABLE_ROWS, STACK), 1)
    return jnp.where((column >= start) & (column < start + GROUPS), 1.0, 0.0).astype(BF)


def table_mask(wide):
    group, _ = table_spots()
    row = iota((24, 1), 0)
    row = jnp.where(row >= GROUPS, row - GROUPS, row)
    keep = group == (row & 1) * 6 + (row >> 1)
    wide = jnp.where(keep[None], wide.reshape(STACK // 24, 24, TABLE_LANES), 0.0)
    return wide.reshape(STACK, TABLE_LANES).astype(BF)


def table_repeat():
    group, offset = table_spots()
    offset = jnp.where(group >= 0, offset, -1)
    return jnp.where(iota((OFFSETS, TABLE_LANES), 0) == offset, 1.0, 0.0).astype(BF)


def table_spread():
    column = iota((1, 256), 1)
    group = (column * 5462) >> 16
    wanted = (group >> 2) * 128 + (group & 3) * OFFSETS + 11 - (column - WIN_SPAN * group)
    wanted = jnp.where(column < WINDOW, wanted, -1)
    return jnp.where(iota((TABLE_LANES, 256), 0) == wanted, 1.0, 0.0).astype(BF)


def compact_table(table_ref, gather, repeat):
    flat = table_ref[...].astype(F32).reshape(STACK, OFFSETS).astype(BF)
    return dot(gather[...], table_mask(dot(flat, repeat[...])))


def marks(valid_ref, region_ref, shifted):
    lat = lax.axis_index("lat")
    column = iota((1, WINDOW), 1)
    row = iota((WINDOW, 1), 0)
    key = jnp.zeros((1, WINDOW), jnp.int32)
    label = jnp.zeros((WINDOW, 1), jnp.int32)
    total = valid_ref.shape[0]
    for block in range(GROUPS):
        level, inner = block // 6, block % 6
        source = lat * WIN_ROWS + inner
        own = jnp.int32(0)
        if shifted:
            source = source + WIN_ROWS // 2
            source = jnp.where(source >= total, source - total, source)
            level = (level + 1) % 2
            own = region_ref[level, source] + jnp.where(source < WIN_ROWS // 2, 4, 0)
            own = own + (8 if level < 1 else 0)
        usable = jnp.where(valid_ref[source] > 0, own, -1)
        key = jnp.where(column >= block * WIN_SPAN, usable, key)
        label = jnp.where(row >= block * WIN_SPAN, own, label)
    return label, key


def build_bias(table_ref, valid_ref, region_ref, shifted, bias, gather, repeat, spread_ref):
    compact = compact_table(table_ref, gather, repeat)
    turned = [compact.astype(BF)]
    for c in range(1, WIN_SPAN):
        turned.append(pltpu.roll(compact, TABLE_LANES - c, 1).astype(BF))
    spread = spread_ref[...]
    for c in range(WIN_SPAN):
        part = dot(turned[c], spread)
        for half in range(2):
            bias[half, pl.ds(c, TABLE_ROWS, stride=WIN_SPAN), :] = part[:, half * 128 : (half + 1) * 128]
    label, key = marks(valid_ref, region_ref, shifted)
    allowed = (label == key) | (iota((WINDOW, WINDOW), 0) == iota((WINDOW, WINDOW), 1))
    minus = jnp.where(allowed, 0.0, -jnp.inf)
    for h in range(HEADS):
        rows = slice(h * WINDOW, (h + 1) * WINDOW)
        bias[0, rows, :] = bias[0, rows, :] + minus[:, :128]
        bias[1, rows, : WINDOW - 128] = bias[1, rows, : WINDOW - 128] + minus[:, 128:]


def attend(triple, bias):
    query = head_masked(triple[:, :CHANNELS])
    keys = triple[:, CHANNELS : 2 * CHANNELS]
    values = triple[:, 2 * CHANNELS :]
    bias = jnp.concatenate([bias[0], bias[1, :, : WINDOW - 128]], axis=1)
    scores = dot(query, keys, 1, 1) * SCALE + bias
    raised = jnp.exp(scores - jnp.max(scores, axis=1, keepdims=True))
    weight = raised * (1.0 / jnp.sum(raised, axis=1, keepdims=True))
    attention = weight.astype(BF)
    mixture = head_merge(dot(attention, values)).astype(BF)
    return query, keys, values, weight, attention, mixture


def attend_backward(query, keys, values, weight, attention, grad_mix):
    stacked = head_masked(grad_mix)
    grad_attention = dot(stacked, values, 1, 1).astype(BF).astype(F32)
    product = weight * grad_attention
    grad_scores = product - weight * jnp.sum(product, axis=1, keepdims=True)
    narrow = grad_scores.astype(BF)
    grad_query = head_merge(dot(narrow, keys)) * SCALE
    grad_keys = dot(narrow, query, 0, 0) * SCALE
    grad_values = dot(attention, stacked, 0, 0)
    grad_triple = jnp.concatenate([grad_query, grad_keys, grad_values], axis=1).astype(BF)
    return grad_scores, grad_triple


def store_payload(keep, send, pay, hidden, grad_triple, mixture, grad_out, grad_scores, gather, gains, spread_ref):
    weight = dot(hidden, grad_triple, 0, 0)
    proj = dot(mixture, grad_out, 0, 0)
    main = jnp.concatenate([weight, proj], axis=1)
    for c in range(6):
        start = (c % 3) * 24
        pay[c // 3, start : start + 24] = main[:, c * 128 : (c + 1) * 128].reshape(24, 8, 128)
    gather[0] = grad_scores[:, :128]
    gather[1] = jnp.concatenate(
        [grad_scores[:, 128:], jnp.zeros((STACK, 256 - WINDOW), F32)], axis=1
    )
    spread = spread_ref[...]
    total = jnp.zeros((TABLE_ROWS, TABLE_LANES), F32)
    for c in range(WIN_SPAN):
        halves = [gather[half, pl.ds(c, TABLE_ROWS, stride=WIN_SPAN), :] for half in range(2)]
        part = dot(jnp.concatenate(halves, axis=1).astype(BF), spread, 1, 1)
        total = total + (part if c == 0 else pltpu.roll(part, c, 1))
    tiles = [total[:, c * 128 : (c + 1) * 128].reshape(9, 8, 128) for c in range(3)]
    pay[0, MAIN_HALF : MAIN_HALF + 9] = tiles[0]
    pay[0, MAIN_HALF + 9 : HALF - 1] = tiles[1][:5]
    pay[1, MAIN_HALF : MAIN_HALF + 4] = tiles[1][5:]
    pay[1, MAIN_HALF + 4 : HALF - 2] = tiles[2]
    pay[1, HALF - 2] = jnp.zeros((8, 128), F32)
    for half in range(2):
        pay[half, HALF - 1] = gain_tile(gains[half])
    core = lax.rem(lax.axis_index("lat"), 2)
    keep[...] = pay[core].astype(BF)
    send[...] = pay[1 - core].astype(BF)


def gain_tile(gain):
    if gain is None:
        return jnp.zeros((8, 128), F32)
    tail = jnp.concatenate([gain[:, 128:], jnp.zeros((1, 256 - CHANNELS), F32)], axis=1)
    return jnp.concatenate([gain[:, :128], tail, jnp.zeros((6, 128), F32)], axis=0)


def join_cores(keep_a, got_a, keep_b, got_b, out, wide):
    core = lax.rem(lax.axis_index("lat"), 2)
    for s, (keep, got) in enumerate(((keep_a, got_a), (keep_b, got_b))):
        mine, theirs = keep[...].astype(F32), got[...].astype(F32)
        wide[s * MAIN_HALF : (s + 1) * MAIN_HALF] = mine[:MAIN_HALF] + theirs[:MAIN_HALF]
        start = TABLE_SPOT + 2 * s * TABLE_HALF
        wide[pl.ds(start + core * TABLE_HALF, TABLE_HALF)] = mine[MAIN_HALF : HALF - 1]
        wide[pl.ds(start + (1 - core) * TABLE_HALF, TABLE_HALF)] = theirs[MAIN_HALF : HALF - 1]
        if s == 0:
            wide[GAIN_SPOT] = mine[HALF - 1] + theirs[HALF - 1]
    if wide.shape[0] > GAIN_SPOT + 1:
        wide[GAIN_SPOT + 1 :] = jnp.zeros((wide.shape[0] - GAIN_SPOT - 1, 8, 128), F32)
    out[...] = wide[...].astype(BF)


def table_places(own):
    place = lax.axis_index("lon") * own + iota((own, 1, 1), 0)
    return (place >= TABLE_SPOT) & (place < GAIN_SPOT)


def sum_sources(count, parts, out):
    own = out.shape[0]
    sums = jnp.sum(parts[...].astype(F32).reshape(count, own, 8, 128), axis=0)
    squares = jnp.sum(sums * sums, axis=(1, 2), keepdims=True)
    noted = (iota(sums.shape, 1) == 0) & (iota(sums.shape, 2) == 96) & table_places(own)
    out[...] = jnp.where(noted, squares, sums)


def spread_sums(count, mine, theirs, out):
    own = mine.shape[0]
    first = iota(mine.shape, 1) == 0
    lane = iota(mine.shape, 2)
    value = mine[...]
    both = value + theirs[...]
    upper = both.astype(BF).astype(F32)
    lower = jnp.sum(jnp.where(first & (lane == 96), both - upper, 0.0), axis=(1, 2), keepdims=True)
    noted = jnp.where(first & (lane == 96), upper, value)
    noted = jnp.where(first & (lane == 97), lower, noted)
    result = jnp.where(table_places(own), noted, both)[None]
    out[...] = jnp.broadcast_to(result, (count,) + mine.shape).reshape(out.shape).astype(BF)


def constant_tables(gather, repeat, spread):
    gather[...] = table_gather()
    repeat[...] = table_repeat()
    spread[...] = table_spread()


def plain_forward(
    fields, upstream, gains, w_in, w_out, table, valid, region, gather, repeat, spread,
    middle, own, by_lat, by_lon, by_both, hidden_out, triple_out, attention_out, mixture_out,
    cells, bias, pieces,
):
    build_bias(table, valid, region, False, bias, gather, repeat, spread)
    value = load_cells(fields, cells)
    unit, _ = norm_parts(value)
    hidden = (unit * gains[0:1, :]).astype(BF)
    hidden_out[...] = hidden
    triple = dot(hidden, w_in[...]).astype(BF)
    triple_out[...] = triple
    _, _, _, _, attention, mixture = attend(triple, bias)
    attention_out[...] = attention
    mixture_out[...] = mixture
    added = dot(mixture, w_out[...]).astype(BF).astype(F32)
    result = (value + added).astype(BF)
    middle[...] = result
    unit, _ = norm_parts(result.astype(F32))
    hidden = (unit * gains[1:2, :]).astype(BF).astype(F32)
    raw = load_cells(upstream, cells)
    for index, (ref, row_start, column_start) in enumerate(
        ((own, 3, 6), (by_lat, 0, 6), (by_lon, 3, 0), (by_both, 0, 0))
    ):
        for which, source in enumerate((hidden, raw)):
            for level in range(2):
                for inner in range(3):
                    start = ((1 - level) * 6 + row_start + inner) * WIN_SPAN + column_start
                    place = which * 36 + (level * 3 + inner) * 6
                    pieces[index, place : place + 6, :] = source[start : start + 6]
        ref[...] = pieces[index].astype(BF)


def shifted_bias(table, valid, region, gather, repeat, spread, bias):
    build_bias(table, valid, region, True, bias, gather, repeat, spread)


def gather_pieces(pieces, which, cells, forward):
    for index, piece in enumerate(pieces):
        far_row, far_column = index & 1, index >> 1
        for level in range(2):
            for inner in range(3):
                if forward:
                    row, column, target = 3 * far_row + inner, 6 * far_column, level
                else:
                    row, column, target = 3 - 3 * far_row + inner, 6 - 6 * far_column, 1 - level
                start = (target * 6 + row) * WIN_SPAN + column
                place = which * 36 + (level * 3 + inner) * 6
                cells[start : start + 6, :] = piece[place : place + 6]
    return cells[...]


def shifted_core(
    own, by_lat, by_lon, by_both, bias, w_in, w_out,
    own_out, lat_out, lon_out, both_out, hidden_out, cot_out, triple_out, mixture_out, scores_out,
    cells, pieces_out,
):
    pieces = [ref[...].astype(F32) for ref in (own, by_lat, by_lon, by_both)]
    hidden = gather_pieces(pieces, 0, cells, True).astype(BF)
    grad_out = gather_pieces(pieces, 1, cells, True).astype(BF)
    hidden_out[...] = hidden
    cot_out[...] = grad_out
    triple = dot(hidden, w_in[...]).astype(BF)
    query, keys, values, weight, attention, mixture = attend(triple, bias)
    mixture_out[...] = mixture
    added = dot(mixture, w_out[...]).astype(BF).astype(F32)
    grad_mix = dot(grad_out, w_out[...], 1, 1).astype(BF)
    grad_scores, grad_triple = attend_backward(query, keys, values, weight, attention, grad_mix)
    triple_out[...] = grad_triple
    scores_out[...] = grad_scores.astype(BF)
    grad_hidden = dot(grad_triple, w_in[...], 1, 1).astype(BF).astype(F32)
    for index, ref in enumerate((own_out, lat_out, lon_out, both_out)):
        far_row, far_column = index & 1, index >> 1
        for which, source in enumerate((added, grad_hidden)):
            for level in range(2):
                for inner in range(3):
                    start = (level * 6 + 3 * far_row + inner) * WIN_SPAN + 6 * far_column
                    place = which * 36 + (level * 3 + inner) * 6
                    pieces_out[index, place : place + 6, :] = source[start : start + 6]
        ref[...] = pieces_out[index].astype(BF)


def shifted_sums(hidden, cot, triple, mixture, scores, spread, keep, send, pay, gather):
    store_payload(
        keep, send, pay, hidden[...], triple[...], mixture[...], cot[...],
        scores[...].astype(F32), gather, (None, None), spread,
    )


def plain_backward(
    own, by_lat, by_lon, by_both, middle, upstream, fields, gains, w_in, w_out,
    hidden_in, triple_in, attention_in, mixture_in, spread,
    keep, send, middle_out, hidden_out,
    cells, pay, gather,
):
    pieces = [ref[...].astype(F32) for ref in (own, by_lat, by_lon, by_both)]
    grad_hidden = gather_pieces(pieces, 1, cells, False)
    unit, inverse = norm_parts(middle[...].astype(F32))
    norm_grad, gain_b = norm_backward(unit, inverse, gains[1:2, :], grad_hidden)
    grad_middle = (load_cells(upstream, cells) + norm_grad).astype(BF)
    middle_out[...] = grad_middle
    grad_mix = dot(grad_middle, w_out[...], 1, 1).astype(BF)
    triple = triple_in[...]
    attention = attention_in[...]
    grad_scores, grad_triple = attend_backward(
        head_masked(triple[:, :CHANNELS]),
        triple[:, CHANNELS : 2 * CHANNELS],
        triple[:, 2 * CHANNELS :],
        attention.astype(F32),
        attention,
        grad_mix,
    )
    grad_hidden = dot(grad_triple, w_in[...], 1, 1).astype(BF)
    hidden_out[...] = grad_hidden
    unit, _ = norm_parts(load_cells(fields, cells))
    gain_a = jnp.sum(grad_hidden.astype(F32) * unit, axis=0, keepdims=True)
    store_payload(
        keep, send, pay, hidden_in[...], grad_triple, mixture_in[...], grad_middle,
        grad_scores, gather, (gain_a, gain_b), spread,
    )


def plain_fields(
    own, by_lat, by_lon, by_both, middle, fields, gains, grad_middle, grad_hidden,
    updated, grad_fields,
    cells, native,
):
    pieces = [ref[...].astype(F32) for ref in (own, by_lat, by_lon, by_both)]
    store_cells(updated, middle[...].astype(F32) + gather_pieces(pieces, 0, cells, False), native)
    unit, inverse = norm_parts(load_cells(fields, cells))
    norm_grad, _ = norm_backward(unit, inverse, gains[0:1, :], grad_hidden[...].astype(F32))
    store_cells(grad_fields, grad_middle[...].astype(F32) + norm_grad, native)


def finish(own, other, gather, repeat, grad_in, grad_proj, grad_bias, grad_gains, halves):
    core = lax.rem(lax.axis_index("lat"), 2)
    s = pl.program_id(0)

    @pl.when(s == 0)
    def _():
        halves[core] = own[...].astype(F32)
        halves[1 - core] = other[...].astype(F32)
        for which in range(2):
            gain = halves[which, GAIN_SPOT]
            factor = 1.0 / jnp.sqrt(jnp.sum(gain * gain, keepdims=True) / CHANNELS + RMS_EPS)
            grad_gains[which : which + 1, :128] = gain[0:1, :] * factor
            grad_gains[which : which + 1, 128:] = gain[1:2, : CHANNELS - 128] * factor

    main = jnp.concatenate(
        [halves[c // 3, pl.ds(s * MAIN_HALF + (c % 3) * 24, 24)].reshape(CHANNELS, 128)
         for c in range(6)],
        axis=1,
    )
    weight = main[:, : 3 * CHANNELS]
    factor = 1.0 / jnp.sqrt(jnp.sum(weight * weight, keepdims=True) / weight.size + RMS_EPS)
    grad_in[...] = weight * factor
    proj = main[:, 3 * CHANNELS :]
    factor = 1.0 / jnp.sqrt(jnp.sum(proj * proj, keepdims=True) / proj.size + RMS_EPS)
    grad_proj[...] = proj * factor
    start = TABLE_SPOT + 2 * s * TABLE_HALF
    every = halves[:, pl.ds(start, 2 * TABLE_HALF)]
    lane = iota((1, 1, 1, 128), 3)
    squares = jnp.sum(jnp.where((lane >= 96) & (lane < 98), every, 0.0), axis=(0, 1))
    squares = jnp.sum(squares, keepdims=True)
    start = start + core * TABLE_HALF
    found = [halves[half, pl.ds(start, TABLE_HALF)] for half in range(2)]
    found = jnp.concatenate([found[0], found[1][: TABLE_HALF - 1]], axis=0)
    table = jnp.concatenate(
        [found[c * 9 : (c + 1) * 9].reshape(TABLE_ROWS, 128) for c in range(3)], axis=1
    ).astype(BF)
    wide = table_mask(dot(gather[...], table, 0, 0))
    factor = 1.0 / jnp.sqrt(squares / (4 * WINDOW * 6 * OFFSETS) + RMS_EPS)
    spread = dot(wide, repeat[...], 1, 1) * factor
    grad_bias[...] = spread.reshape(HEADS, 2, 6, 6, 2, OFFSETS)


def whole():
    return pl.BlockSpec(memory_space=pltpu.VMEM)


def scalars():
    return pl.BlockSpec(memory_space=pltpu.SMEM)


def picked(shape, s):
    return pl.BlockSpec((None,) + shape, lambda i: (s,) + (0,) * len(shape))


def stepped(shape):
    return pl.BlockSpec((None,) + shape, lambda i: (i,) + (0,) * len(shape))


def table_spec(s):
    return pl.BlockSpec(
        (None, None, None, HEADS, 2, 6, 6, 2, OFFSETS), lambda i: (s,) + (0,) * 8
    )


def run(body, outs, in_specs, scratch, args, out_specs=None, steps=1, cost=None):
    return pl.pallas_call(
        body,
        grid=(steps,),
        out_shape=[jax.ShapeDtypeStruct(shape, kind) for shape, kind in outs],
        in_specs=in_specs,
        out_specs=out_specs or [whole() for _ in outs],
        scratch_shapes=[
            pltpu.VMEM(shape, F32) if isinstance(shape, tuple) else shape for shape in scratch
        ],
        cost_estimate=cost and pl.CostEstimate(flops=cost, bytes_accessed=0, transcendentals=0),
        compiler_params=pltpu.CompilerParams(vmem_limit_bytes=40 * 1024 * 1024),
    )(*args)


CELLS = (WINDOW, CHANNELS)
PIECE = ((72, CHANNELS), BF)
NATIVE = (WIN_ROWS, WIN_SPAN, 2, CHANNELS)
WEIGHT = (CHANNELS, 3 * CHANNELS)
SQUARE = (CHANNELS, CHANNELS)
SCORES = (STACK, WINDOW)
SPREAD = (2, STACK, 128)
PAY = (2, HALF, 8, 128)
PART = ((HALF, 8, 128), BF)
GRADS = [((2,) + WEIGHT, F32), ((2,) + SQUARE, F32), ((2, 1, 1, HEADS, 2, 6, 6, 2, OFFSETS), F32)]


def exchange(pieces, sign):
    lons, lats = lax.axis_size("lon"), lax.axis_size("lat")
    own, by_lat, by_lon, by_both = pieces

    def move(block, lon_step, lat_step):
        route = []
        for lon in range(lons):
            for lat in range(lats):
                target = ((lon + sign * lon_step) % lons) * lats + (lat + sign * lat_step) % lats
                route.append((lon * lats + lat, target))
        return lax.ppermute(block, AXES, route)

    return [own, move(by_lat, 0, 1), move(by_lon, 1, 0), move(by_both, 1, 1)]


def on_device(fields, upstream, gains, project_in, project_out, earth_bias, row_valid, regions):
    fields = fields.transpose(1, 2, 0, 3)
    upstream = upstream.transpose(1, 2, 0, 3)
    earth_bias = earth_bias.transpose(0, 1, 2, 3, 4, 6, 7, 5, 8)
    constants = run(
        constant_tables,
        [((TABLE_ROWS, STACK), BF), ((OFFSETS, TABLE_LANES), BF), ((TABLE_LANES, 256), BF)],
        [], [], (), cost=4_000_000_000,
    )
    middle, *rest = run(
        plain_forward,
        [(CELLS, BF), PIECE, PIECE, PIECE, PIECE, (CELLS, BF), ((WINDOW, 3 * CHANNELS), BF),
         (SCORES, BF), (CELLS, BF)],
        [whole(), whole(), whole(), picked(WEIGHT, 0), picked(SQUARE, 0), table_spec(0),
         scalars(), scalars()] + [whole()] * 3,
        [CELLS, SPREAD, (4, 72, CHANNELS)],
        (fields, upstream, gains, project_in, project_out, earth_bias, row_valid, regions,
         *constants),
    )
    pieces = exchange(rest[:4], -1)
    saved = rest[4:]
    (bias,) = run(
        shifted_bias,
        [(SPREAD, F32)],
        [table_spec(1), scalars(), scalars()] + [whole()] * 3,
        [],
        (earth_bias, row_valid, regions, *constants),
    )
    *back, hidden, cot, triple, mixture, scores = run(
        shifted_core,
        [PIECE, PIECE, PIECE, PIECE, (CELLS, BF), (CELLS, BF), ((WINDOW, 3 * CHANNELS), BF),
         (CELLS, BF), (SCORES, BF)],
        [whole()] * 5 + [picked(WEIGHT, 1), picked(SQUARE, 1)],
        [CELLS, (4, 72, CHANNELS)],
        (*pieces, bias, project_in, project_out),
    )
    back = exchange(back, 1)
    keep_b, send_b = run(
        shifted_sums,
        [PART, PART],
        [whole()] * 6,
        [PAY, SPREAD],
        (hidden, cot, triple, mixture, scores, constants[2]),
    )
    got_b = swap(send_b, 1)
    keep_a, send_a, grad_middle, grad_hidden = run(
        plain_backward,
        [PART, PART, (CELLS, BF), (CELLS, BF)],
        [whole()] * 8 + [picked(WEIGHT, 0), picked(SQUARE, 0)] + [whole()] * 5,
        [CELLS, PAY, SPREAD],
        (*back, middle, upstream, fields, gains, project_in, project_out, *saved, constants[2]),
    )
    got_a = swap(send_a, 1)
    lons = lax.axis_size("lon")
    own = -(-(GAIN_SPOT + 1) // lons)
    tiles = (own * lons, 8, 128)
    message = (tiles, BF)
    shard = ((own, 8, 128), F32)
    (joined,) = run(
        join_cores, [message], [whole()] * 4, [tiles], (keep_a, got_a, keep_b, got_b)
    )
    (summed,) = run(
        functools.partial(sum_sources, lons), [shard], [whole()], [], (trade(joined),)
    )
    (result,) = run(
        functools.partial(spread_sums, lons), [message], [whole()] * 2, [],
        (summed, swap(summed, 2)),
    )
    mine = trade(result)
    updated, grad_fields = run(
        plain_fields,
        [(NATIVE, BF), (NATIVE, BF)],
        [whole()] * 9,
        [CELLS, NATIVE],
        (*back, middle, fields, gains, grad_middle, grad_hidden),
    )
    grad_in, grad_proj, grad_bias, grad_gains = run(
        finish,
        GRADS + [((2, CHANNELS), F32)],
        [whole()] * 4,
        [(2,) + tiles],
        (mine, swap(mine, 1), constants[0], constants[1]),
        [stepped(WEIGHT), stepped(SQUARE), pl.BlockSpec(
            (None, None, None, HEADS, 2, 6, 6, 2, OFFSETS), lambda i: (i,) + (0,) * 8), whole()],
        2,
    )
    return (
        updated.transpose(2, 0, 1, 3),
        grad_fields.transpose(2, 0, 1, 3),
        grad_gains,
        grad_in,
        grad_proj,
        grad_bias.transpose(0, 1, 2, 3, 4, 7, 5, 6, 8),
    )


def swap(block, bit):
    count = lax.axis_size("lon") * lax.axis_size("lat")
    return lax.ppermute(block, AXES, [(d, d ^ bit) for d in range(count)])


def trade(block):
    return lax.all_to_all(block, "lon", 0, 0, tiled=True)


def solution(mesh):
    spec = P(None, "lat", "lon", None)
    bias_spec = P(None, None, "lat", None, None, None, None, None, None)
    return jax.shard_map(
        on_device,
        mesh=mesh,
        in_specs=(spec, spec, P(), P(), P(), bias_spec, P(), P()),
        out_specs=(spec, spec, P(), P(), P(), bias_spec),
        check_vma=False,
    )
```

```python
import functools

import jax
import jax.numpy as jnp
from jax import lax
from jax.experimental import pallas as pl
from jax.experimental.pallas import tpu as pltpu
from jax.sharding import PartitionSpec as P

CHANNELS = 192
HEADS = 6
HEAD_DIM = 32
WIN_ROWS = 6
WIN_SPAN = 12
WINDOW = 144
STACK = HEADS * WINDOW
GROUPS = 12
OFFSETS = 23
TABLE_LANES = 384
TABLE_ROWS = 72
NORM_EPS = 1e-05
RMS_EPS = 1e-06
SCALE = HEAD_DIM ** (-0.5)
MAIN_HALF = 72
TABLE_HALF = 12
HALF = MAIN_HALF + TABLE_HALF
TABLE_SPOT = 2 * MAIN_HALF
SLOTS = TABLE_SPOT + 4 * TABLE_HALF
FOLD_ROWS = 40
FOLD_LANES = 2 * OFFSETS
NOTE = 120
BF = jnp.bfloat16
F32 = jnp.float32
AXES = ("lon", "lat")


def dot(left, right, left_dim=1, right_dim=0):
    return lax.dot_general(
        left, right, (((left_dim,), (right_dim,)), ((), ())), preferred_element_type=F32
    )


def iota(shape, axis):
    return lax.broadcasted_iota(jnp.int32, shape, axis)


def load_cells(ref, scratch):
    value = ref[...].astype(F32)
    for block in range(GROUPS):
        scratch[block * WIN_SPAN : (block + 1) * WIN_SPAN, :] = value[block % 6, :, block // 6, :]
    return scratch[...]


def store_cells(ref, value, scratch):
    for block in range(GROUPS):
        scratch[block % 6, :, block // 6, :] = value[block * WIN_SPAN : (block + 1) * WIN_SPAN]
    ref[...] = scratch[...].astype(ref.dtype)


def norm_parts(value):
    center = value - jnp.mean(value, axis=1, keepdims=True)
    spread = jnp.mean(center * center, axis=1, keepdims=True)
    inverse = lax.rsqrt(spread + NORM_EPS)
    return center * inverse, inverse


def norm_backward(unit, inverse, gain, cotangent):
    scaled = cotangent * gain
    first = jnp.mean(scaled, axis=1, keepdims=True)
    second = jnp.mean(scaled * unit, axis=1, keepdims=True)
    grad = inverse * (scaled - first - unit * second)
    return grad, jnp.sum(cotangent * unit, axis=0, keepdims=True)


def head_masked(value):
    value = value.astype(F32)
    lane = iota(value.shape, 1)
    parts = [
        jnp.where((lane >= h * HEAD_DIM) & (lane < (h + 1) * HEAD_DIM), value, 0.0).astype(BF)
        for h in range(HEADS)
    ]
    return jnp.concatenate(parts, axis=0)


def head_merge(stacked):
    lane = iota((WINDOW, CHANNELS), 1)
    merged = stacked[:WINDOW]
    for h in range(1, HEADS):
        merged = jnp.where(lane >= h * HEAD_DIM, stacked[h * WINDOW : (h + 1) * WINDOW], merged)
    return merged


def table_spread():
    column = iota((1, 256), 1)
    group = (column * 5462) >> 16
    part = jnp.where(group >= 5, 1, 0) + jnp.where(group >= 10, 1, 0)
    wanted = part * 128 + (group - 5 * part) * OFFSETS + 11 - (column - WIN_SPAN * group)
    wanted = jnp.where(column < WINDOW, wanted, -1)
    return jnp.where(iota((TABLE_LANES, 256), 0) == wanted, 1.0, 0.0).astype(BF)


def group_spots():
    for group in range(GROUPS):
        yield (group % 6) * 2 + group // 6, group // 5, (group % 5) * OFFSETS


def turn(value, lanes):
    return value if lanes % 128 == 0 else pltpu.roll(value, lanes % 128, 1)


def compact_table(flat):
    parts = [jnp.zeros((TABLE_ROWS, 128), F32) for _ in range(3)]
    for row, part, lanes in group_spots():
        parts[part] = parts[part] + turn(flat[pl.ds(row, TABLE_ROWS, stride=GROUPS), :], lanes)
    return parts


def expand_table(parts, flat):
    lane = iota((TABLE_ROWS, 128), 1)
    for row, part, lanes in group_spots():
        value = jnp.where(lane < OFFSETS, turn(parts[part], -lanes), 0.0)
        flat[pl.ds(row, TABLE_ROWS, stride=GROUPS), :] = value


def marks(valid_ref, region_ref, shifted):
    lat = lax.axis_index("lat")
    column = iota((1, WINDOW), 1)
    row = iota((WINDOW, 1), 0)
    key = jnp.zeros((1, WINDOW), jnp.int32)
    label = jnp.zeros((WINDOW, 1), jnp.int32)
    total = valid_ref.shape[0]
    for block in range(GROUPS):
        level, inner = block // 6, block % 6
        source = lat * WIN_ROWS + inner
        own = jnp.int32(0)
        if shifted:
            source = source + WIN_ROWS // 2
            source = jnp.where(source >= total, source - total, source)
            level = (level + 1) % 2
            own = region_ref[level, source] + jnp.where(source < WIN_ROWS // 2, 4, 0)
            own = own + (8 if level < 1 else 0)
        usable = jnp.where(valid_ref[source] > 0, own, -1)
        key = jnp.where(column >= block * WIN_SPAN, usable, key)
        label = jnp.where(row >= block * WIN_SPAN, own, label)
    return label, key


def build_bias(table, valid_ref, region_ref, shifted, bias, flat, spread):
    narrow = table.astype(F32).reshape(STACK, OFFSETS)
    flat[...] = jnp.concatenate([narrow, jnp.zeros((STACK, 128 - OFFSETS), F32)], axis=1)
    parts = compact_table(flat)
    turned = [
        jnp.concatenate([turn(part, -c) for part in parts], axis=1) for c in range(WIN_SPAN)
    ]
    wide = dot(jnp.concatenate(turned, axis=0).astype(BF), spread)
    for c in range(WIN_SPAN):
        part = wide[c * TABLE_ROWS : (c + 1) * TABLE_ROWS]
        for half in range(2):
            bias[half, pl.ds(c, TABLE_ROWS, stride=WIN_SPAN), :] = part[:, half * 128 : (half + 1) * 128]
    label, key = marks(valid_ref, region_ref, shifted)
    allowed = (label == key) | (iota((WINDOW, WINDOW), 0) == iota((WINDOW, WINDOW), 1))
    minus = jnp.where(allowed, 0.0, -jnp.inf)
    for h in range(HEADS):
        rows = slice(h * WINDOW, (h + 1) * WINDOW)
        bias[0, rows, :] = bias[0, rows, :] + minus[:, :128]
        bias[1, rows, : WINDOW - 128] = bias[1, rows, : WINDOW - 128] + minus[:, 128:]


def attend(triple, bias):
    query = head_masked(triple[:, :CHANNELS])
    keys = triple[:, CHANNELS : 2 * CHANNELS]
    values = triple[:, 2 * CHANNELS :]
    bias = jnp.concatenate([bias[0], bias[1, :, : WINDOW - 128]], axis=1)
    scores = dot(query, keys, 1, 1) * SCALE + bias
    raised = jnp.exp(scores - jnp.max(scores, axis=1, keepdims=True))
    weight = raised * (1.0 / jnp.sum(raised, axis=1, keepdims=True))
    attention = weight.astype(BF)
    mixture = head_merge(dot(attention, values)).astype(BF)
    return query, keys, values, weight, attention, mixture


def attend_backward(query, keys, values, weight, attention, grad_mix):
    stacked = head_masked(grad_mix)
    grad_attention = dot(stacked, values, 1, 1).astype(BF).astype(F32)
    product = weight * grad_attention
    grad_scores = product - weight * jnp.sum(product, axis=1, keepdims=True)
    narrow = grad_scores.astype(BF)
    grad_query = head_merge(dot(narrow, keys)) * SCALE
    grad_keys = dot(narrow, query, 0, 0) * SCALE
    grad_values = dot(attention, stacked, 0, 0)
    grad_triple = jnp.concatenate([grad_query, grad_keys, grad_values], axis=1).astype(BF)
    return grad_scores, grad_triple


def store_payload(keep, send, pay, hidden, grad_triple, mixture, grad_out, grad_scores, gather, gains, spread_ref):
    weight = dot(hidden, grad_triple, 0, 0)
    proj = dot(mixture, grad_out, 0, 0)
    main = jnp.concatenate([weight, proj], axis=1)
    for c in range(6):
        start = (c % 3) * 24
        pay[c // 3, start : start + 24] = main[:, c * 128 : (c + 1) * 128].reshape(24, 8, 128)
    gather[0] = grad_scores[:, :128]
    gather[1] = jnp.concatenate(
        [grad_scores[:, 128:], jnp.zeros((STACK, 256 - WINDOW), F32)], axis=1
    )
    halves = [
        jnp.concatenate(
            [gather[half, pl.ds(c, TABLE_ROWS, stride=WIN_SPAN), :] for c in range(WIN_SPAN)], axis=0
        )
        for half in range(2)
    ]
    wide = dot(jnp.concatenate(halves, axis=1).astype(BF), spread_ref[...], 1, 1)
    tiles = []
    for part in range(3):
        total = wide[:TABLE_ROWS, part * 128 : (part + 1) * 128]
        for c in range(1, WIN_SPAN):
            rows = slice(c * TABLE_ROWS, (c + 1) * TABLE_ROWS)
            total = total + turn(wide[rows, part * 128 : (part + 1) * 128], c)
        tiles.append(total)
    tail = jnp.concatenate(
        [turn(tiles[2][FOLD_ROWS:], FOLD_LANES), jnp.zeros((2 * FOLD_ROWS - TABLE_ROWS, 128), F32)],
        axis=0,
    )
    tiles[2] = tiles[2][:FOLD_ROWS] + tail
    tiles = jnp.concatenate(tiles, axis=0).reshape(2 * TABLE_HALF - 1, 8, 128)
    pay[0, MAIN_HALF:] = tiles[:TABLE_HALF]
    pay[1, MAIN_HALF : HALF - 1] = tiles[TABLE_HALF:]
    pay[1, HALF - 1] = gain_tile(gains)
    core = lax.rem(lax.axis_index("lat"), 2)
    keep[...] = pay[core].astype(BF)
    send[...] = pay[1 - core].astype(BF)


def gain_tile(gains):
    rows = []
    for gain in gains:
        rows.append(gain[:, :128])
        rows.append(jnp.concatenate([gain[:, 128:], jnp.zeros((1, 256 - CHANNELS), F32)], axis=1))
    return jnp.concatenate([jnp.zeros((8 - len(rows), 128), F32)] + rows, axis=0)


def join_cores(keep_a, got_a, keep_b, got_b, out, wide):
    core = lax.rem(lax.axis_index("lat"), 2)
    for s, (keep, got) in enumerate(((keep_a, got_a), (keep_b, got_b))):
        mine, theirs = keep[...].astype(F32), got[...].astype(F32)
        wide[s * MAIN_HALF : (s + 1) * MAIN_HALF] = mine[:MAIN_HALF] + theirs[:MAIN_HALF]
        start = TABLE_SPOT + 2 * s * TABLE_HALF
        wide[pl.ds(start + core * TABLE_HALF, TABLE_HALF)] = mine[MAIN_HALF:]
        wide[pl.ds(start + (1 - core) * TABLE_HALF, TABLE_HALF)] = theirs[MAIN_HALF:]
    out[...] = wide[...].astype(BF)


def table_places(own):
    core = lax.rem(lax.axis_index("lat"), 2)
    place = lax.axis_index("lon") * own + iota((own, 1, 1), 0)
    gains = (place == TABLE_SPOT + TABLE_HALF - 1) | (place == TABLE_SPOT + 2 * TABLE_HALF - 1)
    return (place >= TABLE_SPOT) & ~(gains & (core == 1))


def sum_sources(count, parts, out):
    own = out.shape[0]
    sums = jnp.sum(parts[...].astype(F32).reshape(count, own, 8, 128), axis=0)
    squares = jnp.sum(sums * sums, axis=(1, 2), keepdims=True)
    noted = (iota(sums.shape, 1) == 0) & (iota(sums.shape, 2) == NOTE) & table_places(own)
    out[...] = jnp.where(noted, squares, sums)


def spread_sums(count, mine, theirs, out):
    own = mine.shape[0]
    first = iota(mine.shape, 1) == 0
    lane = iota(mine.shape, 2)
    value = mine[...]
    both = value + theirs[...]
    upper = both.astype(BF).astype(F32)
    lower = jnp.sum(jnp.where(first & (lane == NOTE), both - upper, 0.0), axis=(1, 2), keepdims=True)
    noted = jnp.where(first & (lane == NOTE), upper, value)
    noted = jnp.where(first & (lane == NOTE + 1), lower, noted)
    result = jnp.where(table_places(own), noted, both)[None]
    out[...] = jnp.broadcast_to(result, (count,) + mine.shape).reshape(out.shape).astype(BF)


def constant_table(spread):
    spread[...] = table_spread()


def shifted_bias(table, valid, region, spread, bias, flat):
    build_bias(table[...], valid, region, True, bias, flat, spread[...])


def plain_forward(
    fields, upstream, gains, w_in, w_out, table, valid, region, spread,
    middle, own, by_lat, by_lon, by_both, hidden_out, triple_out, attention_out, mixture_out,
    cells, pieces, bias, flat,
):
    build_bias(table[...], valid, region, False, bias, flat, spread[...])
    value = load_cells(fields, cells)
    unit, _ = norm_parts(value)
    hidden = (unit * gains[0:1, :]).astype(BF)
    hidden_out[...] = hidden
    triple = dot(hidden, w_in[...]).astype(BF)
    triple_out[...] = triple
    _, _, _, _, attention, mixture = attend(triple, bias)
    attention_out[...] = attention
    mixture_out[...] = mixture
    added = dot(mixture, w_out[...]).astype(BF).astype(F32)
    result = (value + added).astype(BF)
    middle[...] = result
    unit, _ = norm_parts(result.astype(F32))
    hidden = (unit * gains[1:2, :]).astype(BF).astype(F32)
    raw = load_cells(upstream, cells)
    for index, (ref, row_start, column_start) in enumerate(
        ((own, 3, 6), (by_lat, 0, 6), (by_lon, 3, 0), (by_both, 0, 0))
    ):
        for which, source in enumerate((hidden, raw)):
            for level in range(2):
                for inner in range(3):
                    start = ((1 - level) * 6 + row_start + inner) * WIN_SPAN + column_start
                    place = which * 36 + (level * 3 + inner) * 6
                    pieces[index, place : place + 6, :] = source[start : start + 6]
        ref[...] = pieces[index].astype(BF)


def gather_pieces(pieces, which, cells, forward):
    for index, piece in enumerate(pieces):
        far_row, far_column = index & 1, index >> 1
        if not forward:
            far_row, far_column = index >> 1, (index + 1) >> 1 & 1
        for level in range(2):
            for inner in range(3):
                if forward:
                    row, column, target = 3 * far_row + inner, 6 * far_column, level
                else:
                    row, column, target = 3 - 3 * far_row + inner, 6 - 6 * far_column, 1 - level
                start = (target * 6 + row) * WIN_SPAN + column
                place = which * 36 + (level * 3 + inner) * 6
                cells[start : start + 6, :] = piece[place : place + 6]
    return cells[...]


def shifted_core(
    own, by_lat, by_lon, by_both, bias, w_in, w_out,
    own_out, lon_out, both_out, lat_out, hidden_out, cot_out, triple_out, mixture_out, scores_out,
    cells, pieces_out,
):
    pieces = [ref[...].astype(F32) for ref in (own, by_lat, by_lon, by_both)]
    hidden = gather_pieces(pieces, 0, cells, True).astype(BF)
    grad_out = gather_pieces(pieces, 1, cells, True).astype(BF)
    hidden_out[...] = hidden
    cot_out[...] = grad_out
    triple = dot(hidden, w_in[...]).astype(BF)
    query, keys, values, weight, attention, mixture = attend(triple, bias)
    mixture_out[...] = mixture
    added = dot(mixture, w_out[...]).astype(BF).astype(F32)
    grad_mix = dot(grad_out, w_out[...], 1, 1).astype(BF)
    grad_scores, grad_triple = attend_backward(query, keys, values, weight, attention, grad_mix)
    triple_out[...] = grad_triple
    scores_out[...] = grad_scores.astype(BF)
    grad_hidden = dot(grad_triple, w_in[...], 1, 1).astype(BF).astype(F32)
    for index, ref in enumerate((own_out, lon_out, both_out, lat_out)):
        far_row, far_column = index >> 1, (index + 1) >> 1 & 1
        for which, source in enumerate((added, grad_hidden)):
            for level in range(2):
                for inner in range(3):
                    start = (level * 6 + 3 * far_row + inner) * WIN_SPAN + 6 * far_column
                    place = which * 36 + (level * 3 + inner) * 6
                    pieces_out[index, place : place + 6, :] = source[start : start + 6]
        ref[...] = pieces_out[index].astype(BF)


def shifted_sums(hidden, cot, triple, mixture, scores, spread, keep, send, pay, gather):
    store_payload(
        keep, send, pay, hidden[...], triple[...], mixture[...], cot[...],
        scores[...].astype(F32), gather, (), spread,
    )


def plain_backward(
    own, by_lon, by_both, by_lat, middle, upstream, fields, gains, w_in, w_out,
    hidden_in, triple_in, attention_in, mixture_in, spread,
    keep, send, middle_out, hidden_out,
    cells, pay, gather,
):
    pieces = [ref[...].astype(F32) for ref in (own, by_lon, by_both, by_lat)]
    grad_hidden = gather_pieces(pieces, 1, cells, False)
    unit, inverse = norm_parts(middle[...].astype(F32))
    norm_grad, gain_b = norm_backward(unit, inverse, gains[1:2, :], grad_hidden)
    grad_middle = (load_cells(upstream, cells) + norm_grad).astype(BF)
    middle_out[...] = grad_middle
    grad_mix = dot(grad_middle, w_out[...], 1, 1).astype(BF)
    triple = triple_in[...]
    attention = attention_in[...]
    grad_scores, grad_triple = attend_backward(
        head_masked(triple[:, :CHANNELS]),
        triple[:, CHANNELS : 2 * CHANNELS],
        triple[:, 2 * CHANNELS :],
        attention.astype(F32),
        attention,
        grad_mix,
    )
    grad_hidden = dot(grad_triple, w_in[...], 1, 1).astype(BF)
    hidden_out[...] = grad_hidden
    unit, _ = norm_parts(load_cells(fields, cells))
    gain_a = jnp.sum(grad_hidden.astype(F32) * unit, axis=0, keepdims=True)
    store_payload(
        keep, send, pay, hidden_in[...], grad_triple, mixture_in[...], grad_middle,
        grad_scores, gather, (gain_a, gain_b), spread,
    )


def plain_fields(
    own, by_lon, by_both, by_lat, middle, fields, gains, grad_middle, grad_hidden,
    updated, grad_fields,
    cells, native,
):
    pieces = [ref[...].astype(F32) for ref in (own, by_lon, by_both, by_lat)]
    store_cells(updated, middle[...].astype(F32) + gather_pieces(pieces, 0, cells, False), native)
    unit, inverse = norm_parts(load_cells(fields, cells))
    norm_grad, _ = norm_backward(unit, inverse, gains[0:1, :], grad_hidden[...].astype(F32))
    store_cells(grad_fields, grad_middle[...].astype(F32) + norm_grad, native)


def finish(own, other, grad_in, grad_proj, grad_bias, grad_gains, halves, flat):
    core = lax.rem(lax.axis_index("lat"), 2)
    s = pl.program_id(0)

    @pl.when(s == 0)
    def _():
        halves[core] = own[...].astype(F32)
        halves[1 - core] = other[...].astype(F32)
        gains = halves[1, TABLE_SPOT + TABLE_HALF - 1] + halves[1, TABLE_SPOT + 2 * TABLE_HALF - 1]
        for which in range(2):
            gain = gains[4 + 2 * which : 6 + 2 * which]
            factor = 1.0 / jnp.sqrt(jnp.sum(gain * gain, keepdims=True) / CHANNELS + RMS_EPS)
            grad_gains[which : which + 1, :128] = gain[0:1, :] * factor
            grad_gains[which : which + 1, 128:] = gain[1:2, : CHANNELS - 128] * factor

    main = jnp.concatenate(
        [halves[c // 3, pl.ds(s * MAIN_HALF + (c % 3) * 24, 24)].reshape(CHANNELS, 128)
         for c in range(6)],
        axis=1,
    )
    weight = main[:, : 3 * CHANNELS]
    factor = 1.0 / jnp.sqrt(jnp.sum(weight * weight, keepdims=True) / weight.size + RMS_EPS)
    grad_in[...] = weight * factor
    proj = main[:, 3 * CHANNELS :]
    factor = 1.0 / jnp.sqrt(jnp.sum(proj * proj, keepdims=True) / proj.size + RMS_EPS)
    grad_proj[...] = proj * factor
    start = TABLE_SPOT + 2 * s * TABLE_HALF
    every = halves[:, pl.ds(start, 2 * TABLE_HALF)]
    noted = (iota((8, 128), 0) == 0) & ((iota((8, 128), 1) >> 1) == NOTE // 2)
    squares = jnp.sum(jnp.where(noted, jnp.sum(every, axis=(0, 1)), 0.0), keepdims=True)
    start = start + core * TABLE_HALF
    found = [halves[half, pl.ds(start, TABLE_HALF)] for half in range(2)]
    found = jnp.concatenate([found[0], found[1][: TABLE_HALF - 1]], axis=0)
    factor = 1.0 / jnp.sqrt(squares / (4 * WINDOW * 6 * OFFSETS) + RMS_EPS)
    found = found.reshape(2 * TABLE_ROWS + FOLD_ROWS, 128) * factor
    parts = [found[:TABLE_ROWS], found[TABLE_ROWS : 2 * TABLE_ROWS]]
    tail = found[2 * TABLE_ROWS :]
    parts.append(jnp.concatenate(
        [tail, turn(tail[: TABLE_ROWS - FOLD_ROWS], -FOLD_LANES)], axis=0
    ))
    expand_table(parts, flat)
    grad_bias[...] = flat[:, :OFFSETS].reshape(HEADS, 2, 6, 6, 2, OFFSETS)


def whole():
    return pl.BlockSpec(memory_space=pltpu.VMEM)


def scalars():
    return pl.BlockSpec(memory_space=pltpu.SMEM)


def picked(shape, s):
    return pl.BlockSpec((None,) + shape, lambda i: (s,) + (0,) * len(shape))


def stepped(shape):
    return pl.BlockSpec((None,) + shape, lambda i: (i,) + (0,) * len(shape))


def table_spec(s):
    return pl.BlockSpec(
        (None, None, None, HEADS, 2, 6, 6, 2, OFFSETS), lambda i: (s,) + (0,) * 8
    )


def run(body, outs, in_specs, scratch, args, out_specs=None, steps=1, cost=None):
    return pl.pallas_call(
        body,
        grid=(steps,),
        out_shape=[jax.ShapeDtypeStruct(shape, kind) for shape, kind in outs],
        in_specs=in_specs,
        out_specs=out_specs or [whole() for _ in outs],
        scratch_shapes=[
            pltpu.VMEM(shape, F32) if isinstance(shape, tuple) else shape for shape in scratch
        ],
        cost_estimate=cost and pl.CostEstimate(flops=cost, bytes_accessed=0, transcendentals=0),
        compiler_params=pltpu.CompilerParams(vmem_limit_bytes=40 * 1024 * 1024),
    )(*args)


CELLS = (WINDOW, CHANNELS)
PIECE = ((72, CHANNELS), BF)
NATIVE = (WIN_ROWS, WIN_SPAN, 2, CHANNELS)
WEIGHT = (CHANNELS, 3 * CHANNELS)
SQUARE = (CHANNELS, CHANNELS)
SCORES = (STACK, WINDOW)
SPREAD = (2, STACK, 128)
PAY = (2, HALF, 8, 128)
PART = ((HALF, 8, 128), BF)
GRADS = [((2,) + WEIGHT, F32), ((2,) + SQUARE, F32), ((2, 1, 1, HEADS, 2, 6, 6, 2, OFFSETS), F32)]


def exchange(pieces, sign):
    lons, lats = lax.axis_size("lon"), lax.axis_size("lat")
    own, by_lat, by_lon, by_both = pieces

    def move(block, lon_step, lat_step):
        route = []
        for lon in range(lons):
            for lat in range(lats):
                target = ((lon + sign * lon_step) % lons) * lats + (lat + sign * lat_step) % lats
                route.append((lon * lats + lat, target))
        return lax.ppermute(block, AXES, route)

    if sign > 0:
        own, by_lon, by_both, by_lat = pieces
        return [own, move(by_lon, 1, 0), move(by_both, 1, 1), move(by_lat, 0, 1)]
    return [own, move(by_lat, 0, 1), move(by_lon, 1, 0), move(by_both, 1, 1)]


def on_device(fields, upstream, gains, project_in, project_out, earth_bias, row_valid, regions):
    fields = fields.transpose(1, 2, 0, 3)
    upstream = upstream.transpose(1, 2, 0, 3)
    earth_bias = earth_bias.transpose(0, 1, 2, 3, 4, 6, 7, 5, 8)
    (spread,) = run(
        constant_table, [((TABLE_LANES, 256), BF)], [], [], (), cost=4_000_000_000
    )
    middle, *rest = run(
        plain_forward,
        [(CELLS, BF), PIECE, PIECE, PIECE, PIECE, (CELLS, BF), ((WINDOW, 3 * CHANNELS), BF),
         (SCORES, BF), (CELLS, BF)],
        [whole(), whole(), whole(), picked(WEIGHT, 0), picked(SQUARE, 0), table_spec(0),
         scalars(), scalars(), whole()],
        [CELLS, (4, 72, CHANNELS), SPREAD, (STACK, 128)],
        (fields, upstream, gains, project_in, project_out, earth_bias, row_valid, regions, spread),
    )
    pieces = exchange(rest[:4], -1)
    (bias,) = run(
        shifted_bias,
        [(SPREAD, F32)],
        [table_spec(1), scalars(), scalars(), whole()],
        [(STACK, 128)],
        (earth_bias, row_valid, regions, spread),
    )
    saved = rest[4:]
    *back, hidden, cot, triple, mixture, scores = run(
        shifted_core,
        [PIECE, PIECE, PIECE, PIECE, (CELLS, BF), (CELLS, BF), ((WINDOW, 3 * CHANNELS), BF),
         (CELLS, BF), (SCORES, BF)],
        [whole()] * 5 + [picked(WEIGHT, 1), picked(SQUARE, 1)],
        [CELLS, (4, 72, CHANNELS)],
        (*pieces, bias, project_in, project_out),
    )
    back = exchange(back, 1)
    keep_b, send_b = run(
        shifted_sums,
        [PART, PART],
        [whole()] * 6,
        [PAY, SPREAD],
        (hidden, cot, triple, mixture, scores, spread),
    )
    got_b = swap(send_b, 1)
    keep_a, send_a, grad_middle, grad_hidden = run(
        plain_backward,
        [PART, PART, (CELLS, BF), (CELLS, BF)],
        [whole()] * 8 + [picked(WEIGHT, 0), picked(SQUARE, 0)] + [whole()] * 5,
        [CELLS, PAY, SPREAD],
        (*back, middle, upstream, fields, gains, project_in, project_out, *saved, spread),
    )
    got_a = swap(send_a, 1)
    lons = lax.axis_size("lon")
    own = SLOTS // lons
    tiles = (own * lons, 8, 128)
    message = (tiles, BF)
    shard = ((own, 8, 128), F32)
    (joined,) = run(
        join_cores, [message], [whole()] * 4, [tiles], (keep_a, got_a, keep_b, got_b)
    )
    (summed,) = run(
        functools.partial(sum_sources, lons), [shard], [whole()], [], (trade(joined),)
    )
    (result,) = run(
        functools.partial(spread_sums, lons), [message], [whole()] * 2, [],
        (summed, swap(summed, 2)),
    )
    mine = trade(result)
    updated, grad_fields = run(
        plain_fields,
        [(NATIVE, BF), (NATIVE, BF)],
        [whole()] * 9,
        [CELLS, NATIVE],
        (*back, middle, fields, gains, grad_middle, grad_hidden),
    )
    grad_in, grad_proj, grad_bias, grad_gains = run(
        finish,
        GRADS + [((2, CHANNELS), F32)],
        [whole()] * 2,
        [(2,) + tiles, (STACK, 128)],
        (mine, swap(mine, 1)),
        [stepped(WEIGHT), stepped(SQUARE), pl.BlockSpec(
            (None, None, None, HEADS, 2, 6, 6, 2, OFFSETS), lambda i: (i,) + (0,) * 8), whole()],
        2,
    )
    return (
        updated.transpose(2, 0, 1, 3),
        grad_fields.transpose(2, 0, 1, 3),
        grad_gains,
        grad_in,
        grad_proj,
        grad_bias.transpose(0, 1, 2, 3, 4, 7, 5, 6, 8),
    )


def swap(block, bit):
    count = lax.axis_size("lon") * lax.axis_size("lat")
    return lax.ppermute(block, AXES, [(d, d ^ bit) for d in range(count)])


def trade(block):
    return lax.all_to_all(block, "lon", 0, 0, tiled=True)


def solution(mesh):
    spec = P(None, "lat", "lon", None)
    bias_spec = P(None, None, "lat", None, None, None, None, None, None)
    return jax.shard_map(
        on_device,
        mesh=mesh,
        in_specs=(spec, spec, P(), P(), P(), bias_spec, P(), P()),
        out_specs=(spec, spec, P(), P(), P(), bias_spec),
        check_vma=False,
    )
```

```python
import functools

import jax
import jax.numpy as jnp
from jax import lax
from jax.experimental import pallas as pl
from jax.experimental.pallas import tpu as pltpu
from jax.sharding import PartitionSpec as P

CHANNELS = 192
HEADS = 6
HEAD_DIM = 32
WIN_ROWS = 6
WIN_SPAN = 12
WINDOW = 144
STACK = HEADS * WINDOW
GROUPS = 12
OFFSETS = 23
TABLE_LANES = 384
TABLE_ROWS = 72
NORM_EPS = 1e-05
RMS_EPS = 1e-06
SCALE = HEAD_DIM ** (-0.5)
MAIN_HALF = 72
TABLE_HALF = 12
HALF = MAIN_HALF + TABLE_HALF
TABLE_SPOT = 2 * MAIN_HALF
SLOTS = TABLE_SPOT + 4 * TABLE_HALF
FOLD_ROWS = 40
FOLD_LANES = 2 * OFFSETS
NOTE = 120
BF = jnp.bfloat16
F32 = jnp.float32
AXES = ("lon", "lat")


def dot(left, right, left_dim=1, right_dim=0):
    return lax.dot_general(
        left, right, (((left_dim,), (right_dim,)), ((), ())), preferred_element_type=F32
    )


def iota(shape, axis):
    return lax.broadcasted_iota(jnp.int32, shape, axis)


def load_cells(ref, scratch):
    value = ref[...].astype(F32)
    for block in range(GROUPS):
        scratch[block * WIN_SPAN : (block + 1) * WIN_SPAN, :] = value[block % 6, :, block // 6, :]
    return scratch[...]


def store_cells(ref, value, scratch):
    for block in range(GROUPS):
        scratch[block % 6, :, block // 6, :] = value[block * WIN_SPAN : (block + 1) * WIN_SPAN]
    ref[...] = scratch[...].astype(ref.dtype)


def norm_parts(value):
    center = value - jnp.mean(value, axis=1, keepdims=True)
    spread = jnp.mean(center * center, axis=1, keepdims=True)
    inverse = lax.rsqrt(spread + NORM_EPS)
    return center * inverse, inverse


def norm_backward(unit, inverse, gain, cotangent):
    scaled = cotangent * gain
    first = jnp.mean(scaled, axis=1, keepdims=True)
    second = jnp.mean(scaled * unit, axis=1, keepdims=True)
    grad = inverse * (scaled - first - unit * second)
    return grad, jnp.sum(cotangent * unit, axis=0, keepdims=True)


def head_masked(value):
    value = value.astype(F32)
    lane = iota(value.shape, 1)
    parts = [
        jnp.where((lane >= h * HEAD_DIM) & (lane < (h + 1) * HEAD_DIM), value, 0.0).astype(BF)
        for h in range(HEADS)
    ]
    return jnp.concatenate(parts, axis=0)


def head_merge(stacked):
    lane = iota((WINDOW, CHANNELS), 1)
    merged = stacked[:WINDOW]
    for h in range(1, HEADS):
        merged = jnp.where(lane >= h * HEAD_DIM, stacked[h * WINDOW : (h + 1) * WINDOW], merged)
    return merged


def table_spread():
    column = iota((1, 256), 1)
    group = (column * 5462) >> 16
    part = jnp.where(group >= 5, 1, 0) + jnp.where(group >= 10, 1, 0)
    wanted = part * 128 + (group - 5 * part) * OFFSETS + 11 - (column - WIN_SPAN * group)
    wanted = jnp.where(column < WINDOW, wanted, -1)
    return jnp.where(iota((TABLE_LANES, 256), 0) == wanted, 1.0, 0.0).astype(BF)


def group_spots():
    for group in range(GROUPS):
        yield (group % 6) * 2 + group // 6, group // 5, (group % 5) * OFFSETS


def turn(value, lanes):
    return value if lanes % 128 == 0 else pltpu.roll(value, lanes % 128, 1)


def compact_table(flat):
    parts = [jnp.zeros((TABLE_ROWS, 128), F32) for _ in range(3)]
    for row, part, lanes in group_spots():
        parts[part] = parts[part] + turn(flat[pl.ds(row, TABLE_ROWS, stride=GROUPS), :], lanes)
    return parts


def expand_table(parts, flat):
    lane = iota((TABLE_ROWS, 128), 1)
    for row, part, lanes in group_spots():
        value = jnp.where(lane < OFFSETS, turn(parts[part], -lanes), 0.0)
        flat[pl.ds(row, TABLE_ROWS, stride=GROUPS), :] = value


def marks(valid_ref, region_ref, shifted):
    lat = lax.axis_index("lat")
    column = iota((1, WINDOW), 1)
    row = iota((WINDOW, 1), 0)
    key = jnp.zeros((1, WINDOW), jnp.int32)
    label = jnp.zeros((WINDOW, 1), jnp.int32)
    total = valid_ref.shape[0]
    for block in range(GROUPS):
        level, inner = block // 6, block % 6
        source = lat * WIN_ROWS + inner
        own = jnp.int32(0)
        if shifted:
            source = source + WIN_ROWS // 2
            source = jnp.where(source >= total, source - total, source)
            level = (level + 1) % 2
            own = region_ref[level, source] + jnp.where(source < WIN_ROWS // 2, 4, 0)
            own = own + (8 if level < 1 else 0)
        usable = jnp.where(valid_ref[source] > 0, own, -1)
        key = jnp.where(column >= block * WIN_SPAN, usable, key)
        label = jnp.where(row >= block * WIN_SPAN, own, label)
    return label, key


def build_bias(table, valid_ref, region_ref, shifted, bias, flat, spread):
    narrow = table.astype(F32).reshape(STACK, OFFSETS)
    flat[...] = jnp.concatenate([narrow, jnp.zeros((STACK, 128 - OFFSETS), F32)], axis=1)
    parts = compact_table(flat)
    turned = [
        jnp.concatenate([turn(part, -c) for part in parts], axis=1) for c in range(WIN_SPAN)
    ]
    wide = dot(jnp.concatenate(turned, axis=0).astype(BF), spread)
    for c in range(WIN_SPAN):
        part = wide[c * TABLE_ROWS : (c + 1) * TABLE_ROWS]
        for half in range(2):
            bias[half, pl.ds(c, TABLE_ROWS, stride=WIN_SPAN), :] = part[:, half * 128 : (half + 1) * 128]
    label, key = marks(valid_ref, region_ref, shifted)
    allowed = (label == key) | (iota((WINDOW, WINDOW), 0) == iota((WINDOW, WINDOW), 1))
    minus = jnp.where(allowed, 0.0, -jnp.inf)
    for h in range(HEADS):
        rows = slice(h * WINDOW, (h + 1) * WINDOW)
        bias[0, rows, :] = bias[0, rows, :] + minus[:, :128]
        bias[1, rows, : WINDOW - 128] = bias[1, rows, : WINDOW - 128] + minus[:, 128:]


def split_triple(triple):
    query = head_masked(triple[:, :CHANNELS])
    return query, triple[:, CHANNELS : 2 * CHANNELS], triple[:, 2 * CHANNELS :]


def attend(query, keys, values, bias):
    bias = jnp.concatenate([bias[0], bias[1, :, : WINDOW - 128]], axis=1)
    scores = dot(query, keys, 1, 1) * SCALE + bias
    raised = jnp.exp(scores - jnp.max(scores, axis=1, keepdims=True))
    weight = raised * (1.0 / jnp.sum(raised, axis=1, keepdims=True))
    attention = weight.astype(BF)
    mixture = head_merge(dot(attention, values)).astype(BF)
    return weight, attention, mixture


def attention_gradient(stacked, values):
    return dot(stacked, values, 1, 1).astype(BF).astype(F32)


def score_gradient(weight, grad_attention):
    product = weight * grad_attention
    return product - weight * jnp.sum(product, axis=1, keepdims=True)


def triple_gradient(query, keys, attention, stacked, narrow):
    grad_query = head_merge(dot(narrow, keys)) * SCALE
    grad_keys = dot(narrow, query, 0, 0) * SCALE
    grad_values = dot(attention, stacked, 0, 0)
    return jnp.concatenate([grad_query, grad_keys, grad_values], axis=1).astype(BF)


def store_table(pay, grad_scores, gather, spread_ref):
    gather[0] = grad_scores[:, :128]
    gather[1] = jnp.concatenate(
        [grad_scores[:, 128:], jnp.zeros((STACK, 256 - WINDOW), F32)], axis=1
    )
    halves = [
        jnp.concatenate(
            [gather[half, pl.ds(c, TABLE_ROWS, stride=WIN_SPAN), :] for c in range(WIN_SPAN)], axis=0
        )
        for half in range(2)
    ]
    wide = dot(jnp.concatenate(halves, axis=1).astype(BF), spread_ref[...], 1, 1)
    tiles = []
    for part in range(3):
        total = wide[:TABLE_ROWS, part * 128 : (part + 1) * 128]
        for c in range(1, WIN_SPAN):
            rows = slice(c * TABLE_ROWS, (c + 1) * TABLE_ROWS)
            total = total + turn(wide[rows, part * 128 : (part + 1) * 128], c)
        tiles.append(total)
    tail = jnp.concatenate(
        [turn(tiles[2][FOLD_ROWS:], FOLD_LANES), jnp.zeros((2 * FOLD_ROWS - TABLE_ROWS, 128), F32)],
        axis=0,
    )
    tiles[2] = tiles[2][:FOLD_ROWS] + tail
    tiles = jnp.concatenate(tiles, axis=0).reshape(2 * TABLE_HALF - 1, 8, 128)
    pay[0, MAIN_HALF:] = tiles[:TABLE_HALF]
    pay[1, MAIN_HALF : HALF - 1] = tiles[TABLE_HALF:]


def store_main(pay, weight, proj):
    whole_columns = jnp.concatenate([weight, proj], axis=1)
    for c in range(6):
        start = (c % 3) * 24
        pay[c // 3, start : start + 24] = whole_columns[:, c * 128 : (c + 1) * 128].reshape(24, 8, 128)


def send_payload(keep, send, pay, gains):
    pay[1, HALF - 1] = gain_tile(gains)
    core = lax.rem(lax.axis_index("lat"), 2)
    keep[...] = pay[core].astype(BF)
    send[...] = pay[1 - core].astype(BF)


def gain_tile(gains):
    rows = []
    for gain in gains:
        rows.append(gain[:, :128])
        rows.append(jnp.concatenate([gain[:, 128:], jnp.zeros((1, 256 - CHANNELS), F32)], axis=1))
    return jnp.concatenate([jnp.zeros((8 - len(rows), 128), F32)] + rows, axis=0)


def join_cores(keep_a, got_a, keep_b, got_b, out, wide):
    core = lax.rem(lax.axis_index("lat"), 2)
    for s, (keep, got) in enumerate(((keep_a, got_a), (keep_b, got_b))):
        mine, theirs = keep[...].astype(F32), got[...].astype(F32)
        wide[s * MAIN_HALF : (s + 1) * MAIN_HALF] = mine[:MAIN_HALF] + theirs[:MAIN_HALF]
        start = TABLE_SPOT + 2 * s * TABLE_HALF
        wide[pl.ds(start + core * TABLE_HALF, TABLE_HALF)] = mine[MAIN_HALF:]
        wide[pl.ds(start + (1 - core) * TABLE_HALF, TABLE_HALF)] = theirs[MAIN_HALF:]
    out[...] = wide[...].astype(BF)


def table_places(own):
    core = lax.rem(lax.axis_index("lat"), 2)
    place = lax.axis_index("lon") * own + iota((own, 1, 1), 0)
    gains = (place == TABLE_SPOT + TABLE_HALF - 1) | (place == TABLE_SPOT + 2 * TABLE_HALF - 1)
    return (place >= TABLE_SPOT) & ~(gains & (core == 1))


def sum_sources(count, parts, out):
    own = out.shape[0]
    sums = jnp.sum(parts[...].astype(F32).reshape(count, own, 8, 128), axis=0)
    squares = jnp.sum(sums * sums, axis=(1, 2), keepdims=True)
    noted = (iota(sums.shape, 1) == 0) & (iota(sums.shape, 2) == NOTE) & table_places(own)
    out[...] = jnp.where(noted, squares, sums)


def spread_sums(count, mine, theirs, out):
    own = mine.shape[0]
    first = iota(mine.shape, 1) == 0
    lane = iota(mine.shape, 2)
    value = mine[...]
    both = value + theirs[...]
    upper = both.astype(BF).astype(F32)
    lower = jnp.sum(jnp.where(first & (lane == NOTE), both - upper, 0.0), axis=(1, 2), keepdims=True)
    noted = jnp.where(first & (lane == NOTE), upper, value)
    noted = jnp.where(first & (lane == NOTE + 1), lower, noted)
    result = jnp.where(table_places(own), noted, both)[None]
    out[...] = jnp.broadcast_to(result, (count,) + mine.shape).reshape(out.shape).astype(BF)


def constant_table(spread):
    spread[...] = table_spread()


def shifted_bias(table, valid, region, spread, bias, flat):
    build_bias(table[1, 0, 0], valid, region, True, bias, flat, spread[...])


def plain_forward(
    fields, upstream, gains, w_in, w_out, table, valid, region, spread,
    middle, own, by_lat, by_lon, by_both, hidden_out, triple_out, attention_out, mixture_out,
    cells, pieces, bias, flat,
):
    value = load_cells(fields, cells)
    unit, _ = norm_parts(value)
    hidden = (unit * gains[0:1, :]).astype(BF)
    hidden_out[...] = hidden
    triple = dot(hidden, w_in[0]).astype(BF)
    triple_out[...] = triple
    build_bias(table[0, 0, 0], valid, region, False, bias, flat, spread[...])
    _, attention, mixture = attend(*split_triple(triple), bias)
    attention_out[...] = attention
    mixture_out[...] = mixture
    added = dot(mixture, w_out[0]).astype(BF).astype(F32)
    result = (value + added).astype(BF)
    middle[...] = result
    unit, _ = norm_parts(result.astype(F32))
    hidden = (unit * gains[1:2, :]).astype(BF).astype(F32)
    raw = load_cells(upstream, cells)
    for index, (ref, row_start, column_start) in enumerate(
        ((own, 3, 0), (by_lat, 0, 0), (by_lon, 3, 6), (by_both, 0, 6))
    ):
        for which, source in enumerate((hidden, raw)):
            for level in range(2):
                for inner in range(3):
                    start = ((1 - level) * 6 + row_start + inner) * WIN_SPAN + column_start
                    place = which * 36 + (level * 3 + inner) * 6
                    pieces[index, place : place + 6, :] = source[start : start + 6]
        ref[...] = pieces[index].astype(BF)


def gather_pieces(pieces, which, cells, forward):
    for index, piece in enumerate(pieces):
        far_row, far_column = index & 1, index >> 1
        if not forward:
            far_row, far_column = index >> 1, (index + 1) >> 1 & 1
        for level in range(2):
            for inner in range(3):
                if forward:
                    row, column, target = 3 * far_row + inner, 6 - 6 * far_column, level
                else:
                    row, column, target = 3 - 3 * far_row + inner, 6 * far_column, 1 - level
                start = (target * 6 + row) * WIN_SPAN + column
                place = which * 36 + (level * 3 + inner) * 6
                cells[start : start + 6, :] = piece[place : place + 6]
    return cells[...]


def shifted_core(
    own, by_lat, by_lon, by_both, bias, w_in, w_out,
    own_out, lon_out, both_out, lat_out, hidden_out, cot_out, triple_out, mixture_out, scores_out,
    cells, pieces_out,
):
    pieces = [ref[...].astype(F32) for ref in (own, by_lat, by_lon, by_both)]
    hidden = gather_pieces(pieces, 0, cells, True).astype(BF)
    grad_out = gather_pieces(pieces, 1, cells, True).astype(BF)
    hidden_out[...] = hidden
    cot_out[...] = grad_out
    triple = dot(hidden, w_in[1]).astype(BF)
    stacked = head_masked(dot(grad_out, w_out[1], 1, 1).astype(BF))
    query, keys, values = split_triple(triple)
    grad_attention = attention_gradient(stacked, values)
    weight, attention, mixture = attend(query, keys, values, bias)
    narrow = score_gradient(weight, grad_attention).astype(BF)
    grad_triple = triple_gradient(query, keys, attention, stacked, narrow)
    grad_hidden = dot(grad_triple, w_in[1], 1, 1).astype(BF).astype(F32)
    added = dot(mixture, w_out[1]).astype(BF).astype(F32)
    mixture_out[...] = mixture
    triple_out[...] = grad_triple
    scores_out[...] = narrow
    for index, ref in enumerate((own_out, lon_out, both_out, lat_out)):
        far_row, far_column = index >> 1, (index + 1) >> 1 & 1
        for which, source in enumerate((added, grad_hidden)):
            for level in range(2):
                for inner in range(3):
                    start = (level * 6 + 3 * far_row + inner) * WIN_SPAN + 6 - 6 * far_column
                    place = which * 36 + (level * 3 + inner) * 6
                    pieces_out[index, place : place + 6, :] = source[start : start + 6]
        ref[...] = pieces_out[index].astype(BF)


def shifted_sums(hidden, cot, triple, mixture, scores, spread, keep, send, pay, gather):
    store_table(pay, scores[...].astype(F32), gather, spread)
    store_main(pay, dot(hidden[...], triple[...], 0, 0), dot(mixture[...], cot[...], 0, 0))
    send_payload(keep, send, pay, ())


def plain_backward(
    own, by_lon, by_both, by_lat, middle, upstream, fields, gains, w_in, w_out,
    hidden_in, triple_in, attention_in, mixture_in, spread,
    keep, send, middle_out, hidden_out,
    cells, pay, gather,
):
    pieces = [ref[...].astype(F32) for ref in (own, by_lon, by_both, by_lat)]
    grad_hidden = gather_pieces(pieces, 1, cells, False)
    unit, inverse = norm_parts(middle[...].astype(F32))
    norm_grad, gain_b = norm_backward(unit, inverse, gains[1:2, :], grad_hidden)
    grad_middle = (load_cells(upstream, cells) + norm_grad).astype(BF)
    middle_out[...] = grad_middle
    stacked = head_masked(dot(grad_middle, w_out[0], 1, 1).astype(BF))
    proj = dot(mixture_in[...], grad_middle, 0, 0)
    query, keys, values = split_triple(triple_in[...])
    attention = attention_in[...]
    grad_scores = score_gradient(attention.astype(F32), attention_gradient(stacked, values))
    grad_triple = triple_gradient(query, keys, attention, stacked, grad_scores.astype(BF))
    grad_hidden = dot(grad_triple, w_in[0], 1, 1).astype(BF)
    weight = dot(hidden_in[...], grad_triple, 0, 0)
    store_table(pay, grad_scores, gather, spread)
    store_main(pay, weight, proj)
    hidden_out[...] = grad_hidden
    unit, _ = norm_parts(load_cells(fields, cells))
    gain_a = jnp.sum(grad_hidden.astype(F32) * unit, axis=0, keepdims=True)
    send_payload(keep, send, pay, (gain_a, gain_b))


def plain_fields(
    own, by_lon, by_both, by_lat, middle, fields, gains, grad_middle, grad_hidden,
    updated, grad_fields,
    cells, native,
):
    pieces = [ref[...].astype(F32) for ref in (own, by_lon, by_both, by_lat)]
    store_cells(updated, middle[...].astype(F32) + gather_pieces(pieces, 0, cells, False), native)
    unit, inverse = norm_parts(load_cells(fields, cells))
    norm_grad, _ = norm_backward(unit, inverse, gains[0:1, :], grad_hidden[...].astype(F32))
    store_cells(grad_fields, grad_middle[...].astype(F32) + norm_grad, native)


def finish(own, other, grad_in, grad_proj, grad_bias, grad_gains, halves, flat):
    core = lax.rem(lax.axis_index("lat"), 2)
    s = pl.program_id(0)

    @pl.when(s == 0)
    def _():
        halves[core] = own[...].astype(F32)
        halves[1 - core] = other[...].astype(F32)
        gains = halves[1, TABLE_SPOT + TABLE_HALF - 1] + halves[1, TABLE_SPOT + 2 * TABLE_HALF - 1]
        for which in range(2):
            gain = gains[4 + 2 * which : 6 + 2 * which]
            factor = 1.0 / jnp.sqrt(jnp.sum(gain * gain, keepdims=True) / CHANNELS + RMS_EPS)
            grad_gains[which : which + 1, :128] = gain[0:1, :] * factor
            grad_gains[which : which + 1, 128:] = gain[1:2, : CHANNELS - 128] * factor

    main = jnp.concatenate(
        [halves[c // 3, pl.ds(s * MAIN_HALF + (c % 3) * 24, 24)].reshape(CHANNELS, 128)
         for c in range(6)],
        axis=1,
    )
    weight = main[:, : 3 * CHANNELS]
    factor = 1.0 / jnp.sqrt(jnp.sum(weight * weight, keepdims=True) / weight.size + RMS_EPS)
    grad_in[...] = weight * factor
    proj = main[:, 3 * CHANNELS :]
    factor = 1.0 / jnp.sqrt(jnp.sum(proj * proj, keepdims=True) / proj.size + RMS_EPS)
    grad_proj[...] = proj * factor
    start = TABLE_SPOT + 2 * s * TABLE_HALF
    every = halves[:, pl.ds(start, 2 * TABLE_HALF)]
    noted = (iota((8, 128), 0) == 0) & ((iota((8, 128), 1) >> 1) == NOTE // 2)
    squares = jnp.sum(jnp.where(noted, jnp.sum(every, axis=(0, 1)), 0.0), keepdims=True)
    start = start + core * TABLE_HALF
    found = [halves[half, pl.ds(start, TABLE_HALF)] for half in range(2)]
    found = jnp.concatenate([found[0], found[1][: TABLE_HALF - 1]], axis=0)
    factor = 1.0 / jnp.sqrt(squares / (4 * WINDOW * 6 * OFFSETS) + RMS_EPS)
    found = found.reshape(2 * TABLE_ROWS + FOLD_ROWS, 128) * factor
    parts = [found[:TABLE_ROWS], found[TABLE_ROWS : 2 * TABLE_ROWS]]
    tail = found[2 * TABLE_ROWS :]
    parts.append(jnp.concatenate(
        [tail, turn(tail[: TABLE_ROWS - FOLD_ROWS], -FOLD_LANES)], axis=0
    ))
    expand_table(parts, flat)
    grad_bias[...] = flat[:, :OFFSETS].reshape(HEADS, 2, 6, 6, 2, OFFSETS)


def whole():
    return pl.BlockSpec(memory_space=pltpu.VMEM)


def scalars():
    return pl.BlockSpec(memory_space=pltpu.SMEM)


def stepped(shape):
    return pl.BlockSpec((None,) + shape, lambda i: (i,) + (0,) * len(shape))


def run(body, outs, in_specs, scratch, args, out_specs=None, steps=1, cost=None):
    return pl.pallas_call(
        body,
        grid=(steps,),
        out_shape=[jax.ShapeDtypeStruct(shape, kind) for shape, kind in outs],
        in_specs=in_specs,
        out_specs=out_specs or [whole() for _ in outs],
        scratch_shapes=[
            pltpu.VMEM(shape, F32) if isinstance(shape, tuple) else shape for shape in scratch
        ],
        cost_estimate=cost and pl.CostEstimate(flops=cost, bytes_accessed=0, transcendentals=0),
        compiler_params=pltpu.CompilerParams(vmem_limit_bytes=40 * 1024 * 1024),
    )(*args)


CELLS = (WINDOW, CHANNELS)
PIECE = ((72, CHANNELS), BF)
NATIVE = (WIN_ROWS, WIN_SPAN, 2, CHANNELS)
WEIGHT = (CHANNELS, 3 * CHANNELS)
SQUARE = (CHANNELS, CHANNELS)
SCORES = (STACK, WINDOW)
SPREAD = (2, STACK, 128)
PAY = (2, HALF, 8, 128)
PART = ((HALF, 8, 128), BF)
GRADS = [((2,) + WEIGHT, F32), ((2,) + SQUARE, F32), ((2, 1, 1, HEADS, 2, 6, 6, 2, OFFSETS), F32)]


def exchange(pieces, sign):
    lons, lats = lax.axis_size("lon"), lax.axis_size("lat")
    own, by_lat, by_lon, by_both = pieces

    def move(block, lon_step, lat_step):
        route = []
        for lon in range(lons):
            for lat in range(lats):
                target = ((lon - sign * lon_step) % lons) * lats + (lat + sign * lat_step) % lats
                route.append((lon * lats + lat, target))
        return lax.ppermute(block, AXES, route)

    if sign > 0:
        own, by_lon, by_both, by_lat = pieces
        return [own, move(by_lon, 1, 0), move(by_both, 1, 1), move(by_lat, 0, 1)]
    return [own, move(by_lat, 0, 1), move(by_lon, 1, 0), move(by_both, 1, 1)]


def on_device(fields, upstream, gains, project_in, project_out, earth_bias, row_valid, regions):
    fields = fields.transpose(1, 2, 0, 3)
    upstream = upstream.transpose(1, 2, 0, 3)
    earth_bias = earth_bias.transpose(0, 1, 2, 3, 4, 6, 7, 5, 8)
    (spread,) = run(
        constant_table, [((TABLE_LANES, 256), BF)], [], [], (), cost=4_000_000_000
    )
    middle, *rest = run(
        plain_forward,
        [(CELLS, BF), PIECE, PIECE, PIECE, PIECE, (CELLS, BF), ((WINDOW, 3 * CHANNELS), BF),
         (SCORES, BF), (CELLS, BF)],
        [whole()] * 6 + [scalars(), scalars(), whole()],
        [CELLS, (4, 72, CHANNELS), SPREAD, (STACK, 128)],
        (fields, upstream, gains, project_in, project_out, earth_bias, row_valid, regions, spread),
    )
    pieces = exchange(rest[:4], -1)
    (bias,) = run(
        shifted_bias,
        [(SPREAD, F32)],
        [whole(), scalars(), scalars(), whole()],
        [(STACK, 128)],
        (earth_bias, row_valid, regions, spread),
    )
    saved = rest[4:]
    *back, hidden, cot, triple, mixture, scores = run(
        shifted_core,
        [PIECE, PIECE, PIECE, PIECE, (CELLS, BF), (CELLS, BF), ((WINDOW, 3 * CHANNELS), BF),
         (CELLS, BF), (SCORES, BF)],
        [whole()] * 7,
        [CELLS, (4, 72, CHANNELS)],
        (*pieces, bias, project_in, project_out),
    )
    back = exchange(back, 1)
    keep_b, send_b = run(
        shifted_sums,
        [PART, PART],
        [whole()] * 6,
        [PAY, SPREAD],
        (hidden, cot, triple, mixture, scores, spread),
    )
    got_b = swap(send_b, 1)
    keep_a, send_a, grad_middle, grad_hidden = run(
        plain_backward,
        [PART, PART, (CELLS, BF), (CELLS, BF)],
        [whole()] * 15,
        [CELLS, PAY, SPREAD],
        (*back, middle, upstream, fields, gains, project_in, project_out, *saved, spread),
    )
    got_a = swap(send_a, 1)
    lons = lax.axis_size("lon")
    own = SLOTS // lons
    tiles = (own * lons, 8, 128)
    message = (tiles, BF)
    shard = ((own, 8, 128), F32)
    (joined,) = run(
        join_cores, [message], [whole()] * 4, [tiles], (keep_a, got_a, keep_b, got_b)
    )
    (summed,) = run(
        functools.partial(sum_sources, lons), [shard], [whole()], [], (trade(joined),)
    )
    (result,) = run(
        functools.partial(spread_sums, lons), [message], [whole()] * 2, [],
        (summed, swap(summed, 2)),
    )
    mine = trade(result)
    updated, grad_fields = run(
        plain_fields,
        [(NATIVE, BF), (NATIVE, BF)],
        [whole()] * 9,
        [CELLS, NATIVE],
        (*back, middle, fields, gains, grad_middle, grad_hidden),
    )
    grad_in, grad_proj, grad_bias, grad_gains = run(
        finish,
        GRADS + [((2, CHANNELS), F32)],
        [whole()] * 2,
        [(2,) + tiles, (STACK, 128)],
        (mine, swap(mine, 1)),
        [stepped(WEIGHT), stepped(SQUARE), pl.BlockSpec(
            (None, None, None, HEADS, 2, 6, 6, 2, OFFSETS), lambda i: (i,) + (0,) * 8), whole()],
        2,
    )
    return (
        updated.transpose(2, 0, 1, 3),
        grad_fields.transpose(2, 0, 1, 3),
        grad_gains,
        grad_in,
        grad_proj,
        grad_bias.transpose(0, 1, 2, 3, 4, 7, 5, 6, 8),
    )


def swap(block, bit):
    count = lax.axis_size("lon") * lax.axis_size("lat")
    return lax.ppermute(block, AXES, [(d, d ^ bit) for d in range(count)])


def trade(block):
    return lax.all_to_all(block, "lon", 0, 0, tiled=True)


def solution(mesh):
    spec = P(None, "lat", "lon", None)
    bias_spec = P(None, None, "lat", None, None, None, None, None, None)
    return jax.shard_map(
        on_device,
        mesh=mesh,
        in_specs=(spec, spec, P(), P(), P(), bias_spec, P(), P()),
        out_specs=(spec, spec, P(), P(), P(), bias_spec),
        check_vma=False,
    )
```

```python
import functools

import jax
import jax.numpy as jnp
from jax import lax
from jax.experimental import pallas as pl
from jax.experimental.pallas import tpu as pltpu
from jax.sharding import PartitionSpec as P

CHANNELS = 192
HEADS = 6
HEAD_DIM = 32
WIN_ROWS = 6
WIN_SPAN = 12
WINDOW = 144
STACK = HEADS * WINDOW
GROUPS = 12
OFFSETS = 23
TABLE_LANES = 384
TABLE_ROWS = 72
NORM_EPS = 1e-05
RMS_EPS = 1e-06
SCALE = HEAD_DIM ** (-0.5)
MAIN_HALF = 72
TABLE_HALF = 12
HALF = MAIN_HALF + TABLE_HALF
TABLE_SPOT = 2 * MAIN_HALF
SLOTS = TABLE_SPOT + 4 * TABLE_HALF
FOLD_ROWS = 40
FOLD_LANES = 2 * OFFSETS
NOTE = 120
BF = jnp.bfloat16
F32 = jnp.float32
AXES = ("lon", "lat")
FIRST = ((0, 0), (1, 0), (1, 1), (0, 1))
SECOND = ((0, 0), (0, 1), (1, 1), (1, 0))


def dot(left, right, left_dim=1, right_dim=0):
    return lax.dot_general(
        left, right, (((left_dim,), (right_dim,)), ((), ())), preferred_element_type=F32
    )


def iota(shape, axis):
    return lax.broadcasted_iota(jnp.int32, shape, axis)


def load_cells(ref, scratch):
    value = ref[...].astype(F32)
    for block in range(GROUPS):
        scratch[block * WIN_SPAN : (block + 1) * WIN_SPAN, :] = value[block % 6, :, block // 6, :]
    return scratch[...]


def store_cells(ref, value, scratch):
    for block in range(GROUPS):
        scratch[block % 6, :, block // 6, :] = value[block * WIN_SPAN : (block + 1) * WIN_SPAN]
    ref[...] = scratch[...].astype(ref.dtype)


def norm_parts(value):
    center = value - jnp.mean(value, axis=1, keepdims=True)
    spread = jnp.mean(center * center, axis=1, keepdims=True)
    inverse = lax.rsqrt(spread + NORM_EPS)
    return center * inverse, inverse


def norm_backward(unit, inverse, gain, cotangent):
    scaled = cotangent * gain
    first = jnp.mean(scaled, axis=1, keepdims=True)
    second = jnp.mean(scaled * unit, axis=1, keepdims=True)
    grad = inverse * (scaled - first - unit * second)
    return grad, jnp.sum(cotangent * unit, axis=0, keepdims=True)


def head_masked(value):
    value = value.astype(F32)
    lane = iota(value.shape, 1)
    parts = [
        jnp.where((lane >= h * HEAD_DIM) & (lane < (h + 1) * HEAD_DIM), value, 0.0).astype(BF)
        for h in range(HEADS)
    ]
    return jnp.concatenate(parts, axis=0)


def head_merge(stacked):
    lane = iota((WINDOW, CHANNELS), 1)
    merged = stacked[:WINDOW]
    for h in range(1, HEADS):
        merged = jnp.where(lane >= h * HEAD_DIM, stacked[h * WINDOW : (h + 1) * WINDOW], merged)
    return merged


def table_spread():
    column = iota((1, 256), 1)
    group = (column * 5462) >> 16
    part = jnp.where(group >= 5, 1, 0) + jnp.where(group >= 10, 1, 0)
    wanted = part * 128 + (group - 5 * part) * OFFSETS + 11 - (column - WIN_SPAN * group)
    wanted = jnp.where(column < WINDOW, wanted, -1)
    return jnp.where(iota((TABLE_LANES, 256), 0) == wanted, 1.0, 0.0).astype(BF)


def group_spots():
    for group in range(GROUPS):
        yield (group % 6) * 2 + group // 6, group // 5, (group % 5) * OFFSETS


def turn(value, lanes):
    return value if lanes % 128 == 0 else pltpu.roll(value, lanes % 128, 1)


def compact_table(flat):
    parts = [jnp.zeros((TABLE_ROWS, 128), F32) for _ in range(3)]
    for row, part, lanes in group_spots():
        parts[part] = parts[part] + turn(flat[pl.ds(row, TABLE_ROWS, stride=GROUPS), :], lanes)
    return parts


def expand_table(parts, flat):
    lane = iota((TABLE_ROWS, 128), 1)
    for row, part, lanes in group_spots():
        value = jnp.where(lane < OFFSETS, turn(parts[part], -lanes), 0.0)
        flat[pl.ds(row, TABLE_ROWS, stride=GROUPS), :] = value


def cell_places(shape, axis, total, shifted):
    cell = iota(shape, axis)
    block = (cell * 5462) >> 16
    level = jnp.where(block >= 6, 1, 0)
    source = lax.axis_index("lat") * WIN_ROWS + block - 6 * level
    if shifted:
        source = source + WIN_ROWS // 2
        source = jnp.where(source >= total, source - total, source)
        level = 1 - level
    return level, source


def cell_labels(picked, level, source, axis):
    one, two = lax.slice_in_dim(picked, 0, 1, axis=axis), lax.slice_in_dim(picked, 1, 2, axis=axis)
    own = jnp.where(level == 0, one, two) + jnp.where(source < WIN_ROWS // 2, 4.0, 0.0)
    return own + jnp.where(level < 1, 8.0, 0.0)


def marks(valid, regions, shifted):
    total = valid.shape[1]
    level, source = cell_places((1, WINDOW), 1, total, shifted)
    pick = jnp.where(iota((total, WINDOW), 0) == source, 1.0, 0.0).astype(BF)
    usable = dot(valid.astype(F32).astype(BF), pick)
    if not shifted:
        return 0.0, jnp.where(usable > 0.5, 0.0, -1.0)
    regions = regions.astype(F32).astype(BF)
    key = jnp.where(usable > 0.5, cell_labels(dot(regions, pick), level, source, 0), -1.0)
    level, source = cell_places((WINDOW, 1), 0, total, shifted)
    pick = jnp.where(iota((WINDOW, total), 1) == source, 1.0, 0.0).astype(BF)
    return cell_labels(dot(pick, regions, 1, 1), level, source, 1), key


def build_bias(table, valid_ref, region_ref, shifted, bias, flat, spread):
    narrow = table.astype(F32).reshape(STACK, OFFSETS)
    flat[...] = jnp.concatenate([narrow, jnp.zeros((STACK, 128 - OFFSETS), F32)], axis=1)
    parts = compact_table(flat)
    turned = [
        jnp.concatenate([turn(part, -c) for part in parts], axis=1) for c in range(WIN_SPAN)
    ]
    wide = dot(jnp.concatenate(turned, axis=0).astype(BF), spread)
    for c in range(WIN_SPAN):
        part = wide[c * TABLE_ROWS : (c + 1) * TABLE_ROWS]
        for half in range(2):
            bias[half, pl.ds(c, TABLE_ROWS, stride=WIN_SPAN), :] = part[:, half * 128 : (half + 1) * 128]
    label, key = marks(valid_ref[...][None, :], region_ref[...], shifted)
    allowed = (label == key) | (iota((WINDOW, WINDOW), 0) == iota((WINDOW, WINDOW), 1))
    minus = jnp.where(allowed, 0.0, -jnp.inf)
    for h in range(HEADS):
        rows = slice(h * WINDOW, (h + 1) * WINDOW)
        bias[0, rows, :] = bias[0, rows, :] + minus[:, :128]
        bias[1, rows, : WINDOW - 128] = bias[1, rows, : WINDOW - 128] + minus[:, 128:]


def split_triple(triple):
    query = head_masked(triple[:, :CHANNELS])
    return query, triple[:, CHANNELS : 2 * CHANNELS], triple[:, 2 * CHANNELS :]


def attend(query, keys, values, bias):
    bias = jnp.concatenate([bias[0], bias[1, :, : WINDOW - 128]], axis=1)
    scores = dot(query, keys, 1, 1) * SCALE + bias
    raised = jnp.exp(scores - jnp.max(scores, axis=1, keepdims=True))
    weight = raised * (1.0 / jnp.sum(raised, axis=1, keepdims=True))
    attention = weight.astype(BF)
    mixture = head_merge(dot(attention, values)).astype(BF)
    return weight, attention, mixture


def attention_gradient(stacked, values):
    return dot(stacked, values, 1, 1).astype(BF).astype(F32)


def score_gradient(weight, grad_attention):
    product = weight * grad_attention
    return product - weight * jnp.sum(product, axis=1, keepdims=True)


def triple_gradient(query, keys, attention, stacked, narrow):
    grad_query = head_merge(dot(narrow, keys)) * SCALE
    grad_keys = dot(narrow, query, 0, 0) * SCALE
    grad_values = dot(attention, stacked, 0, 0)
    return jnp.concatenate([grad_query, grad_keys, grad_values], axis=1).astype(BF)


def store_table(pay, grad_scores, gather, spread_ref):
    gather[0] = grad_scores[:, :128]
    gather[1] = jnp.concatenate(
        [grad_scores[:, 128:], jnp.zeros((STACK, 256 - WINDOW), F32)], axis=1
    )
    halves = [
        jnp.concatenate(
            [gather[half, pl.ds(c, TABLE_ROWS, stride=WIN_SPAN), :] for c in range(WIN_SPAN)], axis=0
        )
        for half in range(2)
    ]
    wide = dot(jnp.concatenate(halves, axis=1).astype(BF), spread_ref[...], 1, 1)
    tiles = []
    for part in range(3):
        total = wide[:TABLE_ROWS, part * 128 : (part + 1) * 128]
        for c in range(1, WIN_SPAN):
            rows = slice(c * TABLE_ROWS, (c + 1) * TABLE_ROWS)
            total = total + turn(wide[rows, part * 128 : (part + 1) * 128], c)
        tiles.append(total)
    tail = jnp.concatenate(
        [turn(tiles[2][FOLD_ROWS:], FOLD_LANES), jnp.zeros((2 * FOLD_ROWS - TABLE_ROWS, 128), F32)],
        axis=0,
    )
    tiles[2] = tiles[2][:FOLD_ROWS] + tail
    tiles = jnp.concatenate(tiles, axis=0).reshape(2 * TABLE_HALF - 1, 8, 128)
    pay[0, MAIN_HALF:] = tiles[:TABLE_HALF]
    pay[1, MAIN_HALF : HALF - 1] = tiles[TABLE_HALF:]


def store_main(pay, weight, proj):
    whole_columns = jnp.concatenate([weight, proj], axis=1)
    for c in range(6):
        start = (c % 3) * 24
        pay[c // 3, start : start + 24] = whole_columns[:, c * 128 : (c + 1) * 128].reshape(24, 8, 128)


def send_payload(keep, send, pay, gains):
    pay[1, HALF - 1] = gain_tile(gains)
    core = lax.rem(lax.axis_index("lat"), 2)
    keep[...] = pay[core].astype(BF)
    send[...] = pay[1 - core].astype(BF)


def gain_tile(gains):
    rows = []
    for gain in gains:
        rows.append(gain[:, :128])
        rows.append(jnp.concatenate([gain[:, 128:], jnp.zeros((1, 256 - CHANNELS), F32)], axis=1))
    return jnp.concatenate([jnp.zeros((8 - len(rows), 128), F32)] + rows, axis=0)


def join_cores(keep_a, got_a, keep_b, got_b, out, wide):
    core = lax.rem(lax.axis_index("lat"), 2)
    for s, (keep, got) in enumerate(((keep_a, got_a), (keep_b, got_b))):
        mine, theirs = keep[...].astype(F32), got[...].astype(F32)
        wide[s * MAIN_HALF : (s + 1) * MAIN_HALF] = mine[:MAIN_HALF] + theirs[:MAIN_HALF]
        start = TABLE_SPOT + 2 * s * TABLE_HALF
        wide[pl.ds(start + core * TABLE_HALF, TABLE_HALF)] = mine[MAIN_HALF:]
        wide[pl.ds(start + (1 - core) * TABLE_HALF, TABLE_HALF)] = theirs[MAIN_HALF:]
    out[...] = wide[...].astype(BF)


def table_places(own):
    core = lax.rem(lax.axis_index("lat"), 2)
    place = lax.axis_index("lon") * own + iota((own, 1, 1), 0)
    gains = (place == TABLE_SPOT + TABLE_HALF - 1) | (place == TABLE_SPOT + 2 * TABLE_HALF - 1)
    return (place >= TABLE_SPOT) & ~(gains & (core == 1))


def sum_sources(count, parts, out):
    own = out.shape[0]
    sums = jnp.sum(parts[...].astype(F32).reshape(count, own, 8, 128), axis=0)
    squares = jnp.sum(sums * sums, axis=(1, 2), keepdims=True)
    noted = (iota(sums.shape, 1) == 0) & (iota(sums.shape, 2) == NOTE) & table_places(own)
    out[...] = jnp.where(noted, squares, sums)


def spread_sums(count, mine, theirs, out):
    own = mine.shape[0]
    first = iota(mine.shape, 1) == 0
    lane = iota(mine.shape, 2)
    value = mine[...]
    both = value + theirs[...]
    upper = both.astype(BF).astype(F32)
    lower = jnp.sum(jnp.where(first & (lane == NOTE), both - upper, 0.0), axis=(1, 2), keepdims=True)
    noted = jnp.where(first & (lane == NOTE), upper, value)
    noted = jnp.where(first & (lane == NOTE + 1), lower, noted)
    result = jnp.where(table_places(own), noted, both)[None]
    out[...] = jnp.broadcast_to(result, (count,) + mine.shape).reshape(out.shape).astype(BF)


def constant_table(spread):
    spread[...] = table_spread()


def shifted_bias(table, valid, region, spread, bias, flat):
    build_bias(table[1, 0, 0], valid, region, True, bias, flat, spread[...])


def plain_forward(
    fields, upstream, gains, w_in, w_out, table, valid, region, spread,
    middle, own, one, two, three, hidden_out, triple_out, attention_out, mixture_out,
    cells, pieces, bias, flat,
):
    value = load_cells(fields, cells)
    unit, _ = norm_parts(value)
    hidden = (unit * gains[0:1, :]).astype(BF)
    hidden_out[...] = hidden
    triple = dot(hidden, w_in[0]).astype(BF)
    triple_out[...] = triple
    build_bias(table[0, 0, 0], valid, region, False, bias, flat, spread[...])
    _, attention, mixture = attend(*split_triple(triple), bias)
    attention_out[...] = attention
    mixture_out[...] = mixture
    added = dot(mixture, w_out[0]).astype(BF).astype(F32)
    result = (value + added).astype(BF)
    middle[...] = result
    unit, _ = norm_parts(result.astype(F32))
    hidden = (unit * gains[1:2, :]).astype(BF).astype(F32)
    raw = load_cells(upstream, cells)
    for index, (ref, (far_row, far_column)) in enumerate(zip((own, one, two, three), FIRST)):
        row_start, column_start = 3 - 3 * far_row, 6 * far_column
        for which, source in enumerate((hidden, raw)):
            for level in range(2):
                for inner in range(3):
                    start = ((1 - level) * 6 + row_start + inner) * WIN_SPAN + column_start
                    place = which * 36 + (level * 3 + inner) * 6
                    pieces[index, place : place + 6, :] = source[start : start + 6]
        ref[...] = pieces[index].astype(BF)


def gather_pieces(pieces, which, cells, forward):
    for piece, (far_row, far_column) in zip(pieces, FIRST if forward else SECOND):
        for level in range(2):
            for inner in range(3):
                if forward:
                    row, column, target = 3 * far_row + inner, 6 - 6 * far_column, level
                else:
                    row, column, target = 3 - 3 * far_row + inner, 6 * far_column, 1 - level
                start = (target * 6 + row) * WIN_SPAN + column
                place = which * 36 + (level * 3 + inner) * 6
                cells[start : start + 6, :] = piece[place : place + 6]
    return cells[...]


def shifted_core(
    own, one, two, three, bias, w_in, w_out,
    own_out, one_out, two_out, three_out, hidden_out, cot_out, triple_out, mixture_out, scores_out,
    cells, pieces_out,
):
    pieces = [ref[...].astype(F32) for ref in (own, one, two, three)]
    hidden = gather_pieces(pieces, 0, cells, True).astype(BF)
    grad_out = gather_pieces(pieces, 1, cells, True).astype(BF)
    hidden_out[...] = hidden
    cot_out[...] = grad_out
    triple = dot(hidden, w_in[1]).astype(BF)
    stacked = head_masked(dot(grad_out, w_out[1], 1, 1).astype(BF))
    query, keys, values = split_triple(triple)
    grad_attention = attention_gradient(stacked, values)
    weight, attention, mixture = attend(query, keys, values, bias)
    narrow = score_gradient(weight, grad_attention).astype(BF)
    grad_triple = triple_gradient(query, keys, attention, stacked, narrow)
    grad_hidden = dot(grad_triple, w_in[1], 1, 1).astype(BF).astype(F32)
    added = dot(mixture, w_out[1]).astype(BF).astype(F32)
    mixture_out[...] = mixture
    triple_out[...] = grad_triple
    scores_out[...] = narrow
    for index, ref in enumerate((own_out, one_out, two_out, three_out)):
        far_row, far_column = SECOND[index]
        for which, source in enumerate((added, grad_hidden)):
            for level in range(2):
                for inner in range(3):
                    start = (level * 6 + 3 * far_row + inner) * WIN_SPAN + 6 - 6 * far_column
                    place = which * 36 + (level * 3 + inner) * 6
                    pieces_out[index, place : place + 6, :] = source[start : start + 6]
        ref[...] = pieces_out[index].astype(BF)


def shifted_sums(hidden, cot, triple, mixture, scores, spread, keep, send, pay, gather):
    store_table(pay, scores[...].astype(F32), gather, spread)
    store_main(pay, dot(hidden[...], triple[...], 0, 0), dot(mixture[...], cot[...], 0, 0))
    send_payload(keep, send, pay, ())


def plain_backward(
    own, one, two, three, middle, upstream, fields, gains, w_in, w_out,
    hidden_in, triple_in, attention_in, mixture_in, spread,
    keep, send, middle_out, hidden_out,
    cells, pay, gather,
):
    pieces = [ref[...].astype(F32) for ref in (own, one, two, three)]
    grad_hidden = gather_pieces(pieces, 1, cells, False)
    unit, inverse = norm_parts(middle[...].astype(F32))
    norm_grad, gain_b = norm_backward(unit, inverse, gains[1:2, :], grad_hidden)
    grad_middle = (load_cells(upstream, cells) + norm_grad).astype(BF)
    middle_out[...] = grad_middle
    stacked = head_masked(dot(grad_middle, w_out[0], 1, 1).astype(BF))
    proj = dot(mixture_in[...], grad_middle, 0, 0)
    query, keys, values = split_triple(triple_in[...])
    attention = attention_in[...]
    grad_scores = score_gradient(attention.astype(F32), attention_gradient(stacked, values))
    grad_triple = triple_gradient(query, keys, attention, stacked, grad_scores.astype(BF))
    grad_hidden = dot(grad_triple, w_in[0], 1, 1).astype(BF)
    weight = dot(hidden_in[...], grad_triple, 0, 0)
    store_table(pay, grad_scores, gather, spread)
    store_main(pay, weight, proj)
    hidden_out[...] = grad_hidden
    unit, _ = norm_parts(load_cells(fields, cells))
    gain_a = jnp.sum(grad_hidden.astype(F32) * unit, axis=0, keepdims=True)
    send_payload(keep, send, pay, (gain_a, gain_b))


def plain_fields(
    own, one, two, three, middle, fields, gains, grad_middle, grad_hidden,
    updated, grad_fields,
    cells, native,
):
    pieces = [ref[...].astype(F32) for ref in (own, one, two, three)]
    store_cells(updated, middle[...].astype(F32) + gather_pieces(pieces, 0, cells, False), native)
    unit, inverse = norm_parts(load_cells(fields, cells))
    norm_grad, _ = norm_backward(unit, inverse, gains[0:1, :], grad_hidden[...].astype(F32))
    store_cells(grad_fields, grad_middle[...].astype(F32) + norm_grad, native)


def finish(own, other, grad_in, grad_proj, grad_bias, grad_gains, halves, flat):
    core = lax.rem(lax.axis_index("lat"), 2)
    s = pl.program_id(0)

    @pl.when(s == 0)
    def _():
        halves[core] = own[...].astype(F32)
        halves[1 - core] = other[...].astype(F32)
        gains = halves[1, TABLE_SPOT + TABLE_HALF - 1] + halves[1, TABLE_SPOT + 2 * TABLE_HALF - 1]
        for which in range(2):
            gain = gains[4 + 2 * which : 6 + 2 * which]
            factor = 1.0 / jnp.sqrt(jnp.sum(gain * gain, keepdims=True) / CHANNELS + RMS_EPS)
            grad_gains[which : which + 1, :128] = gain[0:1, :] * factor
            grad_gains[which : which + 1, 128:] = gain[1:2, : CHANNELS - 128] * factor

    main = jnp.concatenate(
        [halves[c // 3, pl.ds(s * MAIN_HALF + (c % 3) * 24, 24)].reshape(CHANNELS, 128)
         for c in range(6)],
        axis=1,
    )
    weight = main[:, : 3 * CHANNELS]
    factor = 1.0 / jnp.sqrt(jnp.sum(weight * weight, keepdims=True) / weight.size + RMS_EPS)
    grad_in[...] = weight * factor
    proj = main[:, 3 * CHANNELS :]
    factor = 1.0 / jnp.sqrt(jnp.sum(proj * proj, keepdims=True) / proj.size + RMS_EPS)
    grad_proj[...] = proj * factor
    start = TABLE_SPOT + 2 * s * TABLE_HALF
    every = halves[:, pl.ds(start, 2 * TABLE_HALF)]
    noted = (iota((8, 128), 0) == 0) & ((iota((8, 128), 1) >> 1) == NOTE // 2)
    squares = jnp.sum(jnp.where(noted, jnp.sum(every, axis=(0, 1)), 0.0), keepdims=True)
    start = start + core * TABLE_HALF
    found = [halves[half, pl.ds(start, TABLE_HALF)] for half in range(2)]
    found = jnp.concatenate([found[0], found[1][: TABLE_HALF - 1]], axis=0)
    factor = 1.0 / jnp.sqrt(squares / (4 * WINDOW * 6 * OFFSETS) + RMS_EPS)
    found = found.reshape(2 * TABLE_ROWS + FOLD_ROWS, 128) * factor
    parts = [found[:TABLE_ROWS], found[TABLE_ROWS : 2 * TABLE_ROWS]]
    tail = found[2 * TABLE_ROWS :]
    parts.append(jnp.concatenate(
        [tail, turn(tail[: TABLE_ROWS - FOLD_ROWS], -FOLD_LANES)], axis=0
    ))
    expand_table(parts, flat)
    grad_bias[...] = flat[:, :OFFSETS].reshape(HEADS, 2, 6, 6, 2, OFFSETS)


def whole():
    return pl.BlockSpec(memory_space=pltpu.VMEM)


def stepped(shape):
    return pl.BlockSpec((None,) + shape, lambda i: (i,) + (0,) * len(shape))


def run(body, outs, in_specs, scratch, args, out_specs=None, steps=1, cost=None):
    return pl.pallas_call(
        body,
        grid=(steps,),
        out_shape=[jax.ShapeDtypeStruct(shape, kind) for shape, kind in outs],
        in_specs=in_specs,
        out_specs=out_specs or [whole() for _ in outs],
        scratch_shapes=[
            pltpu.VMEM(shape, F32) if isinstance(shape, tuple) else shape for shape in scratch
        ],
        cost_estimate=cost and pl.CostEstimate(flops=cost, bytes_accessed=0, transcendentals=0),
        compiler_params=pltpu.CompilerParams(vmem_limit_bytes=40 * 1024 * 1024),
    )(*args)


CELLS = (WINDOW, CHANNELS)
PIECE = ((72, CHANNELS), BF)
NATIVE = (WIN_ROWS, WIN_SPAN, 2, CHANNELS)
WEIGHT = (CHANNELS, 3 * CHANNELS)
SQUARE = (CHANNELS, CHANNELS)
SCORES = (STACK, WINDOW)
SPREAD = (2, STACK, 128)
PAY = (2, HALF, 8, 128)
PART = ((HALF, 8, 128), BF)
GRADS = [((2,) + WEIGHT, F32), ((2,) + SQUARE, F32), ((2, 1, 1, HEADS, 2, 6, 6, 2, OFFSETS), F32)]


def exchange(pieces, sign):
    lons, lats = lax.axis_size("lon"), lax.axis_size("lat")

    def move(block, lon_step, lat_step):
        route = []
        for lon in range(lons):
            for lat in range(lats):
                target = ((lon - sign * lon_step) % lons) * lats + (lat + sign * lat_step) % lats
                route.append((lon * lats + lat, target))
        return lax.ppermute(block, AXES, route)

    order = FIRST if sign < 0 else SECOND
    moved = [move(piece, column, row) for piece, (row, column) in zip(pieces[1:], order[1:])]
    return [pieces[0], *moved]


def on_device(fields, upstream, gains, project_in, project_out, earth_bias, row_valid, regions):
    fields = fields.transpose(1, 2, 0, 3)
    upstream = upstream.transpose(1, 2, 0, 3)
    earth_bias = earth_bias.transpose(0, 1, 2, 3, 4, 6, 7, 5, 8)
    (spread,) = run(
        constant_table, [((TABLE_LANES, 256), BF)], [], [], (), cost=4_000_000_000
    )
    middle, *rest = run(
        plain_forward,
        [(CELLS, BF), PIECE, PIECE, PIECE, PIECE, (CELLS, BF), ((WINDOW, 3 * CHANNELS), BF),
         (SCORES, BF), (CELLS, BF)],
        [whole()] * 9,
        [CELLS, (4, 72, CHANNELS), SPREAD, (STACK, 128)],
        (fields, upstream, gains, project_in, project_out, earth_bias, row_valid, regions, spread),
    )
    pieces = exchange(rest[:4], -1)
    (bias,) = run(
        shifted_bias,
        [(SPREAD, F32)],
        [whole()] * 4,
        [(STACK, 128)],
        (earth_bias, row_valid, regions, spread),
    )
    saved = rest[4:]
    *back, hidden, cot, triple, mixture, scores = run(
        shifted_core,
        [PIECE, PIECE, PIECE, PIECE, (CELLS, BF), (CELLS, BF), ((WINDOW, 3 * CHANNELS), BF),
         (CELLS, BF), (SCORES, BF)],
        [whole()] * 7,
        [CELLS, (4, 72, CHANNELS)],
        (*pieces, bias, project_in, project_out),
    )
    back = exchange(back, 1)
    keep_b, send_b = run(
        shifted_sums,
        [PART, PART],
        [whole()] * 6,
        [PAY, SPREAD],
        (hidden, cot, triple, mixture, scores, spread),
    )
    got_b = swap(send_b, 1)
    keep_a, send_a, grad_middle, grad_hidden = run(
        plain_backward,
        [PART, PART, (CELLS, BF), (CELLS, BF)],
        [whole()] * 15,
        [CELLS, PAY, SPREAD],
        (*back, middle, upstream, fields, gains, project_in, project_out, *saved, spread),
    )
    got_a = swap(send_a, 1)
    lons = lax.axis_size("lon")
    own = SLOTS // lons
    tiles = (own * lons, 8, 128)
    message = (tiles, BF)
    shard = ((own, 8, 128), F32)
    (joined,) = run(
        join_cores, [message], [whole()] * 4, [tiles], (keep_a, got_a, keep_b, got_b)
    )
    (summed,) = run(
        functools.partial(sum_sources, lons), [shard], [whole()], [], (trade(joined),)
    )
    (result,) = run(
        functools.partial(spread_sums, lons), [message], [whole()] * 2, [],
        (summed, swap(summed, 2)),
    )
    mine = trade(result)
    updated, grad_fields = run(
        plain_fields,
        [(NATIVE, BF), (NATIVE, BF)],
        [whole()] * 9,
        [CELLS, NATIVE],
        (*back, middle, fields, gains, grad_middle, grad_hidden),
    )
    grad_in, grad_proj, grad_bias, grad_gains = run(
        finish,
        GRADS + [((2, CHANNELS), F32)],
        [whole()] * 2,
        [(2,) + tiles, (STACK, 128)],
        (mine, swap(mine, 1)),
        [stepped(WEIGHT), stepped(SQUARE), pl.BlockSpec(
            (None, None, None, HEADS, 2, 6, 6, 2, OFFSETS), lambda i: (i,) + (0,) * 8), whole()],
        2,
    )
    return (
        updated.transpose(2, 0, 1, 3),
        grad_fields.transpose(2, 0, 1, 3),
        grad_gains,
        grad_in,
        grad_proj,
        grad_bias.transpose(0, 1, 2, 3, 4, 7, 5, 6, 8),
    )


def swap(block, bit):
    count = lax.axis_size("lon") * lax.axis_size("lat")
    return lax.ppermute(block, AXES, [(d, d ^ bit) for d in range(count)])


def trade(block):
    return lax.all_to_all(block, "lon", 0, 0, tiled=True)


def solution(mesh):
    spec = P(None, "lat", "lon", None)
    bias_spec = P(None, None, "lat", None, None, None, None, None, None)
    return jax.shard_map(
        on_device,
        mesh=mesh,
        in_specs=(spec, spec, P(), P(), P(), bias_spec, P(), P()),
        out_specs=(spec, spec, P(), P(), P(), bias_spec),
        check_vma=False,
    )
```

```python
import functools

import jax
import jax.numpy as jnp
from jax import lax
from jax.experimental import pallas as pl
from jax.experimental.pallas import tpu as pltpu
from jax.sharding import PartitionSpec as P

CHANNELS = 192
HEADS = 6
HEAD_DIM = 32
WIN_ROWS = 6
WIN_SPAN = 12
WINDOW = 144
STACK = HEADS * WINDOW
GROUPS = 12
OFFSETS = 23
TABLE_LANES = 384
TABLE_ROWS = 72
NORM_EPS = 1e-05
RMS_EPS = 1e-06
SCALE = HEAD_DIM ** (-0.5)
MAIN_HALF = 72
TABLE_TILES = 24
TABLE_SPOT = 2 * MAIN_HALF
GAIN_SPOT = TABLE_SPOT + TABLE_TILES - 1
SLOTS = TABLE_SPOT + 2 * TABLE_TILES
FOLD_ROWS = 40
FOLD_LANES = 2 * OFFSETS
NOTE = 120
BF = jnp.bfloat16
F32 = jnp.float32
AXES = ("lon", "lat")
FIRST = ((0, 0), (1, 0), (1, 1), (0, 1))
SECOND = ((0, 0), (0, 1), (1, 1), (1, 0))


def dot(left, right, left_dim=1, right_dim=0):
    return lax.dot_general(
        left, right, (((left_dim,), (right_dim,)), ((), ())), preferred_element_type=F32
    )


def iota(shape, axis):
    return lax.broadcasted_iota(jnp.int32, shape, axis)


def load_cells(ref, scratch):
    value = ref[...].astype(F32)
    for block in range(GROUPS):
        scratch[block * WIN_SPAN : (block + 1) * WIN_SPAN, :] = value[block % 6, :, block // 6, :]
    return scratch[...]


def store_cells(ref, value, scratch):
    for block in range(GROUPS):
        scratch[block % 6, :, block // 6, :] = value[block * WIN_SPAN : (block + 1) * WIN_SPAN]
    ref[...] = scratch[...].astype(ref.dtype)


def norm_parts(value):
    center = value - jnp.mean(value, axis=1, keepdims=True)
    spread = jnp.mean(center * center, axis=1, keepdims=True)
    inverse = lax.rsqrt(spread + NORM_EPS)
    return center * inverse, inverse


def norm_backward(unit, inverse, gain, cotangent):
    scaled = cotangent * gain
    first = jnp.mean(scaled, axis=1, keepdims=True)
    second = jnp.mean(scaled * unit, axis=1, keepdims=True)
    grad = inverse * (scaled - first - unit * second)
    return grad, jnp.sum(cotangent * unit, axis=0, keepdims=True)


def head_masked(value):
    value = value.astype(F32)
    lane = iota(value.shape, 1)
    parts = [
        jnp.where((lane >= h * HEAD_DIM) & (lane < (h + 1) * HEAD_DIM), value, 0.0).astype(BF)
        for h in range(HEADS)
    ]
    return jnp.concatenate(parts, axis=0)


def head_merge(stacked):
    lane = iota((WINDOW, CHANNELS), 1)
    merged = stacked[:WINDOW]
    for h in range(1, HEADS):
        merged = jnp.where(lane >= h * HEAD_DIM, stacked[h * WINDOW : (h + 1) * WINDOW], merged)
    return merged


def table_spread():
    column = iota((1, 256), 1)
    group = (column * 5462) >> 16
    part = jnp.where(group >= 5, 1, 0) + jnp.where(group >= 10, 1, 0)
    wanted = part * 128 + (group - 5 * part) * OFFSETS + 11 - (column - WIN_SPAN * group)
    wanted = jnp.where(column < WINDOW, wanted, -1)
    return jnp.where(iota((TABLE_LANES, 256), 0) == wanted, 1.0, 0.0).astype(BF)


def group_spots():
    for group in range(GROUPS):
        yield (group % 6) * 2 + group // 6, group // 5, (group % 5) * OFFSETS


def turn(value, lanes):
    return value if lanes % 128 == 0 else pltpu.roll(value, lanes % 128, 1)


def compact_table(flat):
    parts = [jnp.zeros((TABLE_ROWS, 128), F32) for _ in range(3)]
    for row, part, lanes in group_spots():
        parts[part] = parts[part] + turn(flat[pl.ds(row, TABLE_ROWS, stride=GROUPS), :], lanes)
    return parts


def expand_table(parts, flat):
    lane = iota((TABLE_ROWS, 128), 1)
    for row, part, lanes in group_spots():
        value = jnp.where(lane < OFFSETS, turn(parts[part], -lanes), 0.0)
        flat[pl.ds(row, TABLE_ROWS, stride=GROUPS), :] = value


def cell_places(shape, axis, total, shifted):
    cell = iota(shape, axis)
    block = (cell * 5462) >> 16
    level = jnp.where(block >= 6, 1, 0)
    source = lax.axis_index("lat") * WIN_ROWS + block - 6 * level
    if shifted:
        source = source + WIN_ROWS // 2
        source = jnp.where(source >= total, source - total, source)
        level = 1 - level
    return level, source


def cell_labels(picked, level, source, axis):
    one, two = lax.slice_in_dim(picked, 0, 1, axis=axis), lax.slice_in_dim(picked, 1, 2, axis=axis)
    own = jnp.where(level == 0, one, two) + jnp.where(source < WIN_ROWS // 2, 4.0, 0.0)
    return own + jnp.where(level < 1, 8.0, 0.0)


def marks(valid, regions, shifted):
    total = valid.shape[1]
    level, source = cell_places((1, WINDOW), 1, total, shifted)
    pick = jnp.where(iota((total, WINDOW), 0) == source, 1.0, 0.0).astype(BF)
    usable = dot(valid.astype(F32).astype(BF), pick)
    if not shifted:
        return 0.0, jnp.where(usable > 0.5, 0.0, -1.0)
    regions = regions.astype(F32).astype(BF)
    key = jnp.where(usable > 0.5, cell_labels(dot(regions, pick), level, source, 0), -1.0)
    level, source = cell_places((WINDOW, 1), 0, total, shifted)
    pick = jnp.where(iota((WINDOW, total), 1) == source, 1.0, 0.0).astype(BF)
    return cell_labels(dot(pick, regions, 1, 1), level, source, 1), key


def build_bias(table, valid_ref, region_ref, shifted, bias, flat, spread):
    narrow = table.astype(F32).reshape(STACK, OFFSETS)
    flat[...] = jnp.concatenate([narrow, jnp.zeros((STACK, 128 - OFFSETS), F32)], axis=1)
    parts = compact_table(flat)
    turned = [
        jnp.concatenate([turn(part, -c) for part in parts], axis=1) for c in range(WIN_SPAN)
    ]
    wide = dot(jnp.concatenate(turned, axis=0).astype(BF), spread)
    for c in range(WIN_SPAN):
        part = wide[c * TABLE_ROWS : (c + 1) * TABLE_ROWS]
        for half in range(2):
            bias[half, pl.ds(c, TABLE_ROWS, stride=WIN_SPAN), :] = part[:, half * 128 : (half + 1) * 128]
    label, key = marks(valid_ref[...][None, :], region_ref[...], shifted)
    allowed = (label == key) | (iota((WINDOW, WINDOW), 0) == iota((WINDOW, WINDOW), 1))
    minus = jnp.where(allowed, 0.0, -jnp.inf)
    for h in range(HEADS):
        rows = slice(h * WINDOW, (h + 1) * WINDOW)
        bias[0, rows, :] = bias[0, rows, :] + minus[:, :128]
        bias[1, rows, : WINDOW - 128] = bias[1, rows, : WINDOW - 128] + minus[:, 128:]


def split_triple(triple):
    query = head_masked(triple[:, :CHANNELS])
    return query, triple[:, CHANNELS : 2 * CHANNELS], triple[:, 2 * CHANNELS :]


def attend(query, keys, values, bias):
    bias = jnp.concatenate([bias[0], bias[1, :, : WINDOW - 128]], axis=1)
    scores = dot(query, keys, 1, 1) * SCALE + bias
    raised = jnp.exp(scores - jnp.max(scores, axis=1, keepdims=True))
    weight = raised * (1.0 / jnp.sum(raised, axis=1, keepdims=True))
    attention = weight.astype(BF)
    mixture = head_merge(dot(attention, values)).astype(BF)
    return weight, attention, mixture


def attention_gradient(stacked, values):
    return dot(stacked, values, 1, 1).astype(BF).astype(F32)


def score_gradient(weight, grad_attention):
    product = weight * grad_attention
    return product - weight * jnp.sum(product, axis=1, keepdims=True)


def triple_gradient(query, keys, attention, stacked, narrow):
    grad_query = head_merge(dot(narrow, keys)) * SCALE
    grad_keys = dot(narrow, query, 0, 0) * SCALE
    grad_values = dot(attention, stacked, 0, 0)
    return jnp.concatenate([grad_query, grad_keys, grad_values], axis=1).astype(BF)


def store_table(keep, grad_scores, gather, spread_ref):
    gather[0] = grad_scores[:, :128]
    gather[1] = jnp.concatenate(
        [grad_scores[:, 128:], jnp.zeros((STACK, 256 - WINDOW), F32)], axis=1
    )
    halves = [
        jnp.concatenate(
            [gather[half, pl.ds(c, TABLE_ROWS, stride=WIN_SPAN), :] for c in range(WIN_SPAN)], axis=0
        )
        for half in range(2)
    ]
    wide = dot(jnp.concatenate(halves, axis=1).astype(BF), spread_ref[...], 1, 1)
    tiles = []
    for part in range(3):
        total = wide[:TABLE_ROWS, part * 128 : (part + 1) * 128]
        for c in range(1, WIN_SPAN):
            rows = slice(c * TABLE_ROWS, (c + 1) * TABLE_ROWS)
            total = total + turn(wide[rows, part * 128 : (part + 1) * 128], c)
        tiles.append(total)
    tail = jnp.concatenate(
        [turn(tiles[2][FOLD_ROWS:], FOLD_LANES), jnp.zeros((2 * FOLD_ROWS - TABLE_ROWS, 128), F32)],
        axis=0,
    )
    tiles[2] = tiles[2][:FOLD_ROWS] + tail
    tiles = jnp.concatenate(tiles, axis=0).reshape(TABLE_TILES - 1, 8, 128)
    keep[MAIN_HALF : MAIN_HALF + TABLE_TILES - 1] = tiles.astype(BF)


def store_main(pay, weight, proj):
    whole_columns = jnp.concatenate([weight, proj], axis=1)
    for c in range(6):
        start = (c % 3) * 24
        pay[c // 3, start : start + 24] = whole_columns[:, c * 128 : (c + 1) * 128].reshape(24, 8, 128).astype(BF)


def send_payload(keep, send, pay, gains):
    keep[MAIN_HALF + TABLE_TILES - 1] = gain_tile(gains).astype(BF)
    core = lax.rem(lax.axis_index("lat"), 2)
    keep[:MAIN_HALF] = pay[core]
    send[...] = pay[1 - core]


def gain_tile(gains):
    rows = []
    for gain in gains:
        rows.append(gain[:, :128])
        rows.append(jnp.concatenate([gain[:, 128:], jnp.zeros((1, 256 - CHANNELS), F32)], axis=1))
    return jnp.concatenate([jnp.zeros((8 - len(rows), 128), F32)] + rows, axis=0)


def join_cores(keep_a, got_a, keep_b, got_b, out):
    for s, (keep, got) in enumerate(((keep_a, got_a), (keep_b, got_b))):
        total = keep[:MAIN_HALF].astype(F32) + got[...].astype(F32)
        out[s * MAIN_HALF : (s + 1) * MAIN_HALF] = total.astype(BF)
        start = TABLE_SPOT + s * TABLE_TILES
        out[start : start + TABLE_TILES] = keep[MAIN_HALF:]


def table_places(own):
    place = lax.axis_index("lon") * own + iota((own, 1, 1), 0)
    return (place >= TABLE_SPOT) & (place != GAIN_SPOT)


def sum_sources(count, parts, out):
    own = out.shape[0]
    sums = jnp.sum(parts[...].astype(F32).reshape(count, own, 8, 128), axis=0)
    squares = jnp.sum(sums * sums, axis=(1, 2), keepdims=True)
    noted = (iota(sums.shape, 1) == 0) & (iota(sums.shape, 2) == NOTE) & table_places(own)
    out[...] = jnp.where(noted, squares, sums)


def spread_sums(count, mine, theirs, _, out):
    own = mine.shape[0]
    first = iota(mine.shape, 1) == 0
    lane = iota(mine.shape, 2)
    value = mine[...]
    both = value + theirs[...]
    upper = both.astype(BF).astype(F32)
    lower = jnp.sum(jnp.where(first & (lane == NOTE), both - upper, 0.0), axis=(1, 2), keepdims=True)
    noted = jnp.where(first & (lane == NOTE), upper, value)
    noted = jnp.where(first & (lane == NOTE + 1), lower, noted)
    result = jnp.where(table_places(own), noted, both)[None]
    out[...] = jnp.broadcast_to(result, (count,) + mine.shape).reshape(out.shape).astype(BF)


def constant_table(spread):
    spread[...] = table_spread()


def shifted_bias(table, valid, region, spread, bias, flat):
    build_bias(table[1, 0, 0], valid, region, True, bias, flat, spread[...])


def plain_forward(
    fields, upstream, gains, w_in, w_out, table, valid, region, spread,
    middle, own, one, two, three, hidden_out, triple_out, attention_out, mixture_out,
    cells, pieces, bias, flat,
):
    value = load_cells(fields, cells)
    unit, _ = norm_parts(value)
    hidden = (unit * gains[0:1, :]).astype(BF)
    hidden_out[...] = hidden
    triple = dot(hidden, w_in[0]).astype(BF)
    triple_out[...] = triple
    build_bias(table[0, 0, 0], valid, region, False, bias, flat, spread[...])
    _, attention, mixture = attend(*split_triple(triple), bias)
    attention_out[...] = attention
    mixture_out[...] = mixture
    added = dot(mixture, w_out[0]).astype(BF).astype(F32)
    result = (value + added).astype(BF)
    middle[...] = result
    unit, _ = norm_parts(result.astype(F32))
    hidden = (unit * gains[1:2, :]).astype(BF).astype(F32)
    raw = load_cells(upstream, cells)
    for index, (ref, (far_row, far_column)) in enumerate(zip((own, one, two, three), FIRST)):
        row_start, column_start = 3 - 3 * far_row, 6 * far_column
        for which, source in enumerate((hidden, raw)):
            for level in range(2):
                for inner in range(3):
                    start = ((1 - level) * 6 + row_start + inner) * WIN_SPAN + column_start
                    place = which * 36 + (level * 3 + inner) * 6
                    pieces[index, place : place + 6, :] = source[start : start + 6]
        ref[...] = pieces[index].astype(BF)


def gather_pieces(pieces, which, cells, forward):
    for piece, (far_row, far_column) in zip(pieces, FIRST if forward else SECOND):
        for level in range(2):
            for inner in range(3):
                if forward:
                    row, column, target = 3 * far_row + inner, 6 - 6 * far_column, level
                else:
                    row, column, target = 3 - 3 * far_row + inner, 6 * far_column, 1 - level
                start = (target * 6 + row) * WIN_SPAN + column
                place = which * 36 + (level * 3 + inner) * 6
                cells[start : start + 6, :] = piece[place : place + 6]
    return cells[...]


def shifted_core(
    own, one, two, three, bias, w_in, w_out,
    own_out, one_out, two_out, three_out, hidden_out, cot_out, triple_out, mixture_out, scores_out,
    cells, pieces_out,
):
    pieces = [ref[...].astype(F32) for ref in (own, one, two, three)]
    hidden = gather_pieces(pieces, 0, cells, True).astype(BF)
    grad_out = gather_pieces(pieces, 1, cells, True).astype(BF)
    hidden_out[...] = hidden
    cot_out[...] = grad_out
    triple = dot(hidden, w_in[1]).astype(BF)
    stacked = head_masked(dot(grad_out, w_out[1], 1, 1).astype(BF))
    query, keys, values = split_triple(triple)
    grad_attention = attention_gradient(stacked, values)
    weight, attention, mixture = attend(query, keys, values, bias)
    narrow = score_gradient(weight, grad_attention).astype(BF)
    grad_triple = triple_gradient(query, keys, attention, stacked, narrow)
    grad_hidden = dot(grad_triple, w_in[1], 1, 1).astype(BF).astype(F32)
    added = dot(mixture, w_out[1]).astype(BF).astype(F32)
    mixture_out[...] = mixture
    triple_out[...] = grad_triple
    scores_out[...] = narrow
    for index, ref in enumerate((own_out, one_out, two_out, three_out)):
        far_row, far_column = SECOND[index]
        for which, source in enumerate((added, grad_hidden)):
            for level in range(2):
                for inner in range(3):
                    start = (level * 6 + 3 * far_row + inner) * WIN_SPAN + 6 - 6 * far_column
                    place = which * 36 + (level * 3 + inner) * 6
                    pieces_out[index, place : place + 6, :] = source[start : start + 6]
        ref[...] = pieces_out[index].astype(BF)


def shifted_sums(hidden, cot, triple, mixture, scores, spread, keep, send, pay, gather):
    store_table(keep, scores[...].astype(F32), gather, spread)
    store_main(pay, dot(hidden[...], triple[...], 0, 0), dot(mixture[...], cot[...], 0, 0))
    send_payload(keep, send, pay, ())


def ready_backward(
    middle, upstream, fields, triple,
    unit_b, inverse_b, cotangent, unit_a, query_out, keys_out, values_out,
    cells,
):
    unit, inverse = norm_parts(middle[...].astype(F32))
    unit_b[...] = unit
    inverse_b[...] = jnp.broadcast_to(inverse, inverse_b.shape)
    cotangent[...] = load_cells(upstream, cells)
    unit, _ = norm_parts(load_cells(fields, cells))
    unit_a[...] = unit
    query_out[...], keys_out[...], values_out[...] = split_triple(triple[...])


def plain_backward(
    own, one, two, three, gains, w_in, w_out, hidden_in, attention_in, mixture_in, spread,
    unit_b, inverse_b, cotangent, unit_a, query, keys, values,
    keep, send, middle_out, hidden_out,
    cells, pay, gather,
):
    pieces = [ref[...].astype(F32) for ref in (own, one, two, three)]
    grad_hidden = gather_pieces(pieces, 1, cells, False)
    norm_grad, gain_b = norm_backward(unit_b[...], inverse_b[:, :1], gains[1:2, :], grad_hidden)
    grad_middle = (cotangent[...] + norm_grad).astype(BF)
    middle_out[...] = grad_middle
    stacked = head_masked(dot(grad_middle, w_out[0], 1, 1).astype(BF))
    proj = dot(mixture_in[...], grad_middle, 0, 0)
    attention = attention_in[...]
    grad_scores = score_gradient(attention.astype(F32), attention_gradient(stacked, values[...]))
    grad_triple = triple_gradient(query[...], keys[...], attention, stacked, grad_scores.astype(BF))
    grad_hidden = dot(grad_triple, w_in[0], 1, 1).astype(BF)
    weight = dot(hidden_in[...], grad_triple, 0, 0)
    store_table(keep, grad_scores, gather, spread)
    store_main(pay, weight, proj)
    hidden_out[...] = grad_hidden
    gain_a = jnp.sum(grad_hidden.astype(F32) * unit_a[...], axis=0, keepdims=True)
    send_payload(keep, send, pay, (gain_a, gain_b))


def plain_fields(
    own, one, two, three, middle, fields, gains, grad_middle, grad_hidden,
    updated, grad_fields, token,
    cells, native,
):
    token[...] = jnp.zeros(token.shape, F32)
    pieces = [ref[...].astype(F32) for ref in (own, one, two, three)]
    store_cells(updated, middle[...].astype(F32) + gather_pieces(pieces, 0, cells, False), native)
    unit, inverse = norm_parts(load_cells(fields, cells))
    norm_grad, _ = norm_backward(unit, inverse, gains[0:1, :], grad_hidden[...].astype(F32))
    store_cells(grad_fields, grad_middle[...].astype(F32) + norm_grad, native)


def unfold_tables(mine, out, flat):
    for s in range(2):
        start = TABLE_SPOT + s * TABLE_TILES
        found = mine[start : start + TABLE_TILES - 1].astype(F32)
        found = found.reshape(2 * TABLE_ROWS + FOLD_ROWS, 128)
        parts = [found[:TABLE_ROWS], found[TABLE_ROWS : 2 * TABLE_ROWS]]
        tail = found[2 * TABLE_ROWS :]
        parts.append(jnp.concatenate(
            [tail, turn(tail[: TABLE_ROWS - FOLD_ROWS], -FOLD_LANES)], axis=0
        ))
        expand_table(parts, flat)
        out[s] = flat[:, :OFFSETS].reshape(HEADS, 2, 6, 6, 2, OFFSETS)


def unit_factor(square_sum, count):
    return 1.0 / jnp.sqrt(square_sum / count + RMS_EPS)


def finish(own, other, tables, grad_in, grad_proj, grad_bias, grad_gains, halves):
    core = lax.rem(lax.axis_index("lat"), 2)
    s = pl.program_id(0)

    @pl.when(s == 0)
    def _():
        halves[core] = own[:TABLE_SPOT].astype(F32)
        halves[1 - core] = other[:TABLE_SPOT].astype(F32)
        gains = own[GAIN_SPOT].astype(F32) + other[GAIN_SPOT].astype(F32)
        for which in range(2):
            gain = gains[4 + 2 * which : 6 + 2 * which]
            factor = unit_factor(jnp.sum(gain * gain, keepdims=True), CHANNELS)
            grad_gains[which : which + 1, :128] = gain[0:1, :] * factor
            grad_gains[which : which + 1, 128:] = gain[1:2, : CHANNELS - 128] * factor

    main = jnp.concatenate(
        [halves[c // 3, pl.ds(s * MAIN_HALF + (c % 3) * 24, 24)].reshape(CHANNELS, 128)
         for c in range(6)],
        axis=1,
    )
    weight = main[:, : 3 * CHANNELS]
    grad_in[...] = weight * unit_factor(jnp.sum(weight * weight, keepdims=True), weight.size)
    proj = main[:, 3 * CHANNELS :]
    grad_proj[...] = proj * unit_factor(jnp.sum(proj * proj, keepdims=True), proj.size)
    rows = pl.ds(TABLE_SPOT + s * TABLE_TILES, TABLE_TILES - 1)
    every = jnp.sum(own[rows].astype(F32) + other[rows].astype(F32), axis=0)
    noted = (iota((8, 128), 0) == 0) & ((iota((8, 128), 1) >> 1) == NOTE // 2)
    squares = jnp.sum(jnp.where(noted, every, 0.0), keepdims=True)
    factor = unit_factor(squares, 4 * WINDOW * 6 * OFFSETS)
    grad_bias[...] = tables[s] * factor[None, None, None, None]


def whole():
    return pl.BlockSpec(memory_space=pltpu.VMEM)


def stepped(shape):
    return pl.BlockSpec((None,) + shape, lambda i: (i,) + (0,) * len(shape))


def run(body, outs, in_specs, scratch, args, out_specs=None, steps=1, cost=None):
    return pl.pallas_call(
        body,
        grid=(steps,),
        out_shape=[jax.ShapeDtypeStruct(shape, kind) for shape, kind in outs],
        in_specs=in_specs,
        out_specs=out_specs or [whole() for _ in outs],
        scratch_shapes=[
            pltpu.VMEM(shape, F32) if isinstance(shape, tuple) else shape for shape in scratch
        ],
        cost_estimate=cost and pl.CostEstimate(flops=cost, bytes_accessed=0, transcendentals=0),
        compiler_params=pltpu.CompilerParams(vmem_limit_bytes=40 * 1024 * 1024),
    )(*args)


CELLS = (WINDOW, CHANNELS)
PIECE = ((72, CHANNELS), BF)
NATIVE = (WIN_ROWS, WIN_SPAN, 2, CHANNELS)
WEIGHT = (CHANNELS, 3 * CHANNELS)
SQUARE = (CHANNELS, CHANNELS)
SCORES = (STACK, WINDOW)
SPREAD = (2, STACK, 128)
PAY = pltpu.VMEM((2, MAIN_HALF, 8, 128), BF)
PARTS = [((MAIN_HALF + TABLE_TILES, 8, 128), BF), ((MAIN_HALF, 8, 128), BF)]
TABLES = (2, HEADS, 2, 6, 6, 2, OFFSETS)
GRADS = [((2,) + WEIGHT, F32), ((2,) + SQUARE, F32), ((2, 1, 1, HEADS, 2, 6, 6, 2, OFFSETS), F32)]


def exchange(pieces, sign):
    lons, lats = lax.axis_size("lon"), lax.axis_size("lat")

    def move(block, lon_step, lat_step):
        route = []
        for lon in range(lons):
            for lat in range(lats):
                target = ((lon - sign * lon_step) % lons) * lats + (lat + sign * lat_step) % lats
                route.append((lon * lats + lat, target))
        return lax.ppermute(block, AXES, route)

    order = FIRST if sign < 0 else SECOND
    moved = [move(piece, column, row) for piece, (row, column) in zip(pieces[1:], order[1:])]
    return [pieces[0], *moved]


def on_device(fields, upstream, gains, project_in, project_out, earth_bias, row_valid, regions):
    fields = fields.transpose(1, 2, 0, 3)
    upstream = upstream.transpose(1, 2, 0, 3)
    earth_bias = earth_bias.transpose(0, 1, 2, 3, 4, 6, 7, 5, 8)
    (spread,) = run(
        constant_table, [((TABLE_LANES, 256), BF)], [], [], (), cost=4_000_000_000
    )
    middle, *rest = run(
        plain_forward,
        [(CELLS, BF), PIECE, PIECE, PIECE, PIECE, (CELLS, BF), ((WINDOW, 3 * CHANNELS), BF),
         (SCORES, BF), (CELLS, BF)],
        [whole()] * 9,
        [CELLS, (4, 72, CHANNELS), SPREAD, (STACK, 128)],
        (fields, upstream, gains, project_in, project_out, earth_bias, row_valid, regions, spread),
    )
    pieces = exchange(rest[:4], -1)
    (bias,) = run(
        shifted_bias,
        [(SPREAD, F32)],
        [whole()] * 4,
        [(STACK, 128)],
        (earth_bias, row_valid, regions, spread),
    )
    saved = rest[4:]
    ready = run(
        ready_backward,
        [(CELLS, F32), ((WINDOW, 128), F32), (CELLS, F32), (CELLS, F32),
         ((STACK, CHANNELS), BF), (CELLS, BF), (CELLS, BF)],
        [whole()] * 4,
        [CELLS],
        (middle, upstream, fields, saved[1]),
    )
    *back, hidden, cot, triple, mixture, scores = run(
        shifted_core,
        [PIECE, PIECE, PIECE, PIECE, (CELLS, BF), (CELLS, BF), ((WINDOW, 3 * CHANNELS), BF),
         (CELLS, BF), (SCORES, BF)],
        [whole()] * 7,
        [CELLS, (4, 72, CHANNELS)],
        (*pieces, bias, project_in, project_out),
    )
    back = exchange(back, 1)
    keep_b, send_b = run(
        shifted_sums,
        PARTS,
        [whole()] * 6,
        [PAY, SPREAD],
        (hidden, cot, triple, mixture, scores, spread),
    )
    got_b = swap(send_b, 1)
    keep_a, send_a, grad_middle, grad_hidden = run(
        plain_backward,
        PARTS + [(CELLS, BF), (CELLS, BF)],
        [whole()] * 18,
        [CELLS, PAY, SPREAD],
        (*back, gains, project_in, project_out, saved[0], saved[2], saved[3], spread, *ready),
    )
    got_a = swap(send_a, 1)
    lons = lax.axis_size("lon")
    own = SLOTS // lons
    tiles = (own * lons, 8, 128)
    message = (tiles, BF)
    shard = ((own, 8, 128), F32)
    (joined,) = run(
        join_cores, [message], [whole()] * 4, [], (keep_a, got_a, keep_b, got_b)
    )
    (summed,) = run(
        functools.partial(sum_sources, lons), [shard], [whole()], [], (trade(joined),)
    )
    updated, grad_fields, token = run(
        plain_fields,
        [(NATIVE, BF), (NATIVE, BF), ((8, 128), F32)],
        [whole()] * 9,
        [CELLS, NATIVE],
        (*back, middle, fields, gains, grad_middle, grad_hidden),
    )
    (result,) = run(
        functools.partial(spread_sums, lons), [message], [whole()] * 3, [],
        (summed, swap(summed, 2), token),
    )
    mine = trade(result)
    (tables,) = run(unfold_tables, [(TABLES, F32)], [whole()], [(STACK, 128)], (mine,))
    grad_in, grad_proj, grad_bias, grad_gains = run(
        finish,
        GRADS + [((2, CHANNELS), F32)],
        [whole()] * 3,
        [(2, TABLE_SPOT, 8, 128)],
        (mine, swap(mine, 1), tables),
        [stepped(WEIGHT), stepped(SQUARE), pl.BlockSpec(
            (None, None, None, HEADS, 2, 6, 6, 2, OFFSETS), lambda i: (i,) + (0,) * 8), whole()],
        2,
    )
    return (
        updated.transpose(2, 0, 1, 3),
        grad_fields.transpose(2, 0, 1, 3),
        grad_gains,
        grad_in,
        grad_proj,
        grad_bias.transpose(0, 1, 2, 3, 4, 7, 5, 6, 8),
    )


def swap(block, bit):
    count = lax.axis_size("lon") * lax.axis_size("lat")
    return lax.ppermute(block, AXES, [(d, d ^ bit) for d in range(count)])


def trade(block):
    return lax.all_to_all(block, "lon", 0, 0, tiled=True)


def solution(mesh):
    spec = P(None, "lat", "lon", None)
    bias_spec = P(None, None, "lat", None, None, None, None, None, None)
    return jax.shard_map(
        on_device,
        mesh=mesh,
        in_specs=(spec, spec, P(), P(), P(), bias_spec, P(), P()),
        out_specs=(spec, spec, P(), P(), P(), bias_spec),
        check_vma=False,
    )
```

```python
import functools

import jax
import jax.numpy as jnp
from jax import lax
from jax.experimental import pallas as pl
from jax.experimental.pallas import tpu as pltpu
from jax.sharding import PartitionSpec as P

CHANNELS = 192
HEADS = 6
HEAD_DIM = 32
WIN_ROWS = 6
WIN_SPAN = 12
WINDOW = 144
STACK = HEADS * WINDOW
GROUPS = 12
OFFSETS = 23
TABLE_LANES = 384
TABLE_ROWS = 72
NORM_EPS = 1e-05
RMS_EPS = 1e-06
SCALE = HEAD_DIM ** (-0.5)
MAIN_HALF = 72
TABLE_TILES = 24
TABLE_SPOT = 2 * MAIN_HALF
GAIN_SPOT = TABLE_SPOT + TABLE_TILES - 1
SLOTS = TABLE_SPOT + 2 * TABLE_TILES
FOLD_ROWS = 40
FOLD_LANES = 2 * OFFSETS
NOTE = 120
BF = jnp.bfloat16
F32 = jnp.float32
AXES = ("lon", "lat")
FIRST = ((0, 0), (1, 0), (1, 1), (0, 1))
SECOND = ((0, 0), (0, 1), (1, 1), (1, 0))


def dot(left, right, left_dim=1, right_dim=0):
    return lax.dot_general(
        left, right, (((left_dim,), (right_dim,)), ((), ())), preferred_element_type=F32
    )


def iota(shape, axis):
    return lax.broadcasted_iota(jnp.int32, shape, axis)


def load_cells(ref, scratch):
    value = ref[...].astype(F32)
    for block in range(GROUPS):
        scratch[block * WIN_SPAN : (block + 1) * WIN_SPAN, :] = value[block % 6, :, block // 6, :]
    return scratch[...]


def store_cells(ref, value, scratch):
    for block in range(GROUPS):
        scratch[block % 6, :, block // 6, :] = value[block * WIN_SPAN : (block + 1) * WIN_SPAN]
    ref[...] = scratch[...].astype(ref.dtype)


def norm_parts(value):
    center = value - jnp.mean(value, axis=1, keepdims=True)
    spread = jnp.mean(center * center, axis=1, keepdims=True)
    inverse = lax.rsqrt(spread + NORM_EPS)
    return center * inverse, inverse


def norm_backward(unit, inverse, gain, cotangent):
    scaled = cotangent * gain
    first = jnp.mean(scaled, axis=1, keepdims=True)
    second = jnp.mean(scaled * unit, axis=1, keepdims=True)
    grad = inverse * (scaled - first - unit * second)
    return grad, jnp.sum(cotangent * unit, axis=0, keepdims=True)


def head_masked(value):
    value = value.astype(F32)
    lane = iota(value.shape, 1)
    parts = [
        jnp.where((lane >= h * HEAD_DIM) & (lane < (h + 1) * HEAD_DIM), value, 0.0).astype(BF)
        for h in range(HEADS)
    ]
    return jnp.concatenate(parts, axis=0)


def head_merge(stacked):
    lane = iota((WINDOW, CHANNELS), 1)
    merged = stacked[:WINDOW]
    for h in range(1, HEADS):
        merged = jnp.where(lane >= h * HEAD_DIM, stacked[h * WINDOW : (h + 1) * WINDOW], merged)
    return merged


def table_spread():
    column = iota((1, 256), 1)
    group = (column * 5462) >> 16
    part = jnp.where(group >= 5, 1, 0) + jnp.where(group >= 10, 1, 0)
    wanted = part * 128 + (group - 5 * part) * OFFSETS + 11 - (column - WIN_SPAN * group)
    wanted = jnp.where(column < WINDOW, wanted, -1)
    return jnp.where(iota((TABLE_LANES, 256), 0) == wanted, 1.0, 0.0).astype(BF)


def group_spots():
    for group in range(GROUPS):
        yield (group % 6) * 2 + group // 6, group // 5, (group % 5) * OFFSETS


def turn(value, lanes):
    return value if lanes % 128 == 0 else pltpu.roll(value, lanes % 128, 1)


def compact_table(flat):
    parts = [jnp.zeros((TABLE_ROWS, 128), F32) for _ in range(3)]
    for row, part, lanes in group_spots():
        parts[part] = parts[part] + turn(flat[pl.ds(row, TABLE_ROWS, stride=GROUPS), :], lanes)
    return parts


def expand_table(parts, flat):
    lane = iota((TABLE_ROWS, 128), 1)
    for row, part, lanes in group_spots():
        value = jnp.where(lane < OFFSETS, turn(parts[part], -lanes), 0.0)
        flat[pl.ds(row, TABLE_ROWS, stride=GROUPS), :] = value


def cell_places(shape, axis, total, shifted):
    cell = iota(shape, axis)
    block = (cell * 5462) >> 16
    level = jnp.where(block >= 6, 1, 0)
    source = lax.axis_index("lat") * WIN_ROWS + block - 6 * level
    if shifted:
        source = source + WIN_ROWS // 2
        source = jnp.where(source >= total, source - total, source)
        level = 1 - level
    return level, source


def cell_labels(picked, level, source, axis):
    one, two = lax.slice_in_dim(picked, 0, 1, axis=axis), lax.slice_in_dim(picked, 1, 2, axis=axis)
    own = jnp.where(level == 0, one, two) + jnp.where(source < WIN_ROWS // 2, 4.0, 0.0)
    return own + jnp.where(level < 1, 8.0, 0.0)


def marks(valid, regions, shifted):
    total = valid.shape[1]
    level, source = cell_places((1, WINDOW), 1, total, shifted)
    pick = jnp.where(iota((total, WINDOW), 0) == source, 1.0, 0.0).astype(BF)
    usable = dot(valid.astype(F32).astype(BF), pick)
    if not shifted:
        return 0.0, jnp.where(usable > 0.5, 0.0, -1.0)
    regions = regions.astype(F32).astype(BF)
    key = jnp.where(usable > 0.5, cell_labels(dot(regions, pick), level, source, 0), -1.0)
    level, source = cell_places((WINDOW, 1), 0, total, shifted)
    pick = jnp.where(iota((WINDOW, total), 1) == source, 1.0, 0.0).astype(BF)
    return cell_labels(dot(pick, regions, 1, 1), level, source, 1), key


def build_bias(table, valid_ref, region_ref, shifted, bias, flat, spread):
    narrow = table.astype(F32).reshape(STACK, OFFSETS)
    flat[...] = jnp.concatenate([narrow, jnp.zeros((STACK, 128 - OFFSETS), F32)], axis=1)
    parts = compact_table(flat)
    turned = [
        jnp.concatenate([turn(part, -c) for part in parts], axis=1) for c in range(WIN_SPAN)
    ]
    wide = dot(jnp.concatenate(turned, axis=0).astype(BF), spread)
    for c in range(WIN_SPAN):
        part = wide[c * TABLE_ROWS : (c + 1) * TABLE_ROWS]
        for half in range(2):
            bias[half, pl.ds(c, TABLE_ROWS, stride=WIN_SPAN), :] = part[:, half * 128 : (half + 1) * 128]
    label, key = marks(valid_ref[...][None, :], region_ref[...], shifted)
    allowed = (label == key) | (iota((WINDOW, WINDOW), 0) == iota((WINDOW, WINDOW), 1))
    minus = jnp.where(allowed, 0.0, -jnp.inf)
    for h in range(HEADS):
        rows = slice(h * WINDOW, (h + 1) * WINDOW)
        bias[0, rows, :] = bias[0, rows, :] + minus[:, :128]
        bias[1, rows, : WINDOW - 128] = bias[1, rows, : WINDOW - 128] + minus[:, 128:]


def split_triple(triple):
    query = head_masked(triple[:, :CHANNELS])
    return query, triple[:, CHANNELS : 2 * CHANNELS], triple[:, 2 * CHANNELS :]


def attend(query, keys, values, bias):
    bias = jnp.concatenate([bias[0], bias[1, :, : WINDOW - 128]], axis=1)
    scores = dot(query, keys, 1, 1) * SCALE + bias
    raised = jnp.exp(scores - jnp.max(scores, axis=1, keepdims=True))
    weight = raised * (1.0 / jnp.sum(raised, axis=1, keepdims=True))
    attention = weight.astype(BF)
    mixture = head_merge(dot(attention, values)).astype(BF)
    return weight, attention, mixture


def attention_gradient(stacked, values):
    return dot(stacked, values, 1, 1).astype(BF).astype(F32)


def score_gradient(weight, grad_attention):
    product = weight * grad_attention
    return product - weight * jnp.sum(product, axis=1, keepdims=True)


def triple_gradient(query, keys, attention, stacked, narrow):
    grad_query = head_merge(dot(narrow, keys)) * SCALE
    grad_keys = dot(narrow, query, 0, 0) * SCALE
    grad_values = dot(attention, stacked, 0, 0)
    return jnp.concatenate([grad_query, grad_keys, grad_values], axis=1).astype(BF)


def store_table(table, grad_scores, gather, spread_ref, gains):
    gather[0] = grad_scores[:, :128]
    gather[1] = jnp.concatenate(
        [grad_scores[:, 128:], jnp.zeros((STACK, 256 - WINDOW), F32)], axis=1
    )
    halves = [
        jnp.concatenate(
            [gather[half, pl.ds(c, TABLE_ROWS, stride=WIN_SPAN), :] for c in range(WIN_SPAN)], axis=0
        )
        for half in range(2)
    ]
    wide = dot(jnp.concatenate(halves, axis=1).astype(BF), spread_ref[...], 1, 1)
    tiles = []
    for part in range(3):
        total = wide[:TABLE_ROWS, part * 128 : (part + 1) * 128]
        for c in range(1, WIN_SPAN):
            rows = slice(c * TABLE_ROWS, (c + 1) * TABLE_ROWS)
            total = total + turn(wide[rows, part * 128 : (part + 1) * 128], c)
        tiles.append(total)
    tail = jnp.concatenate(
        [turn(tiles[2][FOLD_ROWS:], FOLD_LANES), jnp.zeros((2 * FOLD_ROWS - TABLE_ROWS, 128), F32)],
        axis=0,
    )
    tiles[2] = tiles[2][:FOLD_ROWS] + tail
    tiles = jnp.concatenate(tiles, axis=0).reshape(TABLE_TILES - 1, 8, 128)
    table[: TABLE_TILES - 1] = tiles.astype(BF)
    table[TABLE_TILES - 1] = gain_tile(gains).astype(BF)


def store_main(pay, weight, proj):
    whole_columns = jnp.concatenate([weight, proj], axis=1)
    for c in range(6):
        start = (c % 3) * 24
        pay[c // 3, start : start + 24] = whole_columns[:, c * 128 : (c + 1) * 128].reshape(24, 8, 128).astype(BF)


def send_payload(keep, send, pay):
    core = lax.rem(lax.axis_index("lat"), 2)
    keep[...] = pay[core]
    send[...] = pay[1 - core]


def gain_tile(gains):
    rows = []
    for gain in gains:
        rows.append(gain[:, :128])
        rows.append(jnp.concatenate([gain[:, 128:], jnp.zeros((1, 256 - CHANNELS), F32)], axis=1))
    return jnp.concatenate([jnp.zeros((8 - len(rows), 128), F32)] + rows, axis=0)


def join_cores(keep_a, got_a, table_a, keep_b, got_b, table_b, out):
    parts = ((keep_a, got_a, table_a), (keep_b, got_b, table_b))
    for s, (keep, got, table) in enumerate(parts):
        total = keep[...].astype(F32) + got[...].astype(F32)
        out[s * MAIN_HALF : (s + 1) * MAIN_HALF] = total.astype(BF)
        start = TABLE_SPOT + s * TABLE_TILES
        out[start : start + TABLE_TILES] = table[...]


def table_places(own):
    place = lax.axis_index("lon") * own + iota((own, 1, 1), 0)
    return (place >= TABLE_SPOT) & (place != GAIN_SPOT)


def sum_sources(count, parts, out):
    own = out.shape[0]
    sums = jnp.sum(parts[...].astype(F32).reshape(count, own, 8, 128), axis=0)
    squares = jnp.sum(sums * sums, axis=(1, 2), keepdims=True)
    noted = (iota(sums.shape, 1) == 0) & (iota(sums.shape, 2) == NOTE) & table_places(own)
    out[...] = jnp.where(noted, squares, sums)


def spread_sums(count, mine, theirs, _, out):
    own = mine.shape[0]
    first = iota(mine.shape, 1) == 0
    lane = iota(mine.shape, 2)
    value = mine[...]
    both = value + theirs[...]
    upper = both.astype(BF).astype(F32)
    lower = jnp.sum(jnp.where(first & (lane == NOTE), both - upper, 0.0), axis=(1, 2), keepdims=True)
    noted = jnp.where(first & (lane == NOTE), upper, value)
    noted = jnp.where(first & (lane == NOTE + 1), lower, noted)
    result = jnp.where(table_places(own), noted, both)[None]
    out[...] = jnp.broadcast_to(result, (count,) + mine.shape).reshape(out.shape).astype(BF)


def constant_table(spread):
    spread[...] = table_spread()


def shifted_bias(table, valid, region, spread, bias, flat):
    build_bias(table[1, 0, 0], valid, region, True, bias, flat, spread[...])


def plain_forward(
    fields, upstream, gains, w_in, w_out, table, valid, region, spread,
    middle, own, one, two, three, hidden_out, triple_out, attention_out, mixture_out,
    cells, pieces, bias, flat,
):
    value = load_cells(fields, cells)
    unit, _ = norm_parts(value)
    hidden = (unit * gains[0:1, :]).astype(BF)
    hidden_out[...] = hidden
    triple = dot(hidden, w_in[0]).astype(BF)
    triple_out[...] = triple
    build_bias(table[0, 0, 0], valid, region, False, bias, flat, spread[...])
    _, attention, mixture = attend(*split_triple(triple), bias)
    attention_out[...] = attention
    mixture_out[...] = mixture
    added = dot(mixture, w_out[0]).astype(BF).astype(F32)
    result = (value + added).astype(BF)
    middle[...] = result
    unit, _ = norm_parts(result.astype(F32))
    hidden = (unit * gains[1:2, :]).astype(BF).astype(F32)
    raw = load_cells(upstream, cells)
    for index, (ref, (far_row, far_column)) in enumerate(zip((own, one, two, three), FIRST)):
        row_start, column_start = 3 - 3 * far_row, 6 * far_column
        for which, source in enumerate((hidden, raw)):
            for level in range(2):
                for inner in range(3):
                    start = ((1 - level) * 6 + row_start + inner) * WIN_SPAN + column_start
                    place = which * 36 + (level * 3 + inner) * 6
                    pieces[index, place : place + 6, :] = source[start : start + 6]
        ref[...] = pieces[index].astype(BF)


def gather_pieces(pieces, which, cells, forward):
    for piece, (far_row, far_column) in zip(pieces, FIRST if forward else SECOND):
        for level in range(2):
            for inner in range(3):
                if forward:
                    row, column, target = 3 * far_row + inner, 6 - 6 * far_column, level
                else:
                    row, column, target = 3 - 3 * far_row + inner, 6 * far_column, 1 - level
                start = (target * 6 + row) * WIN_SPAN + column
                place = which * 36 + (level * 3 + inner) * 6
                cells[start : start + 6, :] = piece[place : place + 6]
    return cells[...]


def shifted_core(
    own, one, two, three, bias, w_in, w_out,
    own_out, one_out, two_out, three_out, hidden_out, cot_out, triple_out, mixture_out, scores_out,
    cells, pieces_out,
):
    pieces = [ref[...].astype(F32) for ref in (own, one, two, three)]
    hidden = gather_pieces(pieces, 0, cells, True).astype(BF)
    grad_out = gather_pieces(pieces, 1, cells, True).astype(BF)
    hidden_out[...] = hidden
    cot_out[...] = grad_out
    triple = dot(hidden, w_in[1]).astype(BF)
    stacked = head_masked(dot(grad_out, w_out[1], 1, 1).astype(BF))
    query, keys, values = split_triple(triple)
    grad_attention = attention_gradient(stacked, values)
    weight, attention, mixture = attend(query, keys, values, bias)
    narrow = score_gradient(weight, grad_attention).astype(BF)
    grad_triple = triple_gradient(query, keys, attention, stacked, narrow)
    grad_hidden = dot(grad_triple, w_in[1], 1, 1).astype(BF).astype(F32)
    added = dot(mixture, w_out[1]).astype(BF).astype(F32)
    mixture_out[...] = mixture
    triple_out[...] = grad_triple
    scores_out[...] = narrow
    for index, ref in enumerate((own_out, one_out, two_out, three_out)):
        far_row, far_column = SECOND[index]
        for which, source in enumerate((added, grad_hidden)):
            for level in range(2):
                for inner in range(3):
                    start = (level * 6 + 3 * far_row + inner) * WIN_SPAN + 6 - 6 * far_column
                    place = which * 36 + (level * 3 + inner) * 6
                    pieces_out[index, place : place + 6, :] = source[start : start + 6]
        ref[...] = pieces_out[index].astype(BF)


def shifted_sums(hidden, cot, triple, mixture, scores, spread, keep, send, table, pay, gather):
    store_table(table, scores[...].astype(F32), gather, spread, ())
    store_main(pay, dot(hidden[...], triple[...], 0, 0), dot(mixture[...], cot[...], 0, 0))
    send_payload(keep, send, pay)


def ready_backward(
    middle, upstream, fields, triple,
    unit_b, inverse_b, cotangent, unit_a, query_out, keys_out, values_out,
    cells,
):
    unit, inverse = norm_parts(middle[...].astype(F32))
    unit_b[...] = unit
    inverse_b[...] = jnp.broadcast_to(inverse, inverse_b.shape)
    cotangent[...] = load_cells(upstream, cells)
    unit, _ = norm_parts(load_cells(fields, cells))
    unit_a[...] = unit
    query_out[...], keys_out[...], values_out[...] = split_triple(triple[...])


def plain_backward(
    own, one, two, three, gains, w_out, hidden_in, attention_in, mixture_in,
    unit_b, inverse_b, cotangent, query, keys, values,
    keep, send, middle_out, triple_out, scores_out, gain_out,
    cells, pay,
):
    pieces = [ref[...].astype(F32) for ref in (own, one, two, three)]
    grad_hidden = gather_pieces(pieces, 1, cells, False)
    norm_grad, gain_b = norm_backward(unit_b[...], inverse_b[:, :1], gains[1:2, :], grad_hidden)
    grad_middle = (cotangent[...] + norm_grad).astype(BF)
    middle_out[...] = grad_middle
    stacked = head_masked(dot(grad_middle, w_out[0], 1, 1).astype(BF))
    proj = dot(mixture_in[...], grad_middle, 0, 0)
    attention = attention_in[...]
    grad_scores = score_gradient(attention.astype(F32), attention_gradient(stacked, values[...]))
    grad_triple = triple_gradient(query[...], keys[...], attention, stacked, grad_scores.astype(BF))
    store_main(pay, dot(hidden_in[...], grad_triple, 0, 0), proj)
    send_payload(keep, send, pay)
    triple_out[...] = grad_triple
    scores_out[...] = grad_scores
    gain_out[...] = jnp.broadcast_to(gain_b, gain_out.shape)


def plain_rest(triple, scores, gain_b, w_in, unit_a, spread, hidden_out, table, gather):
    grad_hidden = dot(triple[...], w_in[0], 1, 1).astype(BF)
    hidden_out[...] = grad_hidden
    gain_a = jnp.sum(grad_hidden.astype(F32) * unit_a[...], axis=0, keepdims=True)
    store_table(table, scores[...], gather, spread, (gain_a, gain_b[0:1, :]))


def plain_fields(
    own, one, two, three, middle, fields, gains, grad_middle, grad_hidden,
    updated, grad_fields, token,
    cells, native,
):
    token[...] = jnp.zeros(token.shape, F32)
    pieces = [ref[...].astype(F32) for ref in (own, one, two, three)]
    store_cells(updated, middle[...].astype(F32) + gather_pieces(pieces, 0, cells, False), native)
    unit, inverse = norm_parts(load_cells(fields, cells))
    norm_grad, _ = norm_backward(unit, inverse, gains[0:1, :], grad_hidden[...].astype(F32))
    store_cells(grad_fields, grad_middle[...].astype(F32) + norm_grad, native)


def unfold_tables(mine, out, flat):
    for s in range(2):
        start = TABLE_SPOT + s * TABLE_TILES
        found = mine[start : start + TABLE_TILES - 1].astype(F32)
        found = found.reshape(2 * TABLE_ROWS + FOLD_ROWS, 128)
        parts = [found[:TABLE_ROWS], found[TABLE_ROWS : 2 * TABLE_ROWS]]
        tail = found[2 * TABLE_ROWS :]
        parts.append(jnp.concatenate(
            [tail, turn(tail[: TABLE_ROWS - FOLD_ROWS], -FOLD_LANES)], axis=0
        ))
        expand_table(parts, flat)
        out[s] = flat[:, :OFFSETS].reshape(HEADS, 2, 6, 6, 2, OFFSETS)


def unit_factor(square_sum, count):
    return 1.0 / jnp.sqrt(square_sum / count + RMS_EPS)


def finish(own, other, tables, grad_in, grad_proj, grad_bias, grad_gains, halves):
    core = lax.rem(lax.axis_index("lat"), 2)
    s = pl.program_id(0)

    @pl.when(s == 0)
    def _():
        halves[core] = own[:TABLE_SPOT].astype(F32)
        halves[1 - core] = other[:TABLE_SPOT].astype(F32)
        gains = own[GAIN_SPOT].astype(F32) + other[GAIN_SPOT].astype(F32)
        for which in range(2):
            gain = gains[4 + 2 * which : 6 + 2 * which]
            factor = unit_factor(jnp.sum(gain * gain, keepdims=True), CHANNELS)
            grad_gains[which : which + 1, :128] = gain[0:1, :] * factor
            grad_gains[which : which + 1, 128:] = gain[1:2, : CHANNELS - 128] * factor

    main = jnp.concatenate(
        [halves[c // 3, pl.ds(s * MAIN_HALF + (c % 3) * 24, 24)].reshape(CHANNELS, 128)
         for c in range(6)],
        axis=1,
    )
    weight = main[:, : 3 * CHANNELS]
    grad_in[...] = weight * unit_factor(jnp.sum(weight * weight, keepdims=True), weight.size)
    proj = main[:, 3 * CHANNELS :]
    grad_proj[...] = proj * unit_factor(jnp.sum(proj * proj, keepdims=True), proj.size)
    rows = pl.ds(TABLE_SPOT + s * TABLE_TILES, TABLE_TILES - 1)
    every = jnp.sum(own[rows].astype(F32) + other[rows].astype(F32), axis=0)
    noted = (iota((8, 128), 0) == 0) & ((iota((8, 128), 1) >> 1) == NOTE // 2)
    squares = jnp.sum(jnp.where(noted, every, 0.0), keepdims=True)
    factor = unit_factor(squares, 4 * WINDOW * 6 * OFFSETS)
    grad_bias[...] = tables[s] * factor[None, None, None, None]


def whole():
    return pl.BlockSpec(memory_space=pltpu.VMEM)


def stepped(shape):
    return pl.BlockSpec((None,) + shape, lambda i: (i,) + (0,) * len(shape))


def run(body, outs, in_specs, scratch, args, out_specs=None, steps=1, cost=None):
    return pl.pallas_call(
        body,
        grid=(steps,),
        out_shape=[jax.ShapeDtypeStruct(shape, kind) for shape, kind in outs],
        in_specs=in_specs,
        out_specs=out_specs or [whole() for _ in outs],
        scratch_shapes=[
            pltpu.VMEM(shape, F32) if isinstance(shape, tuple) else shape for shape in scratch
        ],
        cost_estimate=cost and pl.CostEstimate(flops=cost, bytes_accessed=0, transcendentals=0),
        compiler_params=pltpu.CompilerParams(vmem_limit_bytes=40 * 1024 * 1024),
    )(*args)


CELLS = (WINDOW, CHANNELS)
PIECE = ((72, CHANNELS), BF)
NATIVE = (WIN_ROWS, WIN_SPAN, 2, CHANNELS)
WEIGHT = (CHANNELS, 3 * CHANNELS)
SQUARE = (CHANNELS, CHANNELS)
SCORES = (STACK, WINDOW)
SPREAD = (2, STACK, 128)
PAY = pltpu.VMEM((2, MAIN_HALF, 8, 128), BF)
PARTS = [((MAIN_HALF, 8, 128), BF), ((MAIN_HALF, 8, 128), BF)]
TABLE_PART = ((TABLE_TILES, 8, 128), BF)
TABLES = (2, HEADS, 2, 6, 6, 2, OFFSETS)
GRADS = [((2,) + WEIGHT, F32), ((2,) + SQUARE, F32), ((2, 1, 1, HEADS, 2, 6, 6, 2, OFFSETS), F32)]


def exchange(pieces, sign):
    lons, lats = lax.axis_size("lon"), lax.axis_size("lat")

    def move(block, lon_step, lat_step):
        route = []
        for lon in range(lons):
            for lat in range(lats):
                target = ((lon - sign * lon_step) % lons) * lats + (lat + sign * lat_step) % lats
                route.append((lon * lats + lat, target))
        return lax.ppermute(block, AXES, route)

    order = FIRST if sign < 0 else SECOND
    moved = [move(piece, column, row) for piece, (row, column) in zip(pieces[1:], order[1:])]
    return [pieces[0], *moved]


def on_device(fields, upstream, gains, project_in, project_out, earth_bias, row_valid, regions):
    fields = fields.transpose(1, 2, 0, 3)
    upstream = upstream.transpose(1, 2, 0, 3)
    earth_bias = earth_bias.transpose(0, 1, 2, 3, 4, 6, 7, 5, 8)
    (spread,) = run(
        constant_table, [((TABLE_LANES, 256), BF)], [], [], (), cost=4_000_000_000
    )
    middle, *rest = run(
        plain_forward,
        [(CELLS, BF), PIECE, PIECE, PIECE, PIECE, (CELLS, BF), ((WINDOW, 3 * CHANNELS), BF),
         (SCORES, BF), (CELLS, BF)],
        [whole()] * 9,
        [CELLS, (4, 72, CHANNELS), SPREAD, (STACK, 128)],
        (fields, upstream, gains, project_in, project_out, earth_bias, row_valid, regions, spread),
    )
    pieces = exchange(rest[:4], -1)
    (bias,) = run(
        shifted_bias,
        [(SPREAD, F32)],
        [whole()] * 4,
        [(STACK, 128)],
        (earth_bias, row_valid, regions, spread),
    )
    saved = rest[4:]
    ready = run(
        ready_backward,
        [(CELLS, F32), ((WINDOW, 128), F32), (CELLS, F32), (CELLS, F32),
         ((STACK, CHANNELS), BF), (CELLS, BF), (CELLS, BF)],
        [whole()] * 4,
        [CELLS],
        (middle, upstream, fields, saved[1]),
    )
    *back, hidden, cot, triple, mixture, scores = run(
        shifted_core,
        [PIECE, PIECE, PIECE, PIECE, (CELLS, BF), (CELLS, BF), ((WINDOW, 3 * CHANNELS), BF),
         (CELLS, BF), (SCORES, BF)],
        [whole()] * 7,
        [CELLS, (4, 72, CHANNELS)],
        (*pieces, bias, project_in, project_out),
    )
    back = exchange(back, 1)
    keep_b, send_b, table_b = run(
        shifted_sums,
        PARTS + [TABLE_PART],
        [whole()] * 6,
        [PAY, SPREAD],
        (hidden, cot, triple, mixture, scores, spread),
    )
    got_b = swap(send_b, 1)
    unit_b, inverse_b, cotangent, unit_a, *heads = ready
    keep_a, send_a, grad_middle, grad_triple, grad_scores, gain_b = run(
        plain_backward,
        PARTS + [(CELLS, BF), ((WINDOW, 3 * CHANNELS), BF), (SCORES, F32), ((8, CHANNELS), F32)],
        [whole()] * 15,
        [CELLS, PAY],
        (*back, gains, project_out, saved[0], saved[2], saved[3],
         unit_b, inverse_b, cotangent, *heads),
    )
    grad_hidden, table_a = run(
        plain_rest,
        [(CELLS, BF), TABLE_PART],
        [whole()] * 6,
        [SPREAD],
        (grad_triple, grad_scores, gain_b, project_in, unit_a, spread),
    )
    got_a = swap(send_a, 1)
    lons = lax.axis_size("lon")
    own = SLOTS // lons
    tiles = (own * lons, 8, 128)
    message = (tiles, BF)
    shard = ((own, 8, 128), F32)
    (joined,) = run(
        join_cores, [message], [whole()] * 6, [],
        (keep_a, got_a, table_a, keep_b, got_b, table_b),
    )
    (summed,) = run(
        functools.partial(sum_sources, lons), [shard], [whole()], [], (trade(joined),)
    )
    updated, grad_fields, token = run(
        plain_fields,
        [(NATIVE, BF), (NATIVE, BF), ((8, 128), F32)],
        [whole()] * 9,
        [CELLS, NATIVE],
        (*back, middle, fields, gains, grad_middle, grad_hidden),
    )
    (result,) = run(
        functools.partial(spread_sums, lons), [message], [whole()] * 3, [],
        (summed, swap(summed, 2), token),
    )
    mine = trade(result)
    (tables,) = run(unfold_tables, [(TABLES, F32)], [whole()], [(STACK, 128)], (mine,))
    grad_in, grad_proj, grad_bias, grad_gains = run(
        finish,
        GRADS + [((2, CHANNELS), F32)],
        [whole()] * 3,
        [(2, TABLE_SPOT, 8, 128)],
        (mine, swap(mine, 1), tables),
        [stepped(WEIGHT), stepped(SQUARE), pl.BlockSpec(
            (None, None, None, HEADS, 2, 6, 6, 2, OFFSETS), lambda i: (i,) + (0,) * 8), whole()],
        2,
    )
    return (
        updated.transpose(2, 0, 1, 3),
        grad_fields.transpose(2, 0, 1, 3),
        grad_gains,
        grad_in,
        grad_proj,
        grad_bias.transpose(0, 1, 2, 3, 4, 7, 5, 6, 8),
    )


def swap(block, bit):
    count = lax.axis_size("lon") * lax.axis_size("lat")
    return lax.ppermute(block, AXES, [(d, d ^ bit) for d in range(count)])


def trade(block):
    return lax.all_to_all(block, "lon", 0, 0, tiled=True)


def solution(mesh):
    spec = P(None, "lat", "lon", None)
    bias_spec = P(None, None, "lat", None, None, None, None, None, None)
    return jax.shard_map(
        on_device,
        mesh=mesh,
        in_specs=(spec, spec, P(), P(), P(), bias_spec, P(), P()),
        out_specs=(spec, spec, P(), P(), P(), bias_spec),
        check_vma=False,
    )
```
